256 devices in a mesh: member: 8 (over x_lo, y), grid: 32 (over x_hi, z, core).
Axes of the slice: x: 4 (x_hi: 2, x_lo: 2; x = x_hi * 2 + x_lo), y: 4, z: 8, core: 2. Of those that a mesh axis runs over, the one named last changes fastest.
Arguments:
- latent: bfloat16 [8, 8192, 1024], P('member', 'grid'), may hold values from -6 to 6
- grid_latent_skip: bfloat16 [8, 16384, 1024], P('member', 'grid'), may hold values from -6 to 6
- initial_member_state: float32 [8, 100, 16384], P('member', None, 'grid'), may hold values from -6 to 6
- target: float32 [100, 16384], P(None, 'grid'), may hold values from -6 to 6
- neighbours: int32 [3, 16384], P(None, 'grid'), may hold values from 0 to 511, as said below
- edge_weight: float32 [3, 16384], P(None, 'grid'), may hold values from 0.2 to 1
- area_weight: float32 [16384], P('grid'), may hold values from 0.3 to 27, as said below
- variable_weight: float32 [100], replicated, may hold values from 0.3 to 3
- output_projection: bfloat16 [100, 1024], replicated, may hold values from -0.1875 to 0.1875
- layer_norm_gain: float32 [1024], replicated, may hold values from 0.1 to 1.9
Outputs:
- fair_crps: float32 [], replicated
- latent_grad: bfloat16 [8, 8192, 1024], P('member', 'grid')
- out_weight_grad: float32 [100, 1024], replicated
- norm_gain_grad: float32 [1024], replicated
The draws below stay inside these ranges and needn't reach their ends.
Inputs may be any that keep to these rules, and one draw needn't show every extreme that they name: neighbours[k, p] indexes 256 + 2 * 128 rows ordered by latitude: the 128 last mesh rows of the slab below the point's slab, the slab's own 256 rows, then the 128 first rows of the slab above. `area_weight`: positive.
All inputs are finite; a program needn't handle non-finite values.
Results may differ from the reference program's by a relative error of at most 0.0067.
Values may be sent and summed in bfloat16 or wider, within the bound.
No kernel may reach another device: no remote copies, remote signals or barrier semaphores. Data moves between devices by JAX's collectives and lax.ppermute only.
A program may use at most 64 MiB of HBM per device.

```python
import math
import jax
import jax.numpy as jnp
from jax import lax

C = 1024
V = 100
K = 3
G_DEV = 512
MN_DEV = 256
HALO = 128
MEMBERS = 8
GRID = 16384
MESH = 8192


def draw_neighbours(key, part):
    extent = MN_DEV + 2 * HALO
    local = jnp.arange(GRID, dtype=jnp.int32) % G_DEV
    centre = HALO + local * MN_DEV // G_DEV
    offsets = jax.random.randint(key, (K, GRID), -HALO, HALO + 1)
    picked = jnp.clip(centre[None, :] + offsets, 0, extent - 1)
    first_row = jnp.where(local == 0, 0, picked[0])
    last_row = jnp.where(local == G_DEV - 1, extent - 1, picked[K - 1])
    picked = picked.at[0].set(first_row)
    picked = picked.at[K - 1].set(last_row)
    return picked.astype(jnp.int32)


def draw_area_weight(key, part):
    slabs = GRID // G_DEV
    slab_of = (jnp.arange(GRID, dtype=jnp.int32) // G_DEV).astype(jnp.float32)
    ramp = slab_of / max(slabs - 1, 1)
    spread = jax.random.uniform(key, (GRID,), jnp.float32, math.log(0.3), math.log(3.0))
    trend = jnp.exp(ramp * math.log(3.0))
    return (trend * jnp.exp(spread)).astype(jnp.float32)


def block_scale(own_key, shape, cuts, least, top_value):
    def one(axis_at, parts):
        heights = jax.random.uniform(jax.random.fold_in(jax.random.fold_in(own_key, 6), axis_at), (parts,), jnp.float32, least / len(cuts), top_value / len(cuts))
        return jnp.repeat(jnp.exp(heights), shape[axis_at] // parts).reshape((-1,) + (1,) * (len(shape) - axis_at - 1))

    loudness = one(*cuts[0])
    for cut in cuts[1:]:
        loudness = loudness * one(*cut)
    return loudness


def normal_values(stream_key, dims, width, most, pieces=(), kind=jnp.bfloat16):
    array = jax.random.normal(stream_key, dims, jnp.float32) * width
    if len(pieces) > 0:
        array = block_scale(stream_key, dims, pieces, -0.22, 0.18) * array
    return jnp.clip(array, min=-most, max=most).astype(kind)


def setup_inputs(seed: int = 0) -> dict:
    seeds = jax.random.split(jax.random.key(seed), 11)
    return {
        "latent": normal_values(seeds[0], (MEMBERS, MESH, C), 1.0, 6.0, ((0, 8), (1, 32))),
        "grid_latent_skip": normal_values(seeds[1], (MEMBERS, GRID, C), 1.0, 6.0, ((0, 8), (1, 32))),
        "initial_member_state": normal_values(seeds[2], (MEMBERS, V, GRID), 1.0, 6.0, ((0, 8), (2, 32)), jnp.float32),
        "target": normal_values(seeds[3], (V, GRID), 1.0, 6.0, ((1, 32),), jnp.float32),
        "neighbours": draw_neighbours(jax.random.fold_in(seeds[10], 71), 0),
        "edge_weight": jnp.clip(0.2 + 0.8 * jax.random.uniform(seeds[5], (K, GRID), jnp.float32) ** block_scale(seeds[5], (K, GRID), ((1, 32),), -0.2, 0.2), 0.2, 1.0),
        "area_weight": draw_area_weight(jax.random.fold_in(seeds[10], 71), 0),
        "variable_weight": jnp.clip(jnp.exp(jax.random.uniform(seeds[7], (V,), jnp.float32, math.log(0.3), math.log(3.0))), 0.3, 3.0),
        "output_projection": normal_values(seeds[8], (V, C), C ** -0.5, 0.1875),
        "layer_norm_gain": jnp.clip(1.0 + 0.18 * jax.random.normal(seeds[9], (C,), jnp.float32), 0.1, 1.9),
    }


SMOOTHING = 0.25
FAIRNESS = 0.95
norm_eps = 1e-05

def smooth_abs(value):
    return jnp.sqrt(value * value + SMOOTHING * SMOOTHING)

def mesh_rows(neighbours):
    slab_of = jnp.arange(neighbours.shape[1], dtype=jnp.int32) // G_DEV
    global_rows = slab_of[None, :] * MN_DEV + neighbours - HALO
    inside = (global_rows >= 0) & (global_rows < MESH)
    return (jnp.clip(global_rows, 0, MESH - 1).astype(jnp.int32), inside)

def member_forward_pass(latent_one, embed_one, state_one, guarded_rows, weight_arrays, output_projection, layer_norm_gain):
    total = jnp.zeros((embed_one.shape[0], embed_one.shape[1]), jnp.float32)
    for slot in range(K):
        total = total + weight_arrays[slot][:, None] * latent_one[guarded_rows[slot]].astype(jnp.float32)
    mixed = embed_one.astype(jnp.float32) + total
    average = lax.optimization_barrier(jnp.mean(mixed, axis=1, keepdims=True))
    centred = mixed - average
    rscale = lax.rsqrt(lax.optimization_barrier(jnp.mean(centred * centred, axis=1, keepdims=True)) + norm_eps)
    normed = centred * rscale
    scaled = (normed * layer_norm_gain[None, :]).astype(jnp.bfloat16)
    project = lax.dot_general(output_projection, scaled, (((1,), (1,)), ((), ())), preferred_element_type=jnp.float32)
    return (state_one + project, normed, scaled, rscale)

def reference(latent, grid_latent_skip, initial_member_state, target, neighbours, edge_weight, area_weight, variable_weight, output_projection, layer_norm_gain):
    member_list = latent.shape[0]
    guarded_rows, inside = mesh_rows(neighbours)
    weight_arrays = edge_weight / lax.optimization_barrier(jnp.sum(edge_weight, axis=0, keepdims=True)) * inside.astype(jnp.float32)
    predicted_fields = jnp.stack([member_forward_pass(latent[member_index], grid_latent_skip[member_index], initial_member_state[member_index], guarded_rows, weight_arrays, output_projection, layer_norm_gain)[0] for member_index in range(member_list)])
    weight_map = variable_weight[:, None] * area_weight[None, :]
    eps_fair = (1.0 - FAIRNESS) / member_list
    coef_pair = (1.0 - eps_fair) / (member_list * (member_list - 1))
    total_loss = jnp.zeros((), jnp.float32)
    grads = []
    for single_member in range(member_list):
        pair_distance = predicted_fields[single_member] - target
        spread = smooth_abs(pair_distance)
        member_difference = predicted_fields[single_member][None] - predicted_fields
        dist = smooth_abs(member_difference)
        pair_total = lax.optimization_barrier(jnp.sum(dist, axis=0)) - SMOOTHING
        pair_slope = lax.optimization_barrier(jnp.sum(member_difference / dist, axis=0))
        total_loss = total_loss + jnp.sum(weight_map * (spread / member_list - 0.5 * coef_pair * pair_total))
        grads.append((weight_map * (pair_distance / spread / member_list - coef_pair * pair_slope)).astype(jnp.bfloat16))
    wout_acc = jnp.zeros(output_projection.shape, jnp.float32)
    gain_acc = jnp.zeros(layer_norm_gain.shape, jnp.float32)
    latent_grads = []
    for single_member in range(member_list):
        unused, normed, scaled, rscale = member_forward_pass(latent[single_member], grid_latent_skip[single_member], initial_member_state[single_member], guarded_rows, weight_arrays, output_projection, layer_norm_gain)
        fore_grad = grads[single_member]
        scaled_grad = lax.dot_general(fore_grad, output_projection, (((0,), (0,)), ((), ())), preferred_element_type=jnp.float32)
        wout_acc = wout_acc + jnp.dot(fore_grad, scaled, preferred_element_type=jnp.float32)
        gain_acc = gain_acc + lax.optimization_barrier(jnp.sum(scaled_grad * normed, axis=0))
        norm_grad = scaled_grad * layer_norm_gain[None, :]
        mixed_grad = rscale * (norm_grad - lax.optimization_barrier(jnp.mean(norm_grad, axis=1, keepdims=True)) - normed * lax.optimization_barrier(jnp.mean(norm_grad * normed, axis=1, keepdims=True)))
        collect = jnp.zeros((MESH, latent.shape[2]), jnp.float32)
        for slot in range(K):
            collect = collect.at[guarded_rows[slot]].add(weight_arrays[slot][:, None] * mixed_grad)
        latent_grads.append(collect.astype(jnp.bfloat16))
    fair_crps = total_loss / (GRID * V)
    return (fair_crps, jnp.stack(latent_grads), wout_acc, gain_acc)
```

```python
import jax
import jax.numpy as jnp
from jax import lax
from jax.experimental import pallas as pl
from jax.experimental.pallas import tpu as pltpu
from jax.sharding import Mesh
from jax.sharding import PartitionSpec as P

SMOOTHING = 0.25
FAIRNESS = 0.95
NORM_EPS = 1e-05
MEMBER = ("xl", "y")
GRID = ("xh", "z", "c")
PLANE = ("xl", "y", "xh")
ROWS = 128
BF16 = jnp.bfloat16
F32 = jnp.float32
VMEM_LIMIT = 48 * 1024 * 1024


def dot(a, b, dims):
    return lax.dot_general(a, b, (dims, ((), ())), preferred_element_type=F32)


def call(kernel, outs, flops=0, moved=0, smem=0):
    def run(*operands):
        specs = [
            pl.BlockSpec(memory_space=pltpu.SMEM if i < smem else pltpu.VMEM)
            for i in range(len(operands))
        ]
        return pl.pallas_call(
            kernel,
            out_shape=[jax.ShapeDtypeStruct(s, d) for s, d in outs],
            in_specs=specs,
            out_specs=[pl.BlockSpec(memory_space=pltpu.VMEM) for _ in outs],
            compiler_params=pltpu.CompilerParams(vmem_limit_bytes=VMEM_LIMIT),
            cost_estimate=pl.CostEstimate(flops=flops, bytes_accessed=moved, transcendentals=0),
        )(*operands)

    return run


def prepare_kernel(nb, ew, vw, area, latent, skip, et_out, halo_out, part_out, wm_out):
    slots, points = nb.shape
    mesh_count = latent.shape[0]
    rim = mesh_count // 2
    extent = mesh_count + 2 * rim
    weights = ew[...]
    weights = weights / jnp.sum(weights, axis=0, keepdims=True)
    rows = nb[...]
    row_id = lax.broadcasted_iota(jnp.int32, (extent, points), 0)
    et = jnp.zeros((extent, points), F32)
    for k in range(slots):
        et = et + jnp.where(row_id == rows[k : k + 1, :], weights[k : k + 1, :], 0.0)
    et_out[...] = et.astype(BF16)
    both = jnp.concatenate(
        [rows.astype(F32), weights, jnp.zeros((8 - 2 * slots, points), F32)], axis=0
    )
    columns = jnp.transpose(both)
    lane_id = lax.broadcasted_iota(jnp.int32, (points, extent), 1).astype(F32)
    edges = jnp.zeros((points, extent), F32)
    for k in range(slots):
        edges = edges + jnp.where(
            lane_id == columns[:, k : k + 1], columns[:, slots + k : slots + k + 1], 0.0
        )
    edges = edges.astype(BF16)
    halo_out[:, :rim] = edges[:, :rim]
    halo_out[:, rim:] = edges[:, rim + mesh_count :]
    part_out[...] = skip[...].astype(F32) + dot(
        edges[:, rim : rim + mesh_count], latent[...], ((1,), (0,))
    )
    variables = vw.shape[1]
    diagonal = lax.broadcasted_iota(jnp.int32, (variables, variables), 0) == (
        lax.broadcasted_iota(jnp.int32, (variables, variables), 1)
    )
    vw_column = jnp.sum(jnp.where(diagonal, vw[...], 0.0), axis=1, keepdims=True)
    wm_out[...] = vw_column * area[...]


def forward_kernel(part, edges, before, after, gain, proj, state, f_out, fb_out, sc_out, rs_out):
    rim = before.shape[0]
    mixed = (
        part[...]
        + dot(edges[:, :rim], before[...], ((1,), (0,)))
        + dot(edges[:, rim:], after[...], ((1,), (0,)))
    )
    centred = mixed - jnp.mean(mixed, axis=1, keepdims=True)
    rscale = lax.rsqrt(jnp.mean(centred * centred, axis=1, keepdims=True) + NORM_EPS)
    scaled = (centred * rscale * gain[...]).astype(BF16)
    sc_out[...] = scaled
    rs_out[...] = rscale
    field = state[...] + dot(proj[...], scaled, ((1,), (1,)))
    f_out[...] = field
    low = field.astype(BF16)
    for m in range(fb_out.shape[0]):
        fb_out[m] = low


def loss_kernel(me, every, field, target, wm, proj, scaled, gain, fg_out, keep_out, send_out):
    members, variables, _ = every.shape
    eps_fair = (1.0 - FAIRNESS) / members
    coef_pair = (1.0 - eps_fair) / (members * (members - 1))
    smooth = SMOOTHING * SMOOTHING
    f = field[...]
    weight_map = wm[...]
    d = f - target[...]
    s = d * d + smooth
    r = lax.rsqrt(s)
    spread, slope = s * r, d * r
    pair_total = jnp.full_like(f, -SMOOTHING)
    pair_slope = jnp.zeros_like(f)
    for k in range(members):
        other = jnp.where(me[0] == k, f, every[k].astype(F32))
        d = f - other
        s = d * d + smooth
        r = lax.rsqrt(s)
        pair_total = pair_total + s * r
        pair_slope = pair_slope + d * r
    terms = weight_map * (spread / members - 0.5 * coef_pair * pair_total)
    loss = jnp.sum(jnp.sum(terms, axis=0, keepdims=True), axis=1, keepdims=True)
    fore_grad = (weight_map * (slope / members - coef_pair * pair_slope)).astype(BF16)
    fg_out[...] = fore_grad
    values = scaled[...]
    wout = dot(fore_grad, values, ((1,), (0,)))
    scaled_grad = dot(fore_grad, proj[...], ((0,), (0,)))
    product = jnp.sum(scaled_grad * values.astype(F32), axis=0, keepdims=True) / gain[...]
    half = wout.shape[1] // 2
    upper = me[1] == 1

    def store(out, left):
        out[:variables, :] = jnp.where(left, wout[:, :half], wout[:, half:])
        out[variables : variables + 1, :] = jnp.where(left, product[:, :half], product[:, half:])
        out[variables + 1 : variables + 2, :] = jnp.broadcast_to(loss, (1, half))
        out[variables + 2 :, :] = jnp.zeros((ROWS - variables - 2, half), F32)

    store(keep_out, jnp.logical_not(upper))
    store(send_out, upper)


def back_kernel(fore_grad, proj, scaled, gain, rscale, et, own_out, up_out, down_out):
    channels = scaled.shape[1]
    rim = up_out.shape[0]
    mesh_count = own_out.shape[0]
    scaled_grad = dot(fore_grad[...], proj[...], ((0,), (0,)))
    values = scaled[...].astype(F32)
    norm_grad = scaled_grad * gain[...]
    first = jnp.sum(norm_grad, axis=1, keepdims=True) / channels
    second = jnp.sum(scaled_grad * values, axis=1, keepdims=True) / channels
    mixed_grad = rscale[...] * (norm_grad - first - values * (1.0 / gain[...]) * second)
    mixed_grad = mixed_grad.astype(BF16)
    down_out[...] = dot(et[:rim], mixed_grad, ((1,), (0,))).astype(BF16)
    up_out[...] = dot(et[rim + mesh_count :], mixed_grad, ((1,), (0,))).astype(BF16)
    own_out[...] = dot(et[rim : rim + mesh_count], mixed_grad, ((1,), (0,)))


def finish_latent_kernel(own, below, above, out):
    rim = below.shape[0]
    out[0, :rim] = (own[:rim] + below[...].astype(F32)).astype(BF16)
    out[0, rim:] = (own[rim:] + above[...].astype(F32)).astype(BF16)


def fold_kernel(parts, out):
    total = jnp.sum(parts[...], axis=0)
    for i in range(out.shape[0]):
        out[i] = total


def finish_weights_kernel(me, mine, other, wout_out, gain_out, loss_out):
    variables, channels = wout_out.shape
    half = channels // 2
    left = me[1] == 0
    a, b = mine[...], other[...]
    first = jnp.where(left, a, b)
    second = jnp.where(left, b, a)
    wout_out[:, :half] = first[:variables]
    wout_out[:, half:] = second[:variables]
    gain_out[:, :half] = first[variables : variables + 1]
    gain_out[:, half:] = second[variables : variables + 1]
    loss_out[...] = first[variables + 1 : variables + 2, :1]


def per_device(
    latent,
    grid_latent_skip,
    initial_member_state,
    target,
    neighbours,
    edge_weight,
    area_weight,
    variable_weight,
    output_projection,
    layer_norm_gain,
):
    latent, skip, state = latent[0], grid_latent_skip[0], initial_member_state[0]
    mesh_count, channels = latent.shape
    points = skip.shape[0]
    rim = mesh_count // 2
    extent = mesh_count + 2 * rim
    variables = output_projection.shape[0]
    members = lax.axis_size(MEMBER)
    slabs = lax.axis_size(GRID)
    plane = lax.axis_size(PLANE)
    half = channels // 2
    gain = layer_norm_gain[None]
    up = [(i, i + 1) for i in range(slabs - 1)]
    down = [(i + 1, i) for i in range(slabs - 1)]
    swap = [(0, 1), (1, 0)]
    me = jnp.stack([lax.axis_index(MEMBER), lax.axis_index("c")]).astype(jnp.int32)

    before = lax.ppermute(latent[mesh_count - rim :], GRID, up)
    after = lax.ppermute(latent[:rim], GRID, down)
    et, edges, part, weight_map = call(
        prepare_kernel,
        [
            ((extent, points), BF16),
            ((points, 2 * rim), BF16),
            ((points, channels), F32),
            ((variables, points), F32),
        ],
        flops=2 * points * mesh_count * channels,
        moved=8_000_000,
    )(neighbours, edge_weight, variable_weight[None], area_weight[None], latent, skip)
    field, copies, scaled, rscale = call(
        forward_kernel,
        [
            ((variables, points), F32),
            ((members, variables, points), BF16),
            ((points, channels), BF16),
            ((points, 1), F32),
        ],
        flops=2 * points * channels * (2 * rim + variables),
        moved=5_000_000,
    )(part, edges, before, after, gain, output_projection, state)
    every = lax.all_to_all(copies, MEMBER, 0, 0, tiled=True)
    fore_grad, keep, send = call(
        loss_kernel,
        [((variables, points), BF16), ((ROWS, half), F32), ((ROWS, half), F32)],
        flops=4 * points * channels * variables,
        moved=4_000_000,
        smem=1,
    )(me, every, field, target, weight_map, output_projection, scaled, gain)

    met = keep + lax.ppermute(send, "c", swap)
    parts = lax.all_to_all(met.reshape(plane, ROWS // plane, half), PLANE, 0, 0, tiled=True)
    depth = lax.axis_size("z")
    (spread,) = call(fold_kernel, [((depth, ROWS // plane, half), F32)])(parts)
    parts = lax.all_to_all(spread, "z", 0, 0, tiled=True)
    (spread,) = call(fold_kernel, [((plane, ROWS // plane, half), F32)])(parts)
    mine = lax.all_to_all(spread, PLANE, 0, 0, tiled=True).reshape(ROWS, half)
    other = lax.ppermute(mine, "c", swap)
    wout, gain_grad, loss = call(
        finish_weights_kernel,
        [((variables, channels), F32), ((1, channels), F32), ((1, 1), F32)],
        smem=1,
    )(me, mine, other)

    own, to_above, to_below = call(
        back_kernel,
        [((mesh_count, channels), F32), ((rim, channels), BF16), ((rim, channels), BF16)],
        flops=2 * points * channels * (extent + variables),
        moved=6_000_000,
    )(fore_grad, output_projection, scaled, gain, rscale, et)
    below = lax.ppermute(to_above, GRID, up)
    above = lax.ppermute(to_below, GRID, down)
    (latent_grad,) = call(finish_latent_kernel, [((1, mesh_count, channels), BF16)])(
        own, below, above
    )
    fair_crps = loss[0, 0] / (points * slabs * variables)
    return (fair_crps, latent_grad, wout, gain_grad[0])


def solution(mesh):
    fine = Mesh(mesh.devices.reshape(2, 4, 2, 8, 2), ("xl", "y", "xh", "z", "c"))
    placed = (
        P(MEMBER, GRID, None),
        P(MEMBER, GRID, None),
        P(MEMBER, None, GRID),
        P(None, GRID),
        P(None, GRID),
        P(None, GRID),
        P(GRID),
        P(),
        P(),
        P(),
    )
    return jax.shard_map(
        per_device,
        mesh=fine,
        in_specs=placed,
        out_specs=(P(), P(MEMBER, GRID, None), P(), P()),
        check_vma=False,
    )
```

```python
import jax
import jax.numpy as jnp
from jax import lax
from jax.experimental import pallas as pl
from jax.experimental.pallas import tpu as pltpu
from jax.sharding import Mesh
from jax.sharding import PartitionSpec as P

SMOOTHING = 0.25
FAIRNESS = 0.95
NORM_EPS = 1e-05
MEMBER = ("xl", "y")
GRID = ("xh", "z", "c")
PLANE = ("xl", "y", "xh")
ROWS = 128
BF16 = jnp.bfloat16
F32 = jnp.float32
VMEM_LIMIT = 24 * 1024 * 1024


def dot(a, b, dims):
    return lax.dot_general(a, b, (dims, ((), ())), preferred_element_type=F32)


def call(kernel, outs, spaces="", scratch=(), flops=0, moved=0):
    places = {"s": pltpu.SMEM, "h": pltpu.HBM, "a": pl.ANY, "v": pltpu.VMEM}

    def run(*operands):
        letters = spaces.ljust(len(operands), "v")
        operands = [
            pltpu.with_memory_space_constraint(x, pltpu.HBM) if c == "h" else x
            for x, c in zip(operands, letters)
        ]
        return pl.pallas_call(
            kernel,
            out_shape=[jax.ShapeDtypeStruct(s, d) for s, d in outs],
            in_specs=[pl.BlockSpec(memory_space=places[c]) for c in letters],
            out_specs=[pl.BlockSpec(memory_space=pltpu.VMEM) for _ in outs],
            scratch_shapes=list(scratch),
            compiler_params=pltpu.CompilerParams(vmem_limit_bytes=VMEM_LIMIT),
            cost_estimate=pl.CostEstimate(flops=flops, bytes_accessed=moved, transcendentals=0),
        )(*operands)

    return run


def cut_kernel(me, latent, first_out, second_out, sems):
    rim = first_out.shape[0]
    start = pl.multiple_of((1 - me[1]) * rim, rim)
    other = pl.multiple_of(me[1] * rim, rim)
    one = pltpu.make_async_copy(latent.at[pl.ds(start, rim)], first_out, sems.at[0])
    two = pltpu.make_async_copy(latent.at[pl.ds(other, rim)], second_out, sems.at[1])
    one.start()
    two.start()
    one.wait()
    two.wait()


def prepare_kernel(
    me, nb_in, ew_in, vw_in, area_in, latent_in, skip_in, state_in, near,
    et_out, far_out, part_out, wm_out, state_out,
    nb, ew, vw, area, latent, skip, state, sems,
):
    pairs = (
        (nb_in, nb), (ew_in, ew), (vw_in, vw), (area_in, area),
        (latent_in, latent), (skip_in, skip), (state_in, state),
    )
    copies = [pltpu.make_async_copy(a, b, sems.at[i]) for i, (a, b) in enumerate(pairs)]
    for copy in copies:
        copy.start()
    for copy in copies[:4]:
        copy.wait()
    slots, points = nb.shape
    mesh_count = latent.shape[0]
    rim = mesh_count // 2
    near_start = (1 - me[1]) * (rim + mesh_count)
    far_start = me[1] * (rim + mesh_count)
    far_there = me[2] == 1
    weights = ew[...]
    weights = weights / jnp.sum(weights, axis=0, keepdims=True)
    rows = nb[...]
    both = jnp.concatenate(
        [rows.astype(F32), weights, jnp.zeros((8 - 2 * slots, points), F32)], axis=0
    )
    columns = jnp.transpose(both)
    ids = columns.astype(jnp.int32)

    def edges(start, count):
        lane = lax.broadcasted_iota(jnp.int32, (points, count), 1) + start
        total = jnp.zeros((points, count), F32)
        for k in range(slots):
            total = total + jnp.where(
                lane == ids[:, k : k + 1], columns[:, slots + k : slots + k + 1], 0.0
            )
        return total

    def edges_turned(start, count):
        sublane = lax.broadcasted_iota(jnp.int32, (count, points), 0) + start
        total = jnp.zeros((count, points), F32)
        for k in range(slots):
            total = total + jnp.where(sublane == rows[k : k + 1], weights[k : k + 1], 0.0)
        return total

    def parts(value):
        high = value.astype(BF16)
        return high, (value - high.astype(F32)).astype(BF16)

    near_high, near_low = parts(edges(near_start, rim))
    own_high, own_low = parts(edges(rim, mesh_count))
    far_high, far_low = parts(jnp.where(far_there, edges(far_start, rim), 0.0))
    far_out[:, :rim] = far_high
    far_out[:, rim:] = far_low
    copies[4].wait()
    borrowed, own = near[...], latent[...]
    mix = (
        dot(near_high, borrowed, ((1,), (0,)))
        + dot(near_low, borrowed, ((1,), (0,)))
        + dot(own_high, own, ((1,), (0,)))
        + dot(own_low, own, ((1,), (0,)))
    )
    copies[5].wait()
    part_out[...] = skip[...].astype(F32) + mix
    et_out[:rim] = edges_turned(near_start, rim).astype(BF16)
    et_out[rim : rim + mesh_count] = edges_turned(rim, mesh_count).astype(BF16)
    et_out[rim + mesh_count :] = jnp.where(far_there, edges_turned(far_start, rim), 0.0).astype(BF16)
    variables = vw.shape[1]
    diagonal = lax.broadcasted_iota(jnp.int32, (variables, variables), 0) == (
        lax.broadcasted_iota(jnp.int32, (variables, variables), 1)
    )
    vw_column = jnp.sum(jnp.where(diagonal, vw[...], 0.0), axis=1, keepdims=True)
    wm_out[...] = vw_column * area[...]
    copies[6].wait()
    state_out[...] = state[:, 0, :]


def forward_kernel(part, edges, far, gain, proj, state, f_out, fb_out, sc_out, rs_out):
    rim = far.shape[0]
    borrowed = far[...]
    mixed = (
        part[...]
        + dot(edges[:, :rim], borrowed, ((1,), (0,)))
        + dot(edges[:, rim:], borrowed, ((1,), (0,)))
    )
    centred = mixed - jnp.mean(mixed, axis=1, keepdims=True)
    rscale = lax.rsqrt(jnp.mean(centred * centred, axis=1, keepdims=True) + NORM_EPS)
    scaled = (centred * rscale * gain[...]).astype(BF16)
    sc_out[...] = scaled
    rs_out[...] = rscale
    field = state[...] + dot(proj[...], scaled, ((1,), (1,)))
    f_out[...] = field
    low = field.astype(BF16)
    for m in range(fb_out.shape[0]):
        fb_out[m] = low


def loss_kernel(me, every, field, target, wm, proj, scaled, gain, fg_out, keep_out, send_out):
    members, variables, _ = every.shape
    eps_fair = (1.0 - FAIRNESS) / members
    coef_pair = (1.0 - eps_fair) / (members * (members - 1))
    smooth = SMOOTHING * SMOOTHING
    f = field[...]
    weight_map = wm[...]
    d = f - target[...]
    s = d * d + smooth
    r = lax.rsqrt(s)
    spread, slope = s * r, d * r
    pair_total = jnp.full_like(f, -SMOOTHING)
    pair_slope = jnp.zeros_like(f)
    for k in range(members):
        other = jnp.where(me[0] == k, f, every[k].astype(F32))
        d = f - other
        s = d * d + smooth
        r = lax.rsqrt(s)
        pair_total = pair_total + s * r
        pair_slope = pair_slope + d * r
    terms = weight_map * (spread / members - 0.5 * coef_pair * pair_total)
    loss = jnp.sum(jnp.sum(terms, axis=0, keepdims=True), axis=1, keepdims=True)
    fore_grad = (weight_map * (slope / members - coef_pair * pair_slope)).astype(BF16)
    fg_out[...] = fore_grad
    values = scaled[...]
    wout = dot(fore_grad, values, ((1,), (0,)))
    scaled_grad = dot(fore_grad, proj[...], ((0,), (0,)))
    product = jnp.sum(scaled_grad * values.astype(F32), axis=0, keepdims=True) / gain[...]
    half = wout.shape[1] // 2
    upper = me[1] == 1

    def store(out, left):
        out[:variables, :] = jnp.where(left, wout[:, :half], wout[:, half:])
        out[variables : variables + 1, :] = jnp.where(left, product[:, :half], product[:, half:])
        out[variables + 1 : variables + 2, :] = jnp.broadcast_to(loss, (1, half))
        out[variables + 2 :, :] = jnp.zeros((ROWS - variables - 2, half), F32)

    store(keep_out, jnp.logical_not(upper))
    store(send_out, upper)


def back_kernel(fore_grad, proj, scaled, gain, rscale, et, own_out, near_out, far_out):
    channels = scaled.shape[1]
    rim = near_out.shape[0]
    mesh_count = own_out.shape[0]
    scaled_grad = dot(fore_grad[...], proj[...], ((0,), (0,)))
    values = scaled[...].astype(F32)
    norm_grad = scaled_grad * gain[...]
    first = jnp.sum(norm_grad, axis=1, keepdims=True) / channels
    second = jnp.sum(scaled_grad * values, axis=1, keepdims=True) / channels
    mixed_grad = rscale[...] * (norm_grad - first - values * (1.0 / gain[...]) * second)
    mixed_grad = mixed_grad.astype(BF16)
    near_out[...] = dot(et[:rim], mixed_grad, ((1,), (0,))).astype(BF16)
    far_out[...] = dot(et[rim + mesh_count :], mixed_grad, ((1,), (0,))).astype(BF16)
    own_out[...] = dot(et[rim : rim + mesh_count], mixed_grad, ((1,), (0,)))


def finish_latent_kernel(me, own, near, far, out):
    rim = near.shape[0]
    a, b = near[...].astype(F32), far[...].astype(F32)
    second = me[1] == 1
    out[0, :rim] = (own[:rim] + jnp.where(second, a, b)).astype(BF16)
    out[0, rim:] = (own[rim:] + jnp.where(second, b, a)).astype(BF16)


def fold_kernel(parts, earlier, out):
    total = jnp.sum(parts[...], axis=0)
    for i in range(out.shape[0]):
        out[i] = total


def finish_weights_kernel(me, mine, other, wout_out, gain_out, loss_out):
    variables, channels = wout_out.shape
    half = channels // 2
    left = me[1] == 0
    a, b = mine[...], other[...]
    first = jnp.where(left, a, b)
    second = jnp.where(left, b, a)
    wout_out[:, :half] = first[:variables]
    wout_out[:, half:] = second[:variables]
    gain_out[:, :half] = first[variables : variables + 1]
    gain_out[:, half:] = second[variables : variables + 1]
    loss_out[...] = first[variables + 1 : variables + 2, :1]


def per_device(
    latent,
    grid_latent_skip,
    initial_member_state,
    target,
    neighbours,
    edge_weight,
    area_weight,
    variable_weight,
    output_projection,
    layer_norm_gain,
):
    latent, skip, state = latent[0], grid_latent_skip[0], initial_member_state[0]
    mesh_count, channels = latent.shape
    points = skip.shape[0]
    rim = mesh_count // 2
    extent = mesh_count + 2 * rim
    variables = output_projection.shape[0]
    members = lax.axis_size(MEMBER)
    slabs = lax.axis_size(GRID)
    plane = lax.axis_size(PLANE)
    half = channels // 2
    gain = layer_norm_gain[None]
    swap = [(0, 1), (1, 0)]
    links = [((i + 1) % slabs, (i + 2) % slabs) for i in range(0, slabs, 2)]
    links = links + [(j, i) for i, j in links]
    core, slab = lax.axis_index("c"), lax.axis_index(GRID)
    far_there = jnp.logical_and(slab > 0, slab < slabs - 1)
    me = jnp.stack([lax.axis_index(MEMBER), core, far_there]).astype(jnp.int32)

    near_send, far_send = call(
        cut_kernel,
        [((rim, channels), BF16), ((rim, channels), BF16)],
        "sh",
        [pltpu.SemaphoreType.DMA((2,))],
    )(me, latent)
    far = lax.ppermute(far_send, GRID, links)
    near = lax.ppermute(near_send, "c", swap)
    et, edges, part, weight_map, state = call(
        prepare_kernel,
        [
            ((extent, points), BF16),
            ((points, 2 * rim), BF16),
            ((points, channels), F32),
            ((variables, points), F32),
            ((variables, points), F32),
        ],
        "shhhhhhhv",
        [
            pltpu.VMEM(neighbours.shape, jnp.int32),
            pltpu.VMEM(edge_weight.shape, F32),
            pltpu.VMEM((1, variables), F32),
            pltpu.VMEM((1, points), F32),
            pltpu.VMEM((mesh_count, channels), BF16),
            pltpu.VMEM((points, channels), BF16),
            pltpu.VMEM((variables, 1, points), F32),
            pltpu.SemaphoreType.DMA((7,)),
        ],
        flops=6 * points * mesh_count * channels,
        moved=8_000_000,
    )(
        me, neighbours, edge_weight, variable_weight[None], area_weight[None], latent, skip,
        state.reshape(variables, 1, points), near,
    )
    field, copies, scaled, rscale = call(
        forward_kernel,
        [
            ((variables, points), F32),
            ((members, variables, points), BF16),
            ((points, channels), BF16),
            ((points, 1), F32),
        ],
        flops=2 * points * channels * (2 * rim + variables),
        moved=5_000_000,
    )(part, edges, far, gain, output_projection, state)
    every = lax.all_to_all(copies, MEMBER, 0, 0, tiled=True)
    fore_grad, keep, send = call(
        loss_kernel,
        [((variables, points), BF16), ((ROWS, half), F32), ((ROWS, half), F32)],
        "s",
        flops=4 * points * channels * variables,
        moved=4_000_000,
    )(me, every, field, target, weight_map, output_projection, scaled, gain)

    met = keep + lax.ppermute(send, "c", swap)
    own, near_grad, far_grad = call(
        back_kernel,
        [((mesh_count, channels), F32), ((rim, channels), BF16), ((rim, channels), BF16)],
        flops=2 * points * channels * (extent + variables),
        moved=6_000_000,
    )(fore_grad, output_projection, scaled, gain, rscale, et)
    far_grad = lax.ppermute(far_grad, GRID, links)
    near_grad = lax.ppermute(near_grad, "c", swap)
    (latent_grad,) = call(finish_latent_kernel, [((1, mesh_count, channels), BF16)], "s")(
        me, own, near_grad, far_grad
    )
    depth, rows = lax.axis_size("z"), ROWS // plane
    parts = lax.all_to_all(met.reshape(plane, rows, half), PLANE, 0, 0, tiled=True)
    (parts,) = call(fold_kernel, [((depth, rows, half), F32)], "va")(parts, own)
    parts = lax.all_to_all(parts, "z", 0, 0, tiled=True)
    (parts,) = call(fold_kernel, [((plane, rows, half), F32)], "vh")(parts, latent_grad)
    mine = lax.all_to_all(parts, PLANE, 0, 0, tiled=True).reshape(ROWS, half)
    other = lax.ppermute(mine, "c", swap)
    wout, gain_grad, loss = call(
        finish_weights_kernel,
        [((variables, channels), F32), ((1, channels), F32), ((1, 1), F32)],
        "s",
    )(me, mine, other)
    fair_crps = loss[0, 0] / (points * slabs * variables)
    return (fair_crps, latent_grad, wout, gain_grad[0])


def solution(mesh):
    fine = Mesh(mesh.devices.reshape(2, 4, 2, 8, 2), ("xl", "y", "xh", "z", "c"))
    placed = (
        P(MEMBER, GRID, None),
        P(MEMBER, GRID, None),
        P(MEMBER, None, GRID),
        P(None, GRID),
        P(None, GRID),
        P(None, GRID),
        P(GRID),
        P(),
        P(),
        P(),
    )
    return jax.shard_map(
        per_device,
        mesh=fine,
        in_specs=placed,
        out_specs=(P(), P(MEMBER, GRID, None), P(), P()),
        check_vma=False,
    )
```

```python
import jax
import jax.numpy as jnp
from jax import lax
from jax.experimental import pallas as pl
from jax.experimental.pallas import tpu as pltpu
from jax.sharding import Mesh
from jax.sharding import PartitionSpec as P

SMOOTHING = 0.25
FAIRNESS = 0.95
NORM_EPS = 1e-05
MEMBER = ("xl", "y")
GRID = ("xh", "z", "c")
PLANE = ("xl", "y", "xh")
ROWS = 128
BF16 = jnp.bfloat16
F32 = jnp.float32
VMEM_LIMIT = 24 * 1024 * 1024


def dot(a, b, dims):
    return lax.dot_general(a, b, (dims, ((), ())), preferred_element_type=F32)


def call(kernel, outs, spaces="", scratch=(), flops=0, moved=0):
    places = {"s": pltpu.SMEM, "h": pltpu.HBM, "a": pl.ANY, "v": pltpu.VMEM}

    def run(*operands):
        letters = spaces.ljust(len(operands), "v")
        operands = [
            pltpu.with_memory_space_constraint(x, pltpu.HBM) if c == "h" else x
            for x, c in zip(operands, letters)
        ]
        return pl.pallas_call(
            kernel,
            out_shape=[jax.ShapeDtypeStruct(s, d) for s, d in outs],
            in_specs=[pl.BlockSpec(memory_space=places[c]) for c in letters],
            out_specs=[pl.BlockSpec(memory_space=pltpu.VMEM) for _ in outs],
            scratch_shapes=list(scratch),
            compiler_params=pltpu.CompilerParams(vmem_limit_bytes=VMEM_LIMIT),
            cost_estimate=pl.CostEstimate(flops=flops, bytes_accessed=moved, transcendentals=0),
        )(*operands)

    return run


def cut_kernel(latent, first_out, second_out, sems):
    rim = first_out.shape[0]
    core = lax.axis_index("c")
    start = pl.multiple_of((1 - core) * rim, rim)
    other = pl.multiple_of(core * rim, rim)
    one = pltpu.make_async_copy(latent.at[pl.ds(start, rim)], first_out, sems.at[0])
    two = pltpu.make_async_copy(latent.at[pl.ds(other, rim)], second_out, sems.at[1])
    one.start()
    two.start()
    one.wait()
    two.wait()


def borrowed_rows(distance):
    core, slab = lax.axis_index("c"), lax.axis_index(GRID)
    inner = jnp.logical_and(slab > 0, slab < lax.axis_size(GRID) - 1)
    return (1 - core) * distance, core * distance, inner


def prepare_kernel(
    nb_in, ew_in, vw_in, area_in, latent_in, skip_in, state_in, near,
    far_out, part_out, wm_out, state_out,
    nb, ew, vw, area, latent, skip, state, sems,
):
    pairs = (
        (nb_in, nb), (ew_in, ew), (vw_in, vw), (area_in, area),
        (latent_in, latent), (skip_in, skip), (state_in, state),
    )
    copies = [pltpu.make_async_copy(a, b, sems.at[i]) for i, (a, b) in enumerate(pairs)]
    for copy in copies:
        copy.start()
    for copy in copies[:4]:
        copy.wait()
    slots, points = nb.shape
    mesh_count = latent.shape[0]
    rim = mesh_count // 2
    near_start, far_start, far_there = borrowed_rows(rim + mesh_count)
    weights = ew[...]
    weights = weights / jnp.sum(weights, axis=0, keepdims=True)
    rows = nb[...]
    both = jnp.concatenate(
        [rows.astype(F32), weights, jnp.zeros((8 - 2 * slots, points), F32)], axis=0
    )
    columns = jnp.transpose(both)
    ids = columns.astype(jnp.int32)

    def edges(start, count):
        lane = lax.broadcasted_iota(jnp.int32, (points, count), 1) + start
        total = jnp.zeros((points, count), F32)
        for k in range(slots):
            total = total + jnp.where(
                lane == ids[:, k : k + 1], columns[:, slots + k : slots + k + 1], 0.0
            )
        return total

    def parts(value):
        high = value.astype(BF16)
        return high, (value - high.astype(F32)).astype(BF16)

    near_high, near_low = parts(edges(near_start, rim))
    own_high, own_low = parts(edges(rim, mesh_count))
    far_high, far_low = parts(jnp.where(far_there, edges(far_start, rim), 0.0))
    far_out[:, :rim] = far_high
    far_out[:, rim:] = far_low
    copies[4].wait()
    borrowed, own = near[...], latent[...]
    mix = (
        dot(near_high, borrowed, ((1,), (0,)))
        + dot(near_low, borrowed, ((1,), (0,)))
        + dot(own_high, own, ((1,), (0,)))
        + dot(own_low, own, ((1,), (0,)))
    )
    copies[5].wait()
    part_out[...] = skip[...].astype(F32) + mix
    variables = vw.shape[1]
    diagonal = lax.broadcasted_iota(jnp.int32, (variables, variables), 0) == (
        lax.broadcasted_iota(jnp.int32, (variables, variables), 1)
    )
    vw_column = jnp.sum(jnp.where(diagonal, vw[...], 0.0), axis=1, keepdims=True)
    wm_out[...] = vw_column * area[...]
    copies[6].wait()
    state_out[...] = state[:, 0, :]


def forward_kernel(part, edges, far, gain, proj, state, f_out, fb_out, sc_out, rs_out):
    rim = far.shape[0]
    borrowed = far[...]
    mixed = (
        part[...]
        + dot(edges[:, :rim], borrowed, ((1,), (0,)))
        + dot(edges[:, rim:], borrowed, ((1,), (0,)))
    )
    centred = mixed - jnp.mean(mixed, axis=1, keepdims=True)
    rscale = lax.rsqrt(jnp.mean(centred * centred, axis=1, keepdims=True) + NORM_EPS)
    scaled = (centred * rscale * gain[...]).astype(BF16)
    sc_out[...] = scaled
    rs_out[...] = rscale
    field = state[...] + dot(proj[...], scaled, ((1,), (1,)))
    f_out[...] = field
    low = field.astype(BF16)
    for m in range(fb_out.shape[0]):
        fb_out[m] = low


def loss_kernel(every, field, target, wm, proj, scaled, gain, fg_out, keep_out, send_out):
    members, variables, _ = every.shape
    eps_fair = (1.0 - FAIRNESS) / members
    coef_pair = (1.0 - eps_fair) / (members * (members - 1))
    smooth = SMOOTHING * SMOOTHING
    member = lax.axis_index(MEMBER)
    f = field[...]
    weight_map = wm[...]
    d = f - target[...]
    s = d * d + smooth
    r = lax.rsqrt(s)
    spread, slope = s * r, d * r
    pair_total = jnp.full_like(f, -SMOOTHING)
    pair_slope = jnp.zeros_like(f)
    for k in range(members):
        other = jnp.where(member == k, f, every[k].astype(F32))
        d = f - other
        s = d * d + smooth
        r = lax.rsqrt(s)
        pair_total = pair_total + s * r
        pair_slope = pair_slope + d * r
    terms = weight_map * (spread / members - 0.5 * coef_pair * pair_total)
    loss = jnp.sum(jnp.sum(terms, axis=0, keepdims=True), axis=1, keepdims=True)
    fore_grad = (weight_map * (slope / members - coef_pair * pair_slope)).astype(BF16)
    fg_out[...] = fore_grad
    values = scaled[...]
    wout = dot(fore_grad, values, ((1,), (0,)))
    scaled_grad = dot(fore_grad, proj[...], ((0,), (0,)))
    product = jnp.sum(scaled_grad * values.astype(F32), axis=0, keepdims=True) / gain[...]
    half = wout.shape[1] // 2
    upper = lax.axis_index("c") == 1

    def store(out, left):
        out[:variables, :] = jnp.where(left, wout[:, :half], wout[:, half:])
        out[variables : variables + 1, :] = jnp.where(left, product[:, :half], product[:, half:])
        out[variables + 1 : variables + 2, :] = jnp.broadcast_to(loss, (1, half))
        out[variables + 2 :, :] = jnp.zeros((ROWS - variables - 2, half), F32)

    store(keep_out, jnp.logical_not(upper))
    store(send_out, upper)


def back_kernel(nb, ew, fore_grad, proj, scaled, gain, rscale, own_out, near_out, far_out):
    channels = scaled.shape[1]
    rim = near_out.shape[0]
    mesh_count = own_out.shape[0]
    scaled_grad = dot(fore_grad[...], proj[...], ((0,), (0,)))
    values = scaled[...].astype(F32)
    norm_grad = scaled_grad * gain[...]
    first = jnp.sum(norm_grad, axis=1, keepdims=True) / channels
    second = jnp.sum(scaled_grad * values, axis=1, keepdims=True) / channels
    mixed_grad = rscale[...] * (norm_grad - first - values * (1.0 / gain[...]) * second)
    mixed_grad = mixed_grad.astype(BF16)
    weights = ew[...]
    weights = weights / jnp.sum(weights, axis=0, keepdims=True)
    rows = nb[...]
    near_start, far_start, far_there = borrowed_rows(rim + mesh_count)

    def back(start, count, there=None):
        row = lax.broadcasted_iota(jnp.int32, (count, nb.shape[1]), 0) + start
        edges = jnp.zeros(row.shape, F32)
        for k in range(nb.shape[0]):
            edges = edges + jnp.where(row == rows[k : k + 1], weights[k : k + 1], 0.0)
        if there is not None:
            edges = jnp.where(there, edges, 0.0)
        return dot(edges.astype(BF16), mixed_grad, ((1,), (0,)))

    far_out[...] = back(far_start, rim, far_there).astype(BF16)
    near_out[...] = back(near_start, rim).astype(BF16)
    own_out[...] = back(rim, mesh_count)


def finish_latent_kernel(own, near, far, earlier, out):
    rim = near.shape[0]
    a, b = near[...].astype(F32), far[...].astype(F32)
    second = lax.axis_index("c") == 1
    out[0, :rim] = (own[:rim] + jnp.where(second, a, b)).astype(BF16)
    out[0, rim:] = (own[rim:] + jnp.where(second, b, a)).astype(BF16)


def fold_kernel(parts, *rest):
    out = rest[-1]
    total = jnp.sum(parts[...], axis=0)
    for i in range(out.shape[0]):
        out[i] = total


def finish_weights_kernel(mine, other, earlier, wout_out, gain_out, loss_out):
    variables, channels = wout_out.shape
    half = channels // 2
    left = lax.axis_index("c") == 0
    a, b = mine[...], other[...]
    first = jnp.where(left, a, b)
    second = jnp.where(left, b, a)
    wout_out[:, :half] = first[:variables]
    wout_out[:, half:] = second[:variables]
    gain_out[:, :half] = first[variables : variables + 1]
    gain_out[:, half:] = second[variables : variables + 1]
    loss_out[...] = first[variables + 1 : variables + 2, :1]


def per_device(
    latent,
    grid_latent_skip,
    initial_member_state,
    target,
    neighbours,
    edge_weight,
    area_weight,
    variable_weight,
    output_projection,
    layer_norm_gain,
):
    latent, skip, state = latent[0], grid_latent_skip[0], initial_member_state[0]
    mesh_count, channels = latent.shape
    points = skip.shape[0]
    rim = mesh_count // 2
    extent = mesh_count + 2 * rim
    variables = output_projection.shape[0]
    members = lax.axis_size(MEMBER)
    slabs = lax.axis_size(GRID)
    plane = lax.axis_size(PLANE)
    half = channels // 2
    gain = layer_norm_gain[None]
    swap = [(0, 1), (1, 0)]
    links = [((i + 1) % slabs, (i + 2) % slabs) for i in range(0, slabs, 2)]
    links = links + [(j, i) for i, j in links]

    near_send, far_send = call(
        cut_kernel,
        [((rim, channels), BF16), ((rim, channels), BF16)],
        "h",
        [pltpu.SemaphoreType.DMA((2,))],
    )(latent)
    far = lax.ppermute(far_send, GRID, links)
    near = lax.ppermute(near_send, "c", swap)
    edges, part, weight_map, state = call(
        prepare_kernel,
        [
            ((points, 2 * rim), BF16),
            ((points, channels), F32),
            ((variables, points), F32),
            ((variables, points), F32),
        ],
        "hhhhhhhv",
        [
            pltpu.VMEM(neighbours.shape, jnp.int32),
            pltpu.VMEM(edge_weight.shape, F32),
            pltpu.VMEM((1, variables), F32),
            pltpu.VMEM((1, points), F32),
            pltpu.VMEM((mesh_count, channels), BF16),
            pltpu.VMEM((points, channels), BF16),
            pltpu.VMEM((variables, 1, points), F32),
            pltpu.SemaphoreType.DMA((7,)),
        ],
        flops=6 * points * mesh_count * channels,
        moved=8_000_000,
    )(
        neighbours, edge_weight, variable_weight[None], area_weight[None], latent, skip,
        state.reshape(variables, 1, points), near,
    )
    field, copies, scaled, rscale = call(
        forward_kernel,
        [
            ((variables, points), F32),
            ((members, variables, points), BF16),
            ((points, channels), BF16),
            ((points, 1), F32),
        ],
        flops=2 * points * channels * (2 * rim + variables),
        moved=5_000_000,
    )(part, edges, far, gain, output_projection, state)
    every = lax.all_to_all(copies, MEMBER, 0, 0, tiled=True)
    fore_grad, keep, send = call(
        loss_kernel,
        [((variables, points), BF16), ((ROWS, half), F32), ((ROWS, half), F32)],
        flops=4 * points * channels * variables,
        moved=4_000_000,
    )(every, field, target, weight_map, output_projection, scaled, gain)

    met = keep + lax.ppermute(send, "c", swap)
    own, near_grad, far_grad = call(
        back_kernel,
        [((mesh_count, channels), F32), ((rim, channels), BF16), ((rim, channels), BF16)],
        flops=2 * points * channels * (extent + variables),
        moved=6_000_000,
    )(neighbours, edge_weight, fore_grad, output_projection, scaled, gain, rscale)
    far_grad = lax.ppermute(far_grad, GRID, links)
    near_grad = lax.ppermute(near_grad, "c", swap)
    depth, rows = lax.axis_size("z"), ROWS // plane
    parts = lax.all_to_all(met.reshape(plane, rows, half), PLANE, 0, 0, tiled=True)
    (parts,) = call(fold_kernel, [((depth, rows, half), F32)], "vaa")(
        parts, near_grad, far_grad
    )
    parts = lax.all_to_all(parts, "z", 0, 0, tiled=True)
    (parts,) = call(fold_kernel, [((plane, rows, half), F32)])(parts)
    mine = lax.all_to_all(parts, PLANE, 0, 0, tiled=True).reshape(ROWS, half)
    other = lax.ppermute(mine, "c", swap)
    (latent_grad,) = call(finish_latent_kernel, [((1, mesh_count, channels), BF16)], "vvva")(
        own, near_grad, far_grad, mine
    )
    wout, gain_grad, loss = call(
        finish_weights_kernel,
        [((variables, channels), F32), ((1, channels), F32), ((1, 1), F32)],
        "vvh",
    )(mine, other, latent_grad)
    fair_crps = loss[0, 0] / (points * slabs * variables)
    return (fair_crps, latent_grad, wout, gain_grad[0])


def solution(mesh):
    fine = Mesh(mesh.devices.reshape(2, 4, 2, 8, 2), ("xl", "y", "xh", "z", "c"))
    placed = (
        P(MEMBER, GRID, None),
        P(MEMBER, GRID, None),
        P(MEMBER, None, GRID),
        P(None, GRID),
        P(None, GRID),
        P(None, GRID),
        P(GRID),
        P(),
        P(),
        P(),
    )
    return jax.shard_map(
        per_device,
        mesh=fine,
        in_specs=placed,
        out_specs=(P(), P(MEMBER, GRID, None), P(), P()),
        check_vma=False,
    )
```

```python
import jax
import jax.numpy as jnp
from jax import lax
from jax.experimental import pallas as pl
from jax.experimental.pallas import tpu as pltpu
from jax.sharding import Mesh
from jax.sharding import PartitionSpec as P

SMOOTHING = 0.25
FAIRNESS = 0.95
NORM_EPS = 1e-05
MEMBER = ("xl", "y")
GRID = ("xh", "z", "c")
PLANE = ("xl", "y", "xh")
ROWS = 128
BF16 = jnp.bfloat16
F32 = jnp.float32
VMEM_LIMIT = 24 * 1024 * 1024


def dot(a, b, dims):
    return lax.dot_general(a, b, (dims, ((), ())), preferred_element_type=F32)


def call(kernel, outs, spaces="", scratch=(), flops=0, moved=0):
    places = {"s": pltpu.SMEM, "h": pltpu.HBM, "a": pl.ANY, "v": pltpu.VMEM}

    def run(*operands):
        letters = spaces.ljust(len(operands), "v")
        operands = [
            pltpu.with_memory_space_constraint(x, pltpu.HBM) if c == "h" else x
            for x, c in zip(operands, letters)
        ]
        return pl.pallas_call(
            kernel,
            out_shape=[jax.ShapeDtypeStruct(s, d) for s, d in outs],
            in_specs=[pl.BlockSpec(memory_space=places[c]) for c in letters],
            out_specs=[pl.BlockSpec(memory_space=pltpu.VMEM) for _ in outs],
            scratch_shapes=list(scratch),
            compiler_params=pltpu.CompilerParams(vmem_limit_bytes=VMEM_LIMIT),
            cost_estimate=pl.CostEstimate(flops=flops, bytes_accessed=moved, transcendentals=0),
        )(*operands)

    return run


def cut_kernel(latent, first_out, second_out, sems):
    rim = first_out.shape[0]
    core = lax.axis_index("c")
    start = pl.multiple_of((1 - core) * rim, rim)
    other = pl.multiple_of(core * rim, rim)
    one = pltpu.make_async_copy(latent.at[pl.ds(start, rim)], first_out, sems.at[0])
    two = pltpu.make_async_copy(latent.at[pl.ds(other, rim)], second_out, sems.at[1])
    one.start()
    two.start()
    one.wait()
    two.wait()


def borrowed_rows(distance):
    core, slab = lax.axis_index("c"), lax.axis_index(GRID)
    inner = jnp.logical_and(slab > 0, slab < lax.axis_size(GRID) - 1)
    return (1 - core) * distance, core * distance, inner


def prepare_kernel(
    nb_in, ew_in, vw_in, area_in, latent_in, skip_in, state_in, near,
    far_out, part_out, wm_out, state_out,
    nb, ew, vw, area, latent, skip, state, sems,
):
    pairs = (
        (nb_in, nb), (ew_in, ew), (vw_in, vw), (area_in, area),
        (latent_in, latent), (skip_in, skip), (state_in, state),
    )
    copies = [pltpu.make_async_copy(a, b, sems.at[i]) for i, (a, b) in enumerate(pairs)]
    for copy in copies:
        copy.start()
    for copy in copies[:4]:
        copy.wait()
    slots, points = nb.shape
    mesh_count = latent.shape[0]
    rim = mesh_count // 2
    near_start, far_start, far_there = borrowed_rows(rim + mesh_count)
    weights = ew[...]
    weights = weights / jnp.sum(weights, axis=0, keepdims=True)
    rows = nb[...]
    both = jnp.concatenate(
        [rows.astype(F32), weights, jnp.zeros((8 - 2 * slots, points), F32)], axis=0
    )
    columns = jnp.transpose(both)
    ids = columns.astype(jnp.int32)

    def edges(start, count):
        lane = lax.broadcasted_iota(jnp.int32, (points, count), 1) + start
        total = jnp.zeros((points, count), F32)
        for k in range(slots):
            total = total + jnp.where(
                lane == ids[:, k : k + 1], columns[:, slots + k : slots + k + 1], 0.0
            )
        return total

    def parts(value):
        high = value.astype(BF16)
        return high, (value - high.astype(F32)).astype(BF16)

    near_high, near_low = parts(edges(near_start, rim))
    own_high, own_low = parts(edges(rim, mesh_count))
    far_high, far_low = parts(jnp.where(far_there, edges(far_start, rim), 0.0))
    far_out[:, :rim] = far_high
    far_out[:, rim:] = far_low
    copies[4].wait()
    borrowed, own = near[...], latent[...]
    mix = (
        dot(near_high, borrowed, ((1,), (0,)))
        + dot(near_low, borrowed, ((1,), (0,)))
        + dot(own_high, own, ((1,), (0,)))
        + dot(own_low, own, ((1,), (0,)))
    )
    copies[5].wait()
    part_out[...] = skip[...].astype(F32) + mix
    variables = vw.shape[1]
    diagonal = lax.broadcasted_iota(jnp.int32, (variables, variables), 0) == (
        lax.broadcasted_iota(jnp.int32, (variables, variables), 1)
    )
    vw_column = jnp.sum(jnp.where(diagonal, vw[...], 0.0), axis=1, keepdims=True)
    wm_out[...] = vw_column * area[...]
    copies[6].wait()
    state_out[...] = state[:, 0, :]


def forward_kernel(part, edges, far, gain, proj, state, f_out, sc_out, rs_out):
    rim = far.shape[0]
    borrowed = far[...]
    mixed = (
        part[...]
        + dot(edges[:, :rim], borrowed, ((1,), (0,)))
        + dot(edges[:, rim:], borrowed, ((1,), (0,)))
    )
    centred = mixed - jnp.mean(mixed, axis=1, keepdims=True)
    rscale = lax.rsqrt(jnp.mean(centred * centred, axis=1, keepdims=True) + NORM_EPS)
    scaled = (centred * rscale * gain[...]).astype(BF16)
    sc_out[...] = scaled
    rs_out[...] = rscale
    f_out[...] = state[...] + dot(proj[...], scaled, ((1,), (1,)))


def loss_kernel(every, field, target, wm, proj, scaled, gain, fg_out, keep_out, send_out):
    members, variables, _ = every.shape
    eps_fair = (1.0 - FAIRNESS) / members
    coef_pair = (1.0 - eps_fair) / (members * (members - 1))
    smooth = SMOOTHING * SMOOTHING
    member = lax.axis_index(MEMBER)
    f = field[...]
    weight_map = wm[...]
    d = f - target[...]
    s = d * d + smooth
    r = lax.rsqrt(s)
    spread, slope = s * r, d * r
    pair_total = jnp.full_like(f, -SMOOTHING)
    pair_slope = jnp.zeros_like(f)
    for k in range(members):
        other = jnp.where(member == k, f, every[k])
        d = f - other
        s = d * d + smooth
        r = lax.rsqrt(s)
        pair_total = pair_total + s * r
        pair_slope = pair_slope + d * r
    terms = weight_map * (spread / members - 0.5 * coef_pair * pair_total)
    loss = jnp.sum(jnp.sum(terms, axis=0, keepdims=True), axis=1, keepdims=True)
    fore_grad = (weight_map * (slope / members - coef_pair * pair_slope)).astype(BF16)
    fg_out[...] = fore_grad
    values = scaled[...]
    wout = dot(fore_grad, values, ((1,), (0,)))
    scaled_grad = dot(fore_grad, proj[...], ((0,), (0,)))
    product = jnp.sum(scaled_grad * values.astype(F32), axis=0, keepdims=True) / gain[...]
    half = wout.shape[1] // 2
    upper = lax.axis_index("c") == 1

    def store(out, left):
        out[:variables, :] = jnp.where(left, wout[:, :half], wout[:, half:])
        out[variables : variables + 1, :] = jnp.where(left, product[:, :half], product[:, half:])
        out[variables + 1 : variables + 2, :] = jnp.broadcast_to(loss, (1, half))
        out[variables + 2 :, :] = jnp.zeros((ROWS - variables - 2, half), F32)

    store(keep_out, jnp.logical_not(upper))
    store(send_out, upper)


def back_kernel(earlier, nb, ew, fore_grad, proj, scaled, gain, rscale, own_out, near_out, far_out):
    channels = scaled.shape[1]
    rim = near_out.shape[0]
    mesh_count = own_out.shape[0]
    scaled_grad = dot(fore_grad[...], proj[...], ((0,), (0,)))
    values = scaled[...].astype(F32)
    norm_grad = scaled_grad * gain[...]
    first = jnp.sum(norm_grad, axis=1, keepdims=True) / channels
    second = jnp.sum(scaled_grad * values, axis=1, keepdims=True) / channels
    mixed_grad = rscale[...] * (norm_grad - first - values * (1.0 / gain[...]) * second)
    mixed_grad = mixed_grad.astype(BF16)
    weights = ew[...]
    weights = weights / jnp.sum(weights, axis=0, keepdims=True)
    rows = nb[...]
    near_start, far_start, far_there = borrowed_rows(rim + mesh_count)

    def back(start, count, there=None):
        row = lax.broadcasted_iota(jnp.int32, (count, nb.shape[1]), 0) + start
        edges = jnp.zeros(row.shape, F32)
        for k in range(nb.shape[0]):
            edges = edges + jnp.where(row == rows[k : k + 1], weights[k : k + 1], 0.0)
        if there is not None:
            edges = jnp.where(there, edges, 0.0)
        return dot(edges.astype(BF16), mixed_grad, ((1,), (0,)))

    far_out[...] = back(far_start, rim, far_there).astype(BF16)
    near_out[...] = back(near_start, rim).astype(BF16)
    own_out[...] = back(rim, mesh_count)


def finish_latent_kernel(own, near, far, out):
    rim = near.shape[0]
    a, b = near[...].astype(F32), far[...].astype(F32)
    second = lax.axis_index("c") == 1
    out[0, :rim] = (own[:rim] + jnp.where(second, a, b)).astype(BF16)
    out[0, rim:] = (own[rim:] + jnp.where(second, b, a)).astype(BF16)


def fold_kernel(parts, *rest):
    out = rest[-1]
    total = jnp.sum(parts[...], axis=0)
    for i in range(out.shape[0]):
        out[i] = total


def finish_weights_kernel(mine, other, wout_out, gain_out, loss_out):
    variables, channels = wout_out.shape
    half = channels // 2
    left = lax.axis_index("c") == 0
    a, b = mine[...], other[...]
    first = jnp.where(left, a, b)
    second = jnp.where(left, b, a)
    wout_out[:, :half] = first[:variables]
    wout_out[:, half:] = second[:variables]
    gain_out[:, :half] = first[variables : variables + 1]
    gain_out[:, half:] = second[variables : variables + 1]
    loss_out[...] = first[variables + 1 : variables + 2, :1]


def per_device(
    latent,
    grid_latent_skip,
    initial_member_state,
    target,
    neighbours,
    edge_weight,
    area_weight,
    variable_weight,
    output_projection,
    layer_norm_gain,
):
    latent, skip, state = latent[0], grid_latent_skip[0], initial_member_state[0]
    mesh_count, channels = latent.shape
    points = skip.shape[0]
    rim = mesh_count // 2
    extent = mesh_count + 2 * rim
    variables = output_projection.shape[0]
    members = lax.axis_size(MEMBER)
    slabs = lax.axis_size(GRID)
    plane = lax.axis_size(PLANE)
    half = channels // 2
    gain = layer_norm_gain[None]
    swap = [(0, 1), (1, 0)]
    links = [((i + 1) % slabs, (i + 2) % slabs) for i in range(0, slabs, 2)]
    links = links + [(j, i) for i, j in links]

    near_send, far_send = call(
        cut_kernel,
        [((rim, channels), BF16), ((rim, channels), BF16)],
        "h",
        [pltpu.SemaphoreType.DMA((2,))],
    )(latent)
    far = lax.ppermute(far_send, GRID, links)
    near = lax.ppermute(near_send, "c", swap)
    edges, part, weight_map, state = call(
        prepare_kernel,
        [
            ((points, 2 * rim), BF16),
            ((points, channels), F32),
            ((variables, points), F32),
            ((variables, points), F32),
        ],
        "hhhhhhhv",
        [
            pltpu.VMEM(neighbours.shape, jnp.int32),
            pltpu.VMEM(edge_weight.shape, F32),
            pltpu.VMEM((1, variables), F32),
            pltpu.VMEM((1, points), F32),
            pltpu.VMEM((mesh_count, channels), BF16),
            pltpu.VMEM((points, channels), BF16),
            pltpu.VMEM((variables, 1, points), F32),
            pltpu.SemaphoreType.DMA((7,)),
        ],
        flops=6 * points * mesh_count * channels,
        moved=8_000_000,
    )(
        neighbours, edge_weight, variable_weight[None], area_weight[None], latent, skip,
        state.reshape(variables, 1, points), near,
    )
    field, scaled, rscale = call(
        forward_kernel,
        [
            ((variables, points), F32),
            ((points, channels), BF16),
            ((points, 1), F32),
        ],
        flops=2 * points * channels * (2 * rim + variables),
        moved=5_000_000,
    )(part, edges, far, gain, output_projection, state)
    sent = jnp.broadcast_to(field.astype(jnp.float16)[None], (members, variables, points))
    every = lax.all_to_all(sent, MEMBER, 0, 0, tiled=True).astype(F32)
    fore_grad, keep, send = call(
        loss_kernel,
        [((variables, points), BF16), ((ROWS, half), F32), ((ROWS, half), F32)],
        flops=4 * points * channels * variables,
        moved=4_000_000,
    )(every, field, target, weight_map, output_projection, scaled, gain)

    met = keep + lax.ppermute(send, "c", swap)
    own, near_grad, far_grad = call(
        back_kernel,
        [((mesh_count, channels), F32), ((rim, channels), BF16), ((rim, channels), BF16)],
        flops=2 * points * channels * (extent + variables),
        moved=6_000_000,
        spaces="a",
    )(met, neighbours, edge_weight, fore_grad, output_projection, scaled, gain, rscale)
    far_grad = lax.ppermute(far_grad, GRID, links)
    near_grad = lax.ppermute(near_grad, "c", swap)
    (latent_grad,) = call(finish_latent_kernel, [((1, mesh_count, channels), BF16)])(
        own, near_grad, far_grad
    )
    depth, rows = lax.axis_size("z"), ROWS // plane
    parts = lax.all_to_all(met.reshape(plane, rows, half), PLANE, 0, 0, tiled=True)
    (parts,) = call(fold_kernel, [((depth, rows, half), F32)], "va")(parts, own)
    parts = lax.all_to_all(parts, "z", 0, 0, tiled=True)
    (parts,) = call(fold_kernel, [((plane, rows, half), F32)], "vh")(parts, latent_grad)
    mine = lax.all_to_all(parts, PLANE, 0, 0, tiled=True).reshape(ROWS, half)
    other = lax.ppermute(mine, "c", swap)
    wout, gain_grad, loss = call(
        finish_weights_kernel,
        [((variables, channels), F32), ((1, channels), F32), ((1, 1), F32)],
    )(mine, other)
    fair_crps = loss[0, 0] / (points * slabs * variables)
    return (fair_crps, latent_grad, wout, gain_grad[0])


def solution(mesh):
    fine = Mesh(mesh.devices.reshape(2, 4, 2, 8, 2), ("xl", "y", "xh", "z", "c"))
    placed = (
        P(MEMBER, GRID, None),
        P(MEMBER, GRID, None),
        P(MEMBER, None, GRID),
        P(None, GRID),
        P(None, GRID),
        P(None, GRID),
        P(GRID),
        P(),
        P(),
        P(),
    )
    return jax.shard_map(
        per_device,
        mesh=fine,
        in_specs=placed,
        out_specs=(P(), P(MEMBER, GRID, None), P(), P()),
        check_vma=False,
    )
```

```python
import functools

import jax
import jax.numpy as jnp
from jax import lax
from jax.experimental import pallas as pl
from jax.experimental.pallas import tpu as pltpu
from jax.sharding import Mesh
from jax.sharding import PartitionSpec as P

SMOOTHING = 0.25
FAIRNESS = 0.95
NORM_EPS = 1e-05
MEMBER = ("xl", "y")
GRID = ("xh", "z", "c")
PLANE = ("xl", "y", "xh")
CHUNK = 8
BF16 = jnp.bfloat16
F32 = jnp.float32
VMEM_LIMIT = 24 * 1024 * 1024


def dot(a, b, dims):
    return lax.dot_general(a, b, (dims, ((), ())), preferred_element_type=F32)


def call(kernel, outs, spaces="", scratch=(), flops=0, moved=0):
    places = {"s": pltpu.SMEM, "h": pltpu.HBM, "a": pl.ANY, "v": pltpu.VMEM}

    def run(*operands):
        letters = spaces.ljust(len(operands), "v")
        operands = [
            pltpu.with_memory_space_constraint(x, pltpu.HBM) if c == "h" else x
            for x, c in zip(operands, letters)
        ]
        return pl.pallas_call(
            kernel,
            out_shape=[jax.ShapeDtypeStruct(s, d) for s, d in outs],
            in_specs=[pl.BlockSpec(memory_space=places[c]) for c in letters],
            out_specs=[pl.BlockSpec(memory_space=pltpu.VMEM) for _ in outs],
            scratch_shapes=list(scratch),
            compiler_params=pltpu.CompilerParams(vmem_limit_bytes=VMEM_LIMIT),
            cost_estimate=pl.CostEstimate(flops=flops, bytes_accessed=moved, transcendentals=0),
        )(*operands)

    return run


def cut_kernel(latent, first_out, second_out, sems):
    rim = first_out.shape[0]
    core = lax.axis_index("c")
    start = pl.multiple_of((1 - core) * rim, rim)
    other = pl.multiple_of(core * rim, rim)
    one = pltpu.make_async_copy(latent.at[pl.ds(start, rim)], first_out, sems.at[0])
    two = pltpu.make_async_copy(latent.at[pl.ds(other, rim)], second_out, sems.at[1])
    one.start()
    two.start()
    one.wait()
    two.wait()


def borrowed_rows(distance):
    core, slab = lax.axis_index("c"), lax.axis_index(GRID)
    inner = jnp.logical_and(slab > 0, slab < lax.axis_size(GRID) - 1)
    return (1 - core) * distance, core * distance, inner


def prepare_kernel(
    nb_in, ew_in, vw_in, area_in, latent_in, skip_in, state_in, near,
    far_out, part_out, wm_out, state_out,
    nb, ew, vw, area, latent, skip, state, sems,
):
    pairs = (
        (nb_in, nb), (ew_in, ew), (vw_in, vw), (area_in, area),
        (latent_in, latent), (skip_in, skip), (state_in, state),
    )
    copies = [pltpu.make_async_copy(a, b, sems.at[i]) for i, (a, b) in enumerate(pairs)]
    for copy in copies:
        copy.start()
    for copy in copies[:4]:
        copy.wait()
    slots, points = nb.shape
    mesh_count = latent.shape[0]
    rim = mesh_count // 2
    near_start, far_start, far_there = borrowed_rows(rim + mesh_count)
    weights = ew[...]
    weights = weights / jnp.sum(weights, axis=0, keepdims=True)
    rows = nb[...]
    both = jnp.concatenate(
        [rows.astype(F32), weights, jnp.zeros((8 - 2 * slots, points), F32)], axis=0
    )
    columns = jnp.transpose(both)
    ids = columns.astype(jnp.int32)

    def edges(start, count):
        lane = lax.broadcasted_iota(jnp.int32, (points, count), 1) + start
        total = jnp.zeros((points, count), F32)
        for k in range(slots):
            total = total + jnp.where(
                lane == ids[:, k : k + 1], columns[:, slots + k : slots + k + 1], 0.0
            )
        return total

    def parts(value):
        high = value.astype(BF16)
        return high, (value - high.astype(F32)).astype(BF16)

    near_high, near_low = parts(edges(near_start, rim))
    own_high, own_low = parts(edges(rim, mesh_count))
    far_high, far_low = parts(jnp.where(far_there, edges(far_start, rim), 0.0))
    far_out[:, :rim] = far_high
    far_out[:, rim:] = far_low
    copies[4].wait()
    borrowed, own = near[...], latent[...]
    mix = (
        dot(near_high, borrowed, ((1,), (0,)))
        + dot(near_low, borrowed, ((1,), (0,)))
        + dot(own_high, own, ((1,), (0,)))
        + dot(own_low, own, ((1,), (0,)))
    )
    copies[5].wait()
    part_out[...] = skip[...].astype(F32) + mix
    variables = vw.shape[1]
    diagonal = lax.broadcasted_iota(jnp.int32, (variables, variables), 0) == (
        lax.broadcasted_iota(jnp.int32, (variables, variables), 1)
    )
    vw_column = jnp.sum(jnp.where(diagonal, vw[...], 0.0), axis=1, keepdims=True)
    wm_out[...] = vw_column * area[...]
    copies[6].wait()
    state_out[...] = state[:, 0, :]


def forward_kernel(part, edges, far, gain, proj, state, f_out, sc_out, rs_out):
    rim = far.shape[0]
    borrowed = far[...]
    mixed = (
        part[...]
        + dot(edges[:, :rim], borrowed, ((1,), (0,)))
        + dot(edges[:, rim:], borrowed, ((1,), (0,)))
    )
    centred = mixed - jnp.mean(mixed, axis=1, keepdims=True)
    rscale = lax.rsqrt(jnp.mean(centred * centred, axis=1, keepdims=True) + NORM_EPS)
    scaled = (centred * rscale * gain[...]).astype(BF16)
    sc_out[...] = scaled
    rs_out[...] = rscale
    f_out[...] = state[...] + dot(proj[...], scaled, ((1,), (1,)))


def loss_kernel(every, field, target, wm, proj, scaled, gain, fg_out, parts_out):
    members, variables, _ = every.shape
    eps_fair = (1.0 - FAIRNESS) / members
    coef_pair = (1.0 - eps_fair) / (members * (members - 1))
    smooth = SMOOTHING * SMOOTHING
    member = lax.axis_index(MEMBER)
    f = field[...]
    weight_map = wm[...]
    d = f - target[...]
    s = d * d + smooth
    r = lax.rsqrt(s)
    spread, slope = s * r, d * r
    pair_total = jnp.full_like(f, -SMOOTHING)
    pair_slope = jnp.zeros_like(f)
    for k in range(members):
        other = jnp.where(member == k, f, every[k])
        d = f - other
        s = d * d + smooth
        r = lax.rsqrt(s)
        pair_total = pair_total + s * r
        pair_slope = pair_slope + d * r
    terms = weight_map * (spread / members - 0.5 * coef_pair * pair_total)
    loss = jnp.sum(jnp.sum(terms, axis=0, keepdims=True), axis=1, keepdims=True)
    fore_grad = (weight_map * (slope / members - coef_pair * pair_slope)).astype(BF16)
    fg_out[...] = fore_grad
    values = scaled[...]
    wout = dot(fore_grad, values, ((1,), (0,)))
    scaled_grad = dot(fore_grad, proj[...], ((0,), (0,)))
    product = jnp.sum(scaled_grad * values.astype(F32), axis=0, keepdims=True) / gain[...]
    last = variables // CHUNK
    for i in range(last):
        parts_out[i] = wout[i * CHUNK : (i + 1) * CHUNK].astype(BF16)
    channels = wout.shape[1]
    high = loss.astype(BF16).astype(F32)
    rest = variables - last * CHUNK
    parts_out[last] = jnp.concatenate(
        [
            wout[last * CHUNK :],
            product,
            jnp.broadcast_to(high, (1, channels)),
            jnp.broadcast_to(loss - high, (1, channels)),
            jnp.zeros((CHUNK - rest - 3, channels), F32),
        ],
        axis=0,
    ).astype(BF16)
    for i in range(last + 1, parts_out.shape[0]):
        parts_out[i] = jnp.zeros((CHUNK, channels), BF16)


def back_kernel(nb, ew, fore_grad, proj, scaled, gain, rscale, own_out, near_out, far_out):
    channels = scaled.shape[1]
    rim = near_out.shape[0]
    mesh_count = own_out.shape[0]
    scaled_grad = dot(fore_grad[...], proj[...], ((0,), (0,)))
    values = scaled[...].astype(F32)
    norm_grad = scaled_grad * gain[...]
    first = jnp.sum(norm_grad, axis=1, keepdims=True) / channels
    second = jnp.sum(scaled_grad * values, axis=1, keepdims=True) / channels
    mixed_grad = rscale[...] * (norm_grad - first - values * (1.0 / gain[...]) * second)
    mixed_grad = mixed_grad.astype(BF16)
    weights = ew[...]
    weights = weights / jnp.sum(weights, axis=0, keepdims=True)
    rows = nb[...]
    near_start, far_start, far_there = borrowed_rows(rim + mesh_count)

    def back(start, count, there=None):
        row = lax.broadcasted_iota(jnp.int32, (count, nb.shape[1]), 0) + start
        edges = jnp.zeros(row.shape, F32)
        for k in range(nb.shape[0]):
            edges = edges + jnp.where(row == rows[k : k + 1], weights[k : k + 1], 0.0)
        if there is not None:
            edges = jnp.where(there, edges, 0.0)
        return dot(edges.astype(BF16), mixed_grad, ((1,), (0,)))

    far_out[...] = back(far_start, rim, far_there).astype(BF16)
    near_out[...] = back(near_start, rim).astype(BF16)
    own_out[...] = back(rim, mesh_count)


def finish_latent_kernel(own, near, far, out):
    rim = near.shape[0]
    a, b = near[...].astype(F32), far[...].astype(F32)
    second = lax.axis_index("c") == 1
    out[0, :rim] = (own[:rim] + jnp.where(second, a, b)).astype(BF16)
    out[0, rim:] = (own[rim:] + jnp.where(second, b, a)).astype(BF16)


def narrowed(total, variables):
    here = lax.axis_index(PLANE) == variables // CHUNK
    first = variables % CHUNK + 1
    loss = total[first : first + 1] + total[first + 1 : first + 2]
    high = loss.astype(BF16).astype(F32)
    row = lax.broadcasted_iota(jnp.int32, total.shape, 0)
    split = jnp.where(row == first, high, jnp.where(row == first + 1, loss - high, total))
    return jnp.where(here, split, total).astype(BF16)


def fold_kernel(parts, earlier, out):
    out[...] = jnp.sum(parts[...].astype(F32), axis=0)


def pair_kernel(variables, mine, met, earlier, out):
    total = narrowed(mine[...] + met[...], variables)
    for i in range(out.shape[0]):
        out[i] = total


def spread_kernel(variables, parts, out):
    total = narrowed(jnp.sum(parts[...].astype(F32), axis=0), variables)
    for i in range(out.shape[0]):
        out[i] = total


def finish_weights_kernel(count, parts, wout_out, gain_out, loss_out):
    variables = wout_out.shape[0]
    last = variables // CHUNK
    for i in range(last):
        wout_out[i * CHUNK : (i + 1) * CHUNK] = parts[i].astype(F32)
    chunk = parts[last].astype(F32)
    rest = variables - last * CHUNK
    wout_out[last * CHUNK :] = chunk[:rest]
    gain_out[...] = chunk[rest : rest + 1]
    loss = chunk[rest + 1 : rest + 2, :1] + chunk[rest + 2 : rest + 3, :1]
    loss_out[...] = loss * (1.0 / count)


def per_device(
    latent,
    grid_latent_skip,
    initial_member_state,
    target,
    neighbours,
    edge_weight,
    area_weight,
    variable_weight,
    output_projection,
    layer_norm_gain,
):
    latent, skip, state = latent[0], grid_latent_skip[0], initial_member_state[0]
    mesh_count, channels = latent.shape
    points = skip.shape[0]
    rim = mesh_count // 2
    extent = mesh_count + 2 * rim
    variables = output_projection.shape[0]
    members = lax.axis_size(MEMBER)
    slabs = lax.axis_size(GRID)
    plane = lax.axis_size(PLANE)
    gain = layer_norm_gain[None]
    swap = [(0, 1), (1, 0)]
    links = [((i + 1) % slabs, (i + 2) % slabs) for i in range(0, slabs, 2)]
    links = links + [(j, i) for i, j in links]

    near_send, far_send = call(
        cut_kernel,
        [((rim, channels), BF16), ((rim, channels), BF16)],
        "h",
        [pltpu.SemaphoreType.DMA((2,))],
    )(latent)
    far = lax.ppermute(far_send, GRID, links)
    near = lax.ppermute(near_send, "c", swap)
    edges, part, weight_map, state = call(
        prepare_kernel,
        [
            ((points, 2 * rim), BF16),
            ((points, channels), F32),
            ((variables, points), F32),
            ((variables, points), F32),
        ],
        "hhhhhhhv",
        [
            pltpu.VMEM(neighbours.shape, jnp.int32),
            pltpu.VMEM(edge_weight.shape, F32),
            pltpu.VMEM((1, variables), F32),
            pltpu.VMEM((1, points), F32),
            pltpu.VMEM((mesh_count, channels), BF16),
            pltpu.VMEM((points, channels), BF16),
            pltpu.VMEM((variables, 1, points), F32),
            pltpu.SemaphoreType.DMA((7,)),
        ],
        flops=6 * points * mesh_count * channels,
        moved=8_000_000,
    )(
        neighbours, edge_weight, variable_weight[None], area_weight[None], latent, skip,
        state.reshape(variables, 1, points), near,
    )
    field, scaled, rscale = call(
        forward_kernel,
        [
            ((variables, points), F32),
            ((points, channels), BF16),
            ((points, 1), F32),
        ],
        flops=2 * points * channels * (2 * rim + variables),
        moved=5_000_000,
    )(part, edges, far, gain, output_projection, state)
    sent = jnp.broadcast_to(field.astype(jnp.float16)[None], (members, variables, points))
    every = lax.all_to_all(sent, MEMBER, 0, 0, tiled=True).astype(F32)
    fore_grad, parts = call(
        loss_kernel,
        [((variables, points), BF16), ((plane, CHUNK, channels), BF16)],
        flops=4 * points * channels * variables,
        moved=4_000_000,
    )(every, field, target, weight_map, output_projection, scaled, gain)

    own, near_grad, far_grad = call(
        back_kernel,
        [((mesh_count, channels), F32), ((rim, channels), BF16), ((rim, channels), BF16)],
        flops=2 * points * channels * (extent + variables),
        moved=6_000_000,
    )(neighbours, edge_weight, fore_grad, output_projection, scaled, gain, rscale)
    far_grad = lax.ppermute(far_grad, GRID, links)
    near_grad = lax.ppermute(near_grad, "c", swap)
    (latent_grad,) = call(finish_latent_kernel, [((1, mesh_count, channels), BF16)])(
        own, near_grad, far_grad
    )
    parts = lax.all_to_all(parts, PLANE, 0, 0, tiled=True)
    (mine,) = call(fold_kernel, [((CHUNK, channels), F32)], "va")(parts, own)
    met = lax.ppermute(mine, "c", swap)
    depth = lax.axis_size("z")
    (parts,) = call(
        functools.partial(pair_kernel, variables), [((depth, CHUNK, channels), BF16)], "vvh"
    )(mine, met, latent_grad)
    parts = lax.all_to_all(parts, "z", 0, 0, tiled=True)
    (parts,) = call(
        functools.partial(spread_kernel, variables), [((plane, CHUNK, channels), BF16)]
    )(parts)
    parts = lax.all_to_all(parts, PLANE, 0, 0, tiled=True)
    wout, gain_grad, crps = call(
        functools.partial(finish_weights_kernel, points * slabs * variables),
        [((variables, channels), F32), ((1, channels), F32), ((1, 1), F32)],
    )(parts)
    return (crps[0, 0], latent_grad, wout, gain_grad[0])


def solution(mesh):
    fine = Mesh(mesh.devices.reshape(2, 4, 2, 8, 2), ("xl", "y", "xh", "z", "c"))
    placed = (
        P(MEMBER, GRID, None),
        P(MEMBER, GRID, None),
        P(MEMBER, None, GRID),
        P(None, GRID),
        P(None, GRID),
        P(None, GRID),
        P(GRID),
        P(),
        P(),
        P(),
    )
    return jax.shard_map(
        per_device,
        mesh=fine,
        in_specs=placed,
        out_specs=(P(), P(MEMBER, GRID, None), P(), P()),
        check_vma=False,
    )
```

```python
import functools

import jax
import jax.numpy as jnp
from jax import lax
from jax.experimental import pallas as pl
from jax.experimental.pallas import tpu as pltpu
from jax.sharding import Mesh
from jax.sharding import PartitionSpec as P

SMOOTHING = 0.25
FAIRNESS = 0.95
NORM_EPS = 1e-05
MEMBER = ("xl", "y")
GRID = ("xh", "z", "c")
PLANE = ("xl", "y", "xh")
CHUNK = 8
BF16 = jnp.bfloat16
F32 = jnp.float32
VMEM_LIMIT = 24 * 1024 * 1024


def dot(a, b, dims):
    return lax.dot_general(a, b, (dims, ((), ())), preferred_element_type=F32)


def call(kernel, outs, spaces="", scratch=(), flops=0, moved=0):
    places = {"s": pltpu.SMEM, "h": pltpu.HBM, "a": pl.ANY, "v": pltpu.VMEM}

    def run(*operands):
        letters = spaces.ljust(len(operands), "v")
        operands = [
            pltpu.with_memory_space_constraint(x, pltpu.HBM) if c == "h" else x
            for x, c in zip(operands, letters)
        ]
        return pl.pallas_call(
            kernel,
            out_shape=[jax.ShapeDtypeStruct(s, d) for s, d in outs],
            in_specs=[pl.BlockSpec(memory_space=places[c]) for c in letters],
            out_specs=[pl.BlockSpec(memory_space=pltpu.VMEM) for _ in outs],
            scratch_shapes=list(scratch),
            compiler_params=pltpu.CompilerParams(vmem_limit_bytes=VMEM_LIMIT),
            cost_estimate=pl.CostEstimate(flops=flops, bytes_accessed=moved, transcendentals=0),
        )(*operands)

    return run


def cut_kernel(latent, first_out, second_out, sems):
    rim = first_out.shape[0]
    core = lax.axis_index("c")
    start = pl.multiple_of((1 - core) * rim, rim)
    other = pl.multiple_of(core * rim, rim)
    one = pltpu.make_async_copy(latent.at[pl.ds(start, rim)], first_out, sems.at[0])
    two = pltpu.make_async_copy(latent.at[pl.ds(other, rim)], second_out, sems.at[1])
    one.start()
    two.start()
    one.wait()
    two.wait()


def borrowed_rows(distance):
    core, slab = lax.axis_index("c"), lax.axis_index(GRID)
    inner = jnp.logical_and(slab > 0, slab < lax.axis_size(GRID) - 1)
    return (1 - core) * distance, core * distance, inner


def prepare_kernel(
    nb_in, ew_in, vw_in, area_in, latent_in, skip_in, state_in, near,
    far_out, part_out, wm_out, state_out,
    nb, ew, vw, area, latent, skip, state, sems,
):
    pairs = (
        (nb_in, nb), (ew_in, ew), (vw_in, vw), (area_in, area),
        (latent_in, latent), (skip_in, skip), (state_in, state),
    )
    copies = [pltpu.make_async_copy(a, b, sems.at[i]) for i, (a, b) in enumerate(pairs)]
    for copy in copies:
        copy.start()
    for copy in copies[:4]:
        copy.wait()
    slots, points = nb.shape
    mesh_count = latent.shape[0]
    rim = mesh_count // 2
    near_start, far_start, far_there = borrowed_rows(rim + mesh_count)
    weights = ew[...]
    weights = weights / jnp.sum(weights, axis=0, keepdims=True)
    rows = nb[...]
    both = jnp.concatenate(
        [rows.astype(F32), weights, jnp.zeros((8 - 2 * slots, points), F32)], axis=0
    )
    columns = jnp.transpose(both)
    ids = columns.astype(jnp.int32)

    def edges(start, count):
        lane = lax.broadcasted_iota(jnp.int32, (points, count), 1) + start
        total = jnp.zeros((points, count), F32)
        for k in range(slots):
            total = total + jnp.where(
                lane == ids[:, k : k + 1], columns[:, slots + k : slots + k + 1], 0.0
            )
        return total

    def parts(value):
        high = value.astype(BF16)
        return high, (value - high.astype(F32)).astype(BF16)

    near_high, near_low = parts(edges(near_start, rim))
    own_high, own_low = parts(edges(rim, mesh_count))
    far_high, far_low = parts(jnp.where(far_there, edges(far_start, rim), 0.0))
    far_out[:, :rim] = far_high
    far_out[:, rim:] = far_low
    copies[4].wait()
    borrowed, own = near[...], latent[...]
    mix = (
        dot(near_high, borrowed, ((1,), (0,)))
        + dot(near_low, borrowed, ((1,), (0,)))
        + dot(own_high, own, ((1,), (0,)))
        + dot(own_low, own, ((1,), (0,)))
    )
    copies[5].wait()
    part_out[...] = skip[...].astype(F32) + mix
    variables = vw.shape[1]
    diagonal = lax.broadcasted_iota(jnp.int32, (variables, variables), 0) == (
        lax.broadcasted_iota(jnp.int32, (variables, variables), 1)
    )
    vw_column = jnp.sum(jnp.where(diagonal, vw[...], 0.0), axis=1, keepdims=True)
    wm_out[...] = vw_column * area[...]
    copies[6].wait()
    state_out[...] = state[:, 0, :]


def forward_kernel(part, edges, far, gain, proj, state, f_out, sc_out, rs_out):
    rim = far.shape[0]
    borrowed = far[...]
    mixed = (
        part[...]
        + dot(edges[:, :rim], borrowed, ((1,), (0,)))
        + dot(edges[:, rim:], borrowed, ((1,), (0,)))
    )
    centred = mixed - jnp.mean(mixed, axis=1, keepdims=True)
    rscale = lax.rsqrt(jnp.mean(centred * centred, axis=1, keepdims=True) + NORM_EPS)
    scaled = (centred * rscale * gain[...]).astype(BF16)
    sc_out[...] = scaled
    rs_out[...] = rscale
    f_out[...] = state[...] + dot(proj[...], scaled, ((1,), (1,)))


def loss_kernel(every, field, target, wm, proj, scaled, gain, fg_out, parts_out):
    members, variables, _ = every.shape
    eps_fair = (1.0 - FAIRNESS) / members
    coef_pair = (1.0 - eps_fair) / (members * (members - 1))
    smooth = SMOOTHING * SMOOTHING
    member = lax.axis_index(MEMBER)
    f = field[...]
    weight_map = wm[...]
    d = f - target[...]
    s = d * d + smooth
    r = lax.rsqrt(s)
    spread, slope = s * r, d * r
    pair_total = jnp.full_like(f, -SMOOTHING)
    pair_slope = jnp.zeros_like(f)
    for k in range(members):
        other = jnp.where(member == k, f, every[k])
        d = f - other
        s = d * d + smooth
        r = lax.rsqrt(s)
        pair_total = pair_total + s * r
        pair_slope = pair_slope + d * r
    terms = weight_map * (spread / members - 0.5 * coef_pair * pair_total)
    loss = jnp.sum(jnp.sum(terms, axis=0, keepdims=True), axis=1, keepdims=True)
    fore_grad = (weight_map * (slope / members - coef_pair * pair_slope)).astype(BF16)
    fg_out[...] = fore_grad
    values = scaled[...]
    wout = dot(fore_grad, values, ((1,), (0,)))
    scaled_grad = dot(fore_grad, proj[...], ((0,), (0,)))
    product = jnp.sum(scaled_grad * values.astype(F32), axis=0, keepdims=True) / gain[...]
    last = variables // CHUNK
    for i in range(last):
        parts_out[i] = wout[i * CHUNK : (i + 1) * CHUNK].astype(BF16)
    channels = wout.shape[1]
    high = loss.astype(BF16).astype(F32)
    rest = variables - last * CHUNK
    parts_out[last] = jnp.concatenate(
        [
            wout[last * CHUNK :],
            product,
            jnp.broadcast_to(high, (1, channels)),
            jnp.broadcast_to(loss - high, (1, channels)),
            jnp.zeros((CHUNK - rest - 3, channels), F32),
        ],
        axis=0,
    ).astype(BF16)
    for i in range(last + 1, parts_out.shape[0]):
        parts_out[i] = jnp.zeros((CHUNK, channels), BF16)


def back_kernel(nb, ew, fore_grad, proj, scaled, gain, rscale, own_out, near_out, far_out):
    channels = scaled.shape[1]
    rim = near_out.shape[0]
    mesh_count = own_out.shape[0]
    scaled_grad = dot(fore_grad[...], proj[...], ((0,), (0,)))
    values = scaled[...].astype(F32)
    norm_grad = scaled_grad * gain[...]
    first = jnp.sum(norm_grad, axis=1, keepdims=True) / channels
    second = jnp.sum(scaled_grad * values, axis=1, keepdims=True) / channels
    mixed_grad = rscale[...] * (norm_grad - first - values * (1.0 / gain[...]) * second)
    mixed_grad = mixed_grad.astype(BF16)
    weights = ew[...]
    weights = weights / jnp.sum(weights, axis=0, keepdims=True)
    rows = nb[...]
    near_start, far_start, far_there = borrowed_rows(rim + mesh_count)

    def back(start, count, there=None):
        row = lax.broadcasted_iota(jnp.int32, (count, nb.shape[1]), 0) + start
        edges = jnp.zeros(row.shape, F32)
        for k in range(nb.shape[0]):
            edges = edges + jnp.where(row == rows[k : k + 1], weights[k : k + 1], 0.0)
        if there is not None:
            edges = jnp.where(there, edges, 0.0)
        return dot(edges.astype(BF16), mixed_grad, ((1,), (0,)))

    far_out[...] = back(far_start, rim, far_there).astype(BF16)
    near_out[...] = back(near_start, rim).astype(BF16)
    own_out[...] = back(rim, mesh_count)


def finish_latent_kernel(own, near, far, out):
    rim = near.shape[0]
    a, b = near[...].astype(F32), far[...].astype(F32)
    second = lax.axis_index("c") == 1
    out[0, :rim] = (own[:rim] + jnp.where(second, a, b)).astype(BF16)
    out[0, rim:] = (own[rim:] + jnp.where(second, b, a)).astype(BF16)


def narrowed(total, variables):
    here = lax.axis_index(PLANE) == variables // CHUNK
    first = variables % CHUNK + 1
    loss = total[first : first + 1] + total[first + 1 : first + 2]
    high = loss.astype(BF16).astype(F32)
    row = lax.broadcasted_iota(jnp.int32, total.shape, 0)
    split = jnp.where(row == first, high, jnp.where(row == first + 1, loss - high, total))
    return jnp.where(here, split, total).astype(BF16)


def fold_kernel(parts, earlier, out):
    out[...] = jnp.sum(parts[...].astype(F32), axis=0)


def pair_kernel(variables, mine, met, out):
    total = narrowed(mine[...] + met[...], variables)
    for i in range(out.shape[0]):
        out[i] = total


def spread_kernel(variables, parts, earlier, out):
    total = narrowed(jnp.sum(parts[...].astype(F32), axis=0), variables)
    for i in range(out.shape[0]):
        out[i] = total


def finish_weights_kernel(count, parts, wout_out, gain_out, loss_out):
    variables = wout_out.shape[0]
    last = variables // CHUNK
    for i in range(last):
        wout_out[i * CHUNK : (i + 1) * CHUNK] = parts[i].astype(F32)
    chunk = parts[last].astype(F32)
    rest = variables - last * CHUNK
    wout_out[last * CHUNK :] = chunk[:rest]
    gain_out[...] = chunk[rest : rest + 1]
    loss = chunk[rest + 1 : rest + 2, :1] + chunk[rest + 2 : rest + 3, :1]
    loss_out[...] = loss * (1.0 / count)


def per_device(
    latent,
    grid_latent_skip,
    initial_member_state,
    target,
    neighbours,
    edge_weight,
    area_weight,
    variable_weight,
    output_projection,
    layer_norm_gain,
):
    latent, skip, state = latent[0], grid_latent_skip[0], initial_member_state[0]
    mesh_count, channels = latent.shape
    points = skip.shape[0]
    rim = mesh_count // 2
    extent = mesh_count + 2 * rim
    variables = output_projection.shape[0]
    members = lax.axis_size(MEMBER)
    slabs = lax.axis_size(GRID)
    plane = lax.axis_size(PLANE)
    gain = layer_norm_gain[None]
    swap = [(0, 1), (1, 0)]
    links = [((i + 1) % slabs, (i + 2) % slabs) for i in range(0, slabs, 2)]
    links = links + [(j, i) for i, j in links]

    near_send, far_send = call(
        cut_kernel,
        [((rim, channels), BF16), ((rim, channels), BF16)],
        "h",
        [pltpu.SemaphoreType.DMA((2,))],
    )(latent)
    far = lax.ppermute(far_send, GRID, links)
    near = lax.ppermute(near_send, "c", swap)
    edges, part, weight_map, state = call(
        prepare_kernel,
        [
            ((points, 2 * rim), BF16),
            ((points, channels), F32),
            ((variables, points), F32),
            ((variables, points), F32),
        ],
        "hhhhhhhv",
        [
            pltpu.VMEM(neighbours.shape, jnp.int32),
            pltpu.VMEM(edge_weight.shape, F32),
            pltpu.VMEM((1, variables), F32),
            pltpu.VMEM((1, points), F32),
            pltpu.VMEM((mesh_count, channels), BF16),
            pltpu.VMEM((points, channels), BF16),
            pltpu.VMEM((variables, 1, points), F32),
            pltpu.SemaphoreType.DMA((7,)),
        ],
        flops=6 * points * mesh_count * channels,
        moved=8_000_000,
    )(
        neighbours, edge_weight, variable_weight[None], area_weight[None], latent, skip,
        state.reshape(variables, 1, points), near,
    )
    field, scaled, rscale = call(
        forward_kernel,
        [
            ((variables, points), F32),
            ((points, channels), BF16),
            ((points, 1), F32),
        ],
        flops=2 * points * channels * (2 * rim + variables),
        moved=5_000_000,
    )(part, edges, far, gain, output_projection, state)
    sent = jnp.broadcast_to(field.astype(jnp.float16)[None], (members, variables, points))
    every = lax.all_to_all(sent, MEMBER, 0, 0, tiled=True).astype(F32)
    fore_grad, parts = call(
        loss_kernel,
        [((variables, points), BF16), ((plane, CHUNK, channels), BF16)],
        flops=4 * points * channels * variables,
        moved=4_000_000,
    )(every, field, target, weight_map, output_projection, scaled, gain)

    own, near_grad, far_grad = call(
        back_kernel,
        [((mesh_count, channels), F32), ((rim, channels), BF16), ((rim, channels), BF16)],
        flops=2 * points * channels * (extent + variables),
        moved=6_000_000,
    )(neighbours, edge_weight, fore_grad, output_projection, scaled, gain, rscale)
    far_grad = lax.ppermute(far_grad, GRID, links)
    near_grad = lax.ppermute(near_grad, "c", swap)
    (latent_grad,) = call(finish_latent_kernel, [((1, mesh_count, channels), BF16)])(
        own, near_grad, far_grad
    )
    parts = lax.all_to_all(parts, PLANE, 0, 0, tiled=True)
    (mine,) = call(fold_kernel, [((CHUNK, channels), F32)], "va")(parts, own)
    met = lax.ppermute(mine, "c", swap)
    depth = lax.axis_size("z")
    (parts,) = call(
        functools.partial(pair_kernel, variables), [((depth, CHUNK, channels), BF16)]
    )(mine, met)
    parts = lax.all_to_all(parts, "z", 0, 0, tiled=True)
    (parts,) = call(
        functools.partial(spread_kernel, variables), [((plane, CHUNK, channels), BF16)], "vh"
    )(parts, latent_grad)
    parts = lax.all_to_all(parts, PLANE, 0, 0, tiled=True)
    wout, gain_grad, crps = call(
        functools.partial(finish_weights_kernel, points * slabs * variables),
        [((variables, channels), F32), ((1, channels), F32), ((1, 1), F32)],
    )(parts)
    return (crps[0, 0], latent_grad, wout, gain_grad[0])


def solution(mesh):
    fine = Mesh(mesh.devices.reshape(2, 4, 2, 8, 2), ("xl", "y", "xh", "z", "c"))
    placed = (
        P(MEMBER, GRID, None),
        P(MEMBER, GRID, None),
        P(MEMBER, None, GRID),
        P(None, GRID),
        P(None, GRID),
        P(None, GRID),
        P(GRID),
        P(),
        P(),
        P(),
    )
    return jax.shard_map(
        per_device,
        mesh=fine,
        in_specs=placed,
        out_specs=(P(), P(MEMBER, GRID, None), P(), P()),
        check_vma=False,
    )
```

```python
import functools

import jax
import jax.numpy as jnp
from jax import lax
from jax.experimental import pallas as pl
from jax.experimental.pallas import tpu as pltpu
from jax.sharding import Mesh
from jax.sharding import PartitionSpec as P

SMOOTHING = 0.25
FAIRNESS = 0.95
NORM_EPS = 1e-05
MEMBER = ("xl", "y")
GRID = ("xh", "z", "c")
PLANE = ("xl", "y", "xh")
CHUNK = 8
BF16 = jnp.bfloat16
F32 = jnp.float32
VMEM_LIMIT = 24 * 1024 * 1024


def dot(a, b, dims):
    return lax.dot_general(a, b, (dims, ((), ())), preferred_element_type=F32)


def call(kernel, outs, spaces="", scratch=(), flops=0, moved=0):
    places = {"s": pltpu.SMEM, "h": pltpu.HBM, "a": pl.ANY, "v": pltpu.VMEM}

    def run(*operands):
        letters = spaces.ljust(len(operands), "v")
        operands = [
            pltpu.with_memory_space_constraint(x, pltpu.HBM) if c == "h" else x
            for x, c in zip(operands, letters)
        ]
        return pl.pallas_call(
            kernel,
            out_shape=[jax.ShapeDtypeStruct(s, d) for s, d in outs],
            in_specs=[pl.BlockSpec(memory_space=places[c]) for c in letters],
            out_specs=[pl.BlockSpec(memory_space=pltpu.VMEM) for _ in outs],
            scratch_shapes=list(scratch),
            compiler_params=pltpu.CompilerParams(vmem_limit_bytes=VMEM_LIMIT),
            cost_estimate=pl.CostEstimate(flops=flops, bytes_accessed=moved, transcendentals=0),
        )(*operands)

    return run


def cut_kernel(latent, first_out, second_out, sems):
    rim = first_out.shape[0]
    core = lax.axis_index("c")
    start = pl.multiple_of((1 - core) * rim, rim)
    other = pl.multiple_of(core * rim, rim)
    one = pltpu.make_async_copy(latent.at[pl.ds(start, rim)], first_out, sems.at[0])
    two = pltpu.make_async_copy(latent.at[pl.ds(other, rim)], second_out, sems.at[1])
    one.start()
    two.start()
    one.wait()
    two.wait()


def borrowed_rows(distance):
    core, slab = lax.axis_index("c"), lax.axis_index(GRID)
    inner = jnp.logical_and(slab > 0, slab < lax.axis_size(GRID) - 1)
    return (1 - core) * distance, core * distance, inner


def prepare_kernel(
    nb_in, ew_in, vw_in, area_in, latent_in, skip_in, state_in, near,
    far_out, part_out, wm_out, state_out,
    nb, ew, vw, area, latent, skip, state, sems,
):
    pairs = (
        (nb_in, nb), (ew_in, ew), (vw_in, vw), (area_in, area),
        (latent_in, latent), (skip_in, skip), (state_in, state),
    )
    copies = [pltpu.make_async_copy(a, b, sems.at[i]) for i, (a, b) in enumerate(pairs)]
    for copy in copies:
        copy.start()
    for copy in copies[:4]:
        copy.wait()
    slots, points = nb.shape
    mesh_count = latent.shape[0]
    rim = mesh_count // 2
    near_start, far_start, far_there = borrowed_rows(rim + mesh_count)
    weights = ew[...]
    weights = weights / jnp.sum(weights, axis=0, keepdims=True)
    rows = nb[...]
    both = jnp.concatenate(
        [rows.astype(F32), weights, jnp.zeros((8 - 2 * slots, points), F32)], axis=0
    )
    columns = jnp.transpose(both)
    ids = columns.astype(jnp.int32)

    def edges(start, count):
        lane = lax.broadcasted_iota(jnp.int32, (points, count), 1) + start
        total = jnp.zeros((points, count), F32)
        for k in range(slots):
            total = total + jnp.where(
                lane == ids[:, k : k + 1], columns[:, slots + k : slots + k + 1], 0.0
            )
        return total

    def parts(value):
        high = value.astype(BF16)
        return high, (value - high.astype(F32)).astype(BF16)

    near_high, near_low = parts(edges(near_start, rim))
    own_high, own_low = parts(edges(rim, mesh_count))
    far_high, far_low = parts(jnp.where(far_there, edges(far_start, rim), 0.0))
    far_out[:, :rim] = far_high
    far_out[:, rim:] = far_low
    copies[4].wait()
    borrowed, own = near[...], latent[...]
    mix = dot(
        jnp.concatenate([near_high, near_low, own_high, own_low], axis=1),
        jnp.concatenate([borrowed, borrowed, own, own], axis=0),
        ((1,), (0,)),
    )
    copies[5].wait()
    part_out[...] = skip[...].astype(F32) + mix
    variables = vw.shape[1]
    diagonal = lax.broadcasted_iota(jnp.int32, (variables, variables), 0) == (
        lax.broadcasted_iota(jnp.int32, (variables, variables), 1)
    )
    vw_column = jnp.sum(jnp.where(diagonal, vw[...], 0.0), axis=1, keepdims=True)
    wm_out[...] = vw_column * area[...]
    copies[6].wait()
    state_out[...] = state[:, 0, :]


def forward_kernel(part, edges, far, gain, proj, state, f_out, sc_out, rs_out):
    borrowed = far[...]
    twice = jnp.concatenate([borrowed, borrowed], axis=0)
    mixed = part[...] + dot(edges[...], twice, ((1,), (0,)))
    centred = mixed - jnp.mean(mixed, axis=1, keepdims=True)
    rscale = lax.rsqrt(jnp.mean(centred * centred, axis=1, keepdims=True) + NORM_EPS)
    scaled = (centred * rscale * gain[...]).astype(BF16)
    sc_out[...] = scaled
    rs_out[...] = rscale
    f_out[...] = state[...] + dot(proj[...], scaled, ((1,), (1,)))


def loss_kernel(every, field, target, wm, proj, scaled, gain, fg_out, parts_out):
    members, variables, _ = every.shape
    eps_fair = (1.0 - FAIRNESS) / members
    coef_pair = (1.0 - eps_fair) / (members * (members - 1))
    smooth = SMOOTHING * SMOOTHING
    member = lax.axis_index(MEMBER)
    f = field[...]
    weight_map = wm[...]
    d = f - target[...]
    s = d * d + smooth
    r = lax.rsqrt(s)
    spread, slope = s * r, d * r
    pair_total = jnp.full_like(f, -SMOOTHING)
    pair_slope = jnp.zeros_like(f)
    for k in range(members):
        other = jnp.where(member == k, f, every[k])
        d = f - other
        s = d * d + smooth
        r = lax.rsqrt(s)
        pair_total = pair_total + s * r
        pair_slope = pair_slope + d * r
    terms = weight_map * (spread / members - 0.5 * coef_pair * pair_total)
    loss = jnp.sum(jnp.sum(terms, axis=0, keepdims=True), axis=1, keepdims=True)
    fore_grad = (weight_map * (slope / members - coef_pair * pair_slope)).astype(BF16)
    fg_out[...] = fore_grad
    wout = dot(fore_grad, scaled[...], ((1,), (0,)))
    product = jnp.sum(wout * proj[...].astype(F32), axis=0, keepdims=True) / gain[...]
    last = variables // CHUNK
    for i in range(last):
        parts_out[i] = wout[i * CHUNK : (i + 1) * CHUNK].astype(BF16)
    channels = wout.shape[1]
    high = loss.astype(BF16).astype(F32)
    rest = variables - last * CHUNK
    parts_out[last] = jnp.concatenate(
        [
            wout[last * CHUNK :],
            product,
            jnp.broadcast_to(high, (1, channels)),
            jnp.broadcast_to(loss - high, (1, channels)),
            jnp.zeros((CHUNK - rest - 3, channels), F32),
        ],
        axis=0,
    ).astype(BF16)
    for i in range(last + 1, parts_out.shape[0]):
        parts_out[i] = jnp.zeros((CHUNK, channels), BF16)


def back_kernel(nb, ew, fore_grad, proj, scaled, gain, rscale, own_out, near_out, far_out):
    channels = scaled.shape[1]
    rim = near_out.shape[0]
    mesh_count = own_out.shape[0]
    scaled_grad = dot(fore_grad[...], proj[...], ((0,), (0,)))
    values = scaled[...].astype(F32)
    norm_grad = scaled_grad * gain[...]
    first = jnp.sum(norm_grad, axis=1, keepdims=True) / channels
    second = jnp.sum(scaled_grad * values, axis=1, keepdims=True) / channels
    mixed_grad = rscale[...] * (norm_grad - first - values * (1.0 / gain[...]) * second)
    mixed_grad = mixed_grad.astype(BF16)
    weights = ew[...]
    weights = weights / jnp.sum(weights, axis=0, keepdims=True)
    rows = nb[...]
    near_start, far_start, far_there = borrowed_rows(rim + mesh_count)

    def back(start, count, there=None):
        row = lax.broadcasted_iota(jnp.int32, (count, nb.shape[1]), 0) + start
        edges = jnp.zeros(row.shape, F32)
        for k in range(nb.shape[0]):
            edges = edges + jnp.where(row == rows[k : k + 1], weights[k : k + 1], 0.0)
        if there is not None:
            edges = jnp.where(there, edges, 0.0)
        return dot(edges.astype(BF16), mixed_grad, ((1,), (0,)))

    far_out[...] = back(far_start, rim, far_there).astype(BF16)
    near_out[...] = back(near_start, rim).astype(BF16)
    own_out[...] = back(rim, mesh_count)


def finish_latent_kernel(own, near, far, out):
    rim = near.shape[0]
    a, b = near[...].astype(F32), far[...].astype(F32)
    second = lax.axis_index("c") == 1
    out[0, :rim] = (own[:rim] + jnp.where(second, a, b)).astype(BF16)
    out[0, rim:] = (own[rim:] + jnp.where(second, b, a)).astype(BF16)


def narrowed(total, variables):
    here = lax.axis_index(PLANE) == variables // CHUNK
    first = variables % CHUNK + 1
    loss = total[first : first + 1] + total[first + 1 : first + 2]
    high = loss.astype(BF16).astype(F32)
    row = lax.broadcasted_iota(jnp.int32, total.shape, 0)
    split = jnp.where(row == first, high, jnp.where(row == first + 1, loss - high, total))
    return jnp.where(here, split, total).astype(BF16)


def fold_kernel(parts, earlier, out):
    out[...] = jnp.sum(parts[...].astype(F32), axis=0)


def pair_kernel(variables, mine, met, out):
    total = narrowed(mine[...] + met[...], variables)
    for i in range(out.shape[0]):
        out[i] = total


def spread_kernel(variables, parts, earlier, out):
    total = narrowed(jnp.sum(parts[...].astype(F32), axis=0), variables)
    for i in range(out.shape[0]):
        out[i] = total


def finish_weights_kernel(count, parts, wout_out, gain_out, loss_out):
    variables = wout_out.shape[0]
    last = variables // CHUNK
    for i in range(last):
        wout_out[i * CHUNK : (i + 1) * CHUNK] = parts[i].astype(F32)
    chunk = parts[last].astype(F32)
    rest = variables - last * CHUNK
    wout_out[last * CHUNK :] = chunk[:rest]
    gain_out[...] = chunk[rest : rest + 1]
    loss = chunk[rest + 1 : rest + 2, :1] + chunk[rest + 2 : rest + 3, :1]
    loss_out[...] = loss * (1.0 / count)


def per_device(
    latent,
    grid_latent_skip,
    initial_member_state,
    target,
    neighbours,
    edge_weight,
    area_weight,
    variable_weight,
    output_projection,
    layer_norm_gain,
):
    latent, skip, state = latent[0], grid_latent_skip[0], initial_member_state[0]
    mesh_count, channels = latent.shape
    points = skip.shape[0]
    rim = mesh_count // 2
    extent = mesh_count + 2 * rim
    variables = output_projection.shape[0]
    members = lax.axis_size(MEMBER)
    slabs = lax.axis_size(GRID)
    plane = lax.axis_size(PLANE)
    gain = layer_norm_gain[None]
    swap = [(0, 1), (1, 0)]
    links = [((i + 1) % slabs, (i + 2) % slabs) for i in range(0, slabs, 2)]
    links = links + [(j, i) for i, j in links]

    near_send, far_send = call(
        cut_kernel,
        [((rim, channels), BF16), ((rim, channels), BF16)],
        "h",
        [pltpu.SemaphoreType.DMA((2,))],
    )(latent)
    far = lax.ppermute(far_send, GRID, links)
    near = lax.ppermute(near_send, "c", swap)
    edges, part, weight_map, state = call(
        prepare_kernel,
        [
            ((points, 2 * rim), BF16),
            ((points, channels), F32),
            ((variables, points), F32),
            ((variables, points), F32),
        ],
        "hhhhhhhv",
        [
            pltpu.VMEM(neighbours.shape, jnp.int32),
            pltpu.VMEM(edge_weight.shape, F32),
            pltpu.VMEM((1, variables), F32),
            pltpu.VMEM((1, points), F32),
            pltpu.VMEM((mesh_count, channels), BF16),
            pltpu.VMEM((points, channels), BF16),
            pltpu.VMEM((variables, 1, points), F32),
            pltpu.SemaphoreType.DMA((7,)),
        ],
        flops=6 * points * mesh_count * channels,
        moved=8_000_000,
    )(
        neighbours, edge_weight, variable_weight[None], area_weight[None], latent, skip,
        state.reshape(variables, 1, points), near,
    )
    field, scaled, rscale = call(
        forward_kernel,
        [
            ((variables, points), F32),
            ((points, channels), BF16),
            ((points, 1), F32),
        ],
        flops=2 * points * channels * (2 * rim + variables),
        moved=5_000_000,
    )(part, edges, far, gain, output_projection, state)
    sent = jnp.broadcast_to(field.astype(jnp.float16)[None], (members, variables, points))
    every = lax.all_to_all(sent, MEMBER, 0, 0, tiled=True).astype(F32)
    fore_grad, parts = call(
        loss_kernel,
        [((variables, points), BF16), ((plane, CHUNK, channels), BF16)],
        flops=4 * points * channels * variables,
        moved=4_000_000,
    )(every, field, target, weight_map, output_projection, scaled, gain)

    own, near_grad, far_grad = call(
        back_kernel,
        [((mesh_count, channels), F32), ((rim, channels), BF16), ((rim, channels), BF16)],
        flops=2 * points * channels * (extent + variables),
        moved=6_000_000,
    )(neighbours, edge_weight, fore_grad, output_projection, scaled, gain, rscale)
    far_grad = lax.ppermute(far_grad, GRID, links)
    near_grad = lax.ppermute(near_grad, "c", swap)
    (latent_grad,) = call(finish_latent_kernel, [((1, mesh_count, channels), BF16)])(
        own, near_grad, far_grad
    )
    parts = lax.all_to_all(parts, PLANE, 0, 0, tiled=True)
    (mine,) = call(fold_kernel, [((CHUNK, channels), F32)], "va")(parts, own)
    met = lax.ppermute(mine, "c", swap)
    depth = lax.axis_size("z")
    (parts,) = call(
        functools.partial(pair_kernel, variables), [((depth, CHUNK, channels), BF16)]
    )(mine, met)
    parts = lax.all_to_all(parts, "z", 0, 0, tiled=True)
    (parts,) = call(
        functools.partial(spread_kernel, variables), [((plane, CHUNK, channels), BF16)], "vh"
    )(parts, latent_grad)
    parts = lax.all_to_all(parts, PLANE, 0, 0, tiled=True)
    wout, gain_grad, crps = call(
        functools.partial(finish_weights_kernel, points * slabs * variables),
        [((variables, channels), F32), ((1, channels), F32), ((1, 1), F32)],
    )(parts)
    return (crps[0, 0], latent_grad, wout, gain_grad[0])


def solution(mesh):
    fine = Mesh(mesh.devices.reshape(2, 4, 2, 8, 2), ("xl", "y", "xh", "z", "c"))
    placed = (
        P(MEMBER, GRID, None),
        P(MEMBER, GRID, None),
        P(MEMBER, None, GRID),
        P(None, GRID),
        P(None, GRID),
        P(None, GRID),
        P(GRID),
        P(),
        P(),
        P(),
    )
    return jax.shard_map(
        per_device,
        mesh=fine,
        in_specs=placed,
        out_specs=(P(), P(MEMBER, GRID, None), P(), P()),
        check_vma=False,
    )
```

```python
import functools

import jax
import jax.numpy as jnp
from jax import lax
from jax.experimental import pallas as pl
from jax.experimental.pallas import tpu as pltpu
from jax.sharding import Mesh
from jax.sharding import PartitionSpec as P

SMOOTHING = 0.25
FAIRNESS = 0.95
NORM_EPS = 1e-05
MEMBER = ("xl", "y")
GRID = ("xh", "z", "c")
PLANE = ("xl", "y", "xh")
CHUNK = 8
BF16 = jnp.bfloat16
F32 = jnp.float32
VMEM_LIMIT = 24 * 1024 * 1024


def dot(a, b, dims):
    return lax.dot_general(a, b, (dims, ((), ())), preferred_element_type=F32)


def call(kernel, outs, spaces="", scratch=(), flops=0, moved=0):
    places = {"s": pltpu.SMEM, "h": pltpu.HBM, "a": pl.ANY, "v": pltpu.VMEM}

    def run(*operands):
        letters = spaces.ljust(len(operands), "v")
        operands = [
            pltpu.with_memory_space_constraint(x, pltpu.HBM) if c == "h" else x
            for x, c in zip(operands, letters)
        ]
        return pl.pallas_call(
            kernel,
            out_shape=[jax.ShapeDtypeStruct(s, d) for s, d in outs],
            in_specs=[pl.BlockSpec(memory_space=places[c]) for c in letters],
            out_specs=[pl.BlockSpec(memory_space=pltpu.VMEM) for _ in outs],
            scratch_shapes=list(scratch),
            compiler_params=pltpu.CompilerParams(vmem_limit_bytes=VMEM_LIMIT),
            cost_estimate=pl.CostEstimate(flops=flops, bytes_accessed=moved, transcendentals=0),
        )(*operands)

    return run


def cut_kernel(latent, out, sem):
    rim = out.shape[0]
    start = pl.multiple_of(lax.axis_index("c") * rim, rim)
    copy = pltpu.make_async_copy(latent.at[pl.ds(start, rim)], out, sem)
    copy.start()
    copy.wait()


def borrowed_rows(distance):
    core, slab = lax.axis_index("c"), lax.axis_index(GRID)
    inner = jnp.logical_and(slab > 0, slab < lax.axis_size(GRID) - 1)
    return (1 - core) * distance, core * distance, inner


def prepare_kernel(
    nb_in, ew_in, vw_in, area_in, latent_in, skip_in, state_in, earlier,
    near_out, edges_out, part_out, wm_out, state_out,
    nb, ew, vw, area, latent, skip, state, sems,
):
    pairs = (
        (nb_in, nb), (ew_in, ew), (vw_in, vw), (area_in, area),
        (latent_in, latent), (skip_in, skip), (state_in, state),
    )
    copies = [pltpu.make_async_copy(a, b, sems.at[i]) for i, (a, b) in enumerate(pairs)]
    rim = near_out.shape[0]
    near_rows = pl.ds(pl.multiple_of((1 - lax.axis_index("c")) * rim, rim), rim)
    copies.append(pltpu.make_async_copy(latent_in.at[near_rows], near_out, sems.at[len(pairs)]))
    for copy in copies:
        copy.start()
    for copy in copies[:4]:
        copy.wait()
    slots, points = nb.shape
    mesh_count = latent.shape[0]
    near_start, far_start, far_there = borrowed_rows(rim + mesh_count)
    weights = ew[...]
    weights = weights / jnp.sum(weights, axis=0, keepdims=True)
    rows = nb[...]
    both = jnp.concatenate(
        [rows.astype(F32), weights, jnp.zeros((8 - 2 * slots, points), F32)], axis=0
    )
    columns = jnp.transpose(both)
    ids = columns.astype(jnp.int32)

    def edges(start, count):
        lane = lax.broadcasted_iota(jnp.int32, (points, count), 1) + start
        total = jnp.zeros((points, count), F32)
        for k in range(slots):
            total = total + jnp.where(
                lane == ids[:, k : k + 1], columns[:, slots + k : slots + k + 1], 0.0
            )
        return total

    def parts(value):
        high = value.astype(BF16)
        return high, (value - high.astype(F32)).astype(BF16)

    near_high, near_low = parts(edges(near_start, rim))
    own_high, own_low = parts(edges(rim, mesh_count))
    far_high, far_low = parts(jnp.where(far_there, edges(far_start, rim), 0.0))
    for i, value in enumerate((near_high, near_low, far_high, far_low)):
        edges_out[:, i * rim : (i + 1) * rim] = value
    copies[4].wait()
    own = latent[...]
    mix = dot(
        jnp.concatenate([own_high, own_low], axis=1), jnp.concatenate([own, own], axis=0), ((1,), (0,))
    )
    copies[5].wait()
    part_out[...] = skip[...].astype(F32) + mix
    variables = vw.shape[1]
    diagonal = lax.broadcasted_iota(jnp.int32, (variables, variables), 0) == (
        lax.broadcasted_iota(jnp.int32, (variables, variables), 1)
    )
    vw_column = jnp.sum(jnp.where(diagonal, vw[...], 0.0), axis=1, keepdims=True)
    wm_out[...] = vw_column * area[...]
    copies[6].wait()
    state_out[...] = state[:, 0, :]
    copies[7].wait()


def forward_kernel(part, edges, near, far, gain, proj, state, f_out, sc_out, rs_out):
    close, distant = near[...], far[...]
    twice = jnp.concatenate([close, close, distant, distant], axis=0)
    mixed = part[...] + dot(edges[...], twice, ((1,), (0,)))
    centred = mixed - jnp.mean(mixed, axis=1, keepdims=True)
    rscale = lax.rsqrt(jnp.mean(centred * centred, axis=1, keepdims=True) + NORM_EPS)
    scaled = (centred * rscale * gain[...]).astype(BF16)
    sc_out[...] = scaled
    rs_out[...] = rscale
    f_out[...] = state[...] + dot(proj[...], scaled, ((1,), (1,)))


def loss_kernel(every, field, target, wm, proj, scaled, gain, fg_out, parts_out):
    members, variables, _ = every.shape
    eps_fair = (1.0 - FAIRNESS) / members
    coef_pair = (1.0 - eps_fair) / (members * (members - 1))
    smooth = SMOOTHING * SMOOTHING
    member = lax.axis_index(MEMBER)
    f = field[...]
    weight_map = wm[...]
    d = f - target[...]
    s = d * d + smooth
    r = lax.rsqrt(s)
    spread, slope = s * r, d * r
    pair_total = jnp.full_like(f, -SMOOTHING)
    pair_slope = jnp.zeros_like(f)
    for k in range(members):
        other = jnp.where(member == k, f, every[k])
        d = f - other
        s = d * d + smooth
        r = lax.rsqrt(s)
        pair_total = pair_total + s * r
        pair_slope = pair_slope + d * r
    terms = weight_map * (spread / members - 0.5 * coef_pair * pair_total)
    loss = jnp.sum(jnp.sum(terms, axis=0, keepdims=True), axis=1, keepdims=True)
    fore_grad = (weight_map * (slope / members - coef_pair * pair_slope)).astype(BF16)
    fg_out[...] = fore_grad
    wout = dot(fore_grad, scaled[...], ((1,), (0,)))
    product = jnp.sum(wout * proj[...].astype(F32), axis=0, keepdims=True) / gain[...]
    last = variables // CHUNK
    for i in range(last):
        parts_out[i] = wout[i * CHUNK : (i + 1) * CHUNK].astype(BF16)
    channels = wout.shape[1]
    high = loss.astype(BF16).astype(F32)
    rest = variables - last * CHUNK
    parts_out[last] = jnp.concatenate(
        [
            wout[last * CHUNK :],
            product,
            jnp.broadcast_to(high, (1, channels)),
            jnp.broadcast_to(loss - high, (1, channels)),
            jnp.zeros((CHUNK - rest - 3, channels), F32),
        ],
        axis=0,
    ).astype(BF16)
    for i in range(last + 1, parts_out.shape[0]):
        parts_out[i] = jnp.zeros((CHUNK, channels), BF16)


def back_kernel(earlier, nb, ew, fore_grad, proj, scaled, gain, rscale, own_out, near_out, far_out):
    channels = scaled.shape[1]
    rim = near_out.shape[0]
    mesh_count = own_out.shape[0]
    scaled_grad = dot(fore_grad[...], proj[...], ((0,), (0,)))
    values = scaled[...].astype(F32)
    norm_grad = scaled_grad * gain[...]
    first = jnp.sum(norm_grad, axis=1, keepdims=True) / channels
    second = jnp.sum(scaled_grad * values, axis=1, keepdims=True) / channels
    mixed_grad = rscale[...] * (norm_grad - first - values * (1.0 / gain[...]) * second)
    mixed_grad = mixed_grad.astype(BF16)
    weights = ew[...]
    weights = weights / jnp.sum(weights, axis=0, keepdims=True)
    rows = nb[...]
    near_start, far_start, far_there = borrowed_rows(rim + mesh_count)

    def back(start, count, there=None):
        row = lax.broadcasted_iota(jnp.int32, (count, nb.shape[1]), 0) + start
        edges = jnp.zeros(row.shape, F32)
        for k in range(nb.shape[0]):
            edges = edges + jnp.where(row == rows[k : k + 1], weights[k : k + 1], 0.0)
        if there is not None:
            edges = jnp.where(there, edges, 0.0)
        return dot(edges.astype(BF16), mixed_grad, ((1,), (0,)))

    far_out[...] = back(far_start, rim, far_there).astype(BF16)
    near_out[...] = back(near_start, rim).astype(BF16)
    own_out[...] = back(rim, mesh_count)


def finish_latent_kernel(own, near, far, out):
    rim = near.shape[0]
    a, b = near[...].astype(F32), far[...].astype(F32)
    second = lax.axis_index("c") == 1
    out[0, :rim] = (own[:rim] + jnp.where(second, a, b)).astype(BF16)
    out[0, rim:] = (own[rim:] + jnp.where(second, b, a)).astype(BF16)


def narrowed(total, variables):
    here = lax.axis_index(PLANE) == variables // CHUNK
    first = variables % CHUNK + 1
    loss = total[first : first + 1] + total[first + 1 : first + 2]
    high = loss.astype(BF16).astype(F32)
    row = lax.broadcasted_iota(jnp.int32, total.shape, 0)
    split = jnp.where(row == first, high, jnp.where(row == first + 1, loss - high, total))
    return jnp.where(here, split, total).astype(BF16)


def fold_kernel(parts, out):
    out[...] = jnp.sum(parts[...].astype(F32), axis=0)


def pair_kernel(variables, mine, met, out):
    total = narrowed(mine[...] + met[...], variables)
    for i in range(out.shape[0]):
        out[i] = total


def spread_kernel(variables, parts, earlier, out):
    total = narrowed(jnp.sum(parts[...].astype(F32), axis=0), variables)
    for i in range(out.shape[0]):
        out[i] = total


def finish_weights_kernel(count, parts, earlier, wout_out, gain_out, loss_out):
    variables = wout_out.shape[0]
    last = variables // CHUNK
    for i in range(last):
        wout_out[i * CHUNK : (i + 1) * CHUNK] = parts[i].astype(F32)
    chunk = parts[last].astype(F32)
    rest = variables - last * CHUNK
    wout_out[last * CHUNK :] = chunk[:rest]
    gain_out[...] = chunk[rest : rest + 1]
    loss = chunk[rest + 1 : rest + 2, :1] + chunk[rest + 2 : rest + 3, :1]
    loss_out[...] = loss * (1.0 / count)


def per_device(
    latent,
    grid_latent_skip,
    initial_member_state,
    target,
    neighbours,
    edge_weight,
    area_weight,
    variable_weight,
    output_projection,
    layer_norm_gain,
):
    latent, skip, state = latent[0], grid_latent_skip[0], initial_member_state[0]
    mesh_count, channels = latent.shape
    points = skip.shape[0]
    rim = mesh_count // 2
    extent = mesh_count + 2 * rim
    variables = output_projection.shape[0]
    members = lax.axis_size(MEMBER)
    slabs = lax.axis_size(GRID)
    plane = lax.axis_size(PLANE)
    gain = layer_norm_gain[None]
    swap = [(0, 1), (1, 0)]
    links = [((i + 1) % slabs, (i + 2) % slabs) for i in range(0, slabs, 2)]
    links = links + [(j, i) for i, j in links]

    (far_send,) = call(
        cut_kernel, [((rim, channels), BF16)], "h", [pltpu.SemaphoreType.DMA]
    )(latent)
    far = lax.ppermute(far_send, GRID, links)
    near_send, edges, part, weight_map, state = call(
        prepare_kernel,
        [
            ((rim, channels), BF16),
            ((points, 4 * rim), BF16),
            ((points, channels), F32),
            ((variables, points), F32),
            ((variables, points), F32),
        ],
        "hhhhhhha",
        [
            pltpu.VMEM(neighbours.shape, jnp.int32),
            pltpu.VMEM(edge_weight.shape, F32),
            pltpu.VMEM((1, variables), F32),
            pltpu.VMEM((1, points), F32),
            pltpu.VMEM((mesh_count, channels), BF16),
            pltpu.VMEM((points, channels), BF16),
            pltpu.VMEM((variables, 1, points), F32),
            pltpu.SemaphoreType.DMA((8,)),
        ],
        flops=6 * points * mesh_count * channels,
        moved=8_000_000,
    )(
        neighbours, edge_weight, variable_weight[None], area_weight[None], latent, skip,
        state.reshape(variables, 1, points), far_send,
    )
    near = lax.ppermute(near_send, "c", swap)
    field, scaled, rscale = call(
        forward_kernel,
        [
            ((variables, points), F32),
            ((points, channels), BF16),
            ((points, 1), F32),
        ],
        flops=2 * points * channels * (2 * rim + variables),
        moved=5_000_000,
    )(part, edges, near, far, gain, output_projection, state)
    sent = jnp.broadcast_to(field.astype(jnp.float16)[None], (members, variables, points))
    every = lax.all_to_all(sent, MEMBER, 0, 0, tiled=True).astype(F32)
    fore_grad, parts = call(
        loss_kernel,
        [((variables, points), BF16), ((plane, CHUNK, channels), BF16)],
        flops=4 * points * channels * variables,
        moved=4_000_000,
    )(every, field, target, weight_map, output_projection, scaled, gain)

    parts = lax.all_to_all(parts, PLANE, 0, 0, tiled=True)
    (mine,) = call(fold_kernel, [((CHUNK, channels), F32)])(parts)
    met = lax.ppermute(mine, "c", swap)
    depth = lax.axis_size("z")
    (parts,) = call(
        functools.partial(pair_kernel, variables), [((depth, CHUNK, channels), BF16)]
    )(mine, met)
    own, near_grad, far_grad = call(
        back_kernel,
        [((mesh_count, channels), F32), ((rim, channels), BF16), ((rim, channels), BF16)],
        flops=2 * points * channels * (extent + variables),
        moved=6_000_000,
        spaces="a",
    )(met, neighbours, edge_weight, fore_grad, output_projection, scaled, gain, rscale)
    far_grad = lax.ppermute(far_grad, GRID, links)
    near_grad = lax.ppermute(near_grad, "c", swap)
    (latent_grad,) = call(finish_latent_kernel, [((1, mesh_count, channels), BF16)])(
        own, near_grad, far_grad
    )
    parts = lax.all_to_all(parts, "z", 0, 0, tiled=True)
    (parts,) = call(
        functools.partial(spread_kernel, variables), [((plane, CHUNK, channels), BF16)], "va"
    )(parts, own)
    parts = lax.all_to_all(parts, PLANE, 0, 0, tiled=True)
    wout, gain_grad, crps = call(
        functools.partial(finish_weights_kernel, points * slabs * variables),
        [((variables, channels), F32), ((1, channels), F32), ((1, 1), F32)],
        "vh",
    )(parts, latent_grad)
    return (crps[0, 0], latent_grad, wout, gain_grad[0])


def solution(mesh):
    fine = Mesh(mesh.devices.reshape(2, 4, 2, 8, 2), ("xl", "y", "xh", "z", "c"))
    placed = (
        P(MEMBER, GRID, None),
        P(MEMBER, GRID, None),
        P(MEMBER, None, GRID),
        P(None, GRID),
        P(None, GRID),
        P(None, GRID),
        P(GRID),
        P(),
        P(),
        P(),
    )
    return jax.shard_map(
        per_device,
        mesh=fine,
        in_specs=placed,
        out_specs=(P(), P(MEMBER, GRID, None), P(), P()),
        check_vma=False,
    )
```

```python
import functools

import jax
import jax.numpy as jnp
from jax import lax
from jax.experimental import pallas as pl
from jax.experimental.pallas import tpu as pltpu
from jax.sharding import Mesh
from jax.sharding import PartitionSpec as P

SMOOTHING = 0.25
FAIRNESS = 0.95
NORM_EPS = 1e-05
MEMBER = ("xl", "y")
GRID = ("xh", "z", "c")
NEAR = ("xh", "c")
CHUNK = 16
BF16 = jnp.bfloat16
F32 = jnp.float32
VMEM_LIMIT = 24 * 1024 * 1024


def dot(a, b, dims):
    return lax.dot_general(a, b, (dims, ((), ())), preferred_element_type=F32)


def call(kernel, outs, spaces="", scratch=(), flops=0, moved=0):
    places = {"s": pltpu.SMEM, "h": pltpu.HBM, "a": pl.ANY, "v": pltpu.VMEM}

    def run(*operands):
        letters = spaces.ljust(len(operands), "v")
        operands = [
            pltpu.with_memory_space_constraint(x, pltpu.HBM) if c == "h" else x
            for x, c in zip(operands, letters)
        ]
        return pl.pallas_call(
            kernel,
            out_shape=[jax.ShapeDtypeStruct(s, d) for s, d in outs],
            in_specs=[pl.BlockSpec(memory_space=places[c]) for c in letters],
            out_specs=[pl.BlockSpec(memory_space=pltpu.VMEM) for _ in outs],
            scratch_shapes=list(scratch),
            compiler_params=pltpu.CompilerParams(vmem_limit_bytes=VMEM_LIMIT),
            cost_estimate=pl.CostEstimate(flops=flops, bytes_accessed=moved, transcendentals=0),
        )(*operands)

    return run


def cut_kernel(latent, out, sem):
    rim = out.shape[0]
    start = pl.multiple_of(lax.axis_index("c") * rim, rim)
    copy = pltpu.make_async_copy(latent.at[pl.ds(start, rim)], out, sem)
    copy.start()
    copy.wait()


def borrowed_rows(distance):
    core, slab = lax.axis_index("c"), lax.axis_index(GRID)
    inner = jnp.logical_and(slab > 0, slab < lax.axis_size(GRID) - 1)
    return (1 - core) * distance, core * distance, inner


def prepare_kernel(
    nb_in, ew_in, vw_in, area_in, latent_in, skip_in, state_in, earlier,
    near_out, edges_out, part_out, wm_out, state_out,
    nb, ew, vw, area, latent, skip, state, sems,
):
    pairs = (
        (nb_in, nb), (ew_in, ew), (vw_in, vw), (area_in, area),
        (latent_in, latent), (skip_in, skip), (state_in, state),
    )
    copies = [pltpu.make_async_copy(a, b, sems.at[i]) for i, (a, b) in enumerate(pairs)]
    rim = near_out.shape[0]
    near_rows = pl.ds(pl.multiple_of((1 - lax.axis_index("c")) * rim, rim), rim)
    copies.append(pltpu.make_async_copy(latent_in.at[near_rows], near_out, sems.at[len(pairs)]))
    for copy in copies:
        copy.start()
    for copy in copies[:4]:
        copy.wait()
    slots, points = nb.shape
    mesh_count = latent.shape[0]
    near_start, far_start, far_there = borrowed_rows(rim + mesh_count)
    weights = ew[...]
    weights = weights / jnp.sum(weights, axis=0, keepdims=True)
    rows = nb[...]
    both = jnp.concatenate(
        [rows.astype(F32), weights, jnp.zeros((8 - 2 * slots, points), F32)], axis=0
    )
    columns = jnp.transpose(both)
    ids = columns.astype(jnp.int32)

    def edges(start, count):
        lane = lax.broadcasted_iota(jnp.int32, (points, count), 1) + start
        total = jnp.zeros((points, count), F32)
        for k in range(slots):
            total = total + jnp.where(
                lane == ids[:, k : k + 1], columns[:, slots + k : slots + k + 1], 0.0
            )
        return total

    def parts(value):
        high = value.astype(BF16)
        return high, (value - high.astype(F32)).astype(BF16)

    near_high, near_low = parts(edges(near_start, rim))
    own_high, own_low = parts(edges(rim, mesh_count))
    far_high, far_low = parts(jnp.where(far_there, edges(far_start, rim), 0.0))
    for i, value in enumerate((near_high, near_low, far_high, far_low)):
        edges_out[:, i * rim : (i + 1) * rim] = value
    copies[4].wait()
    own = latent[...]
    mix = dot(
        jnp.concatenate([own_high, own_low], axis=1), jnp.concatenate([own, own], axis=0), ((1,), (0,))
    )
    copies[5].wait()
    part_out[...] = skip[...].astype(F32) + mix
    variables = vw.shape[1]
    diagonal = lax.broadcasted_iota(jnp.int32, (variables, variables), 0) == (
        lax.broadcasted_iota(jnp.int32, (variables, variables), 1)
    )
    vw_column = jnp.sum(jnp.where(diagonal, vw[...], 0.0), axis=1, keepdims=True)
    wm_out[...] = vw_column * area[...]
    copies[6].wait()
    state_out[...] = state[:, 0, :]
    copies[7].wait()


def forward_kernel(part, edges, near, far, gain, proj, state, f_out, sc_out, rs_out):
    close, distant = near[...], far[...]
    twice = jnp.concatenate([close, close, distant, distant], axis=0)
    mixed = part[...] + dot(edges[...], twice, ((1,), (0,)))
    centred = mixed - jnp.mean(mixed, axis=1, keepdims=True)
    rscale = lax.rsqrt(jnp.mean(centred * centred, axis=1, keepdims=True) + NORM_EPS)
    scaled = (centred * rscale * gain[...]).astype(BF16)
    sc_out[...] = scaled
    rs_out[...] = rscale
    f_out[...] = state[...] + dot(proj[...], scaled, ((1,), (1,)))


def loss_kernel(every, field, target, wm, proj, scaled, gain, fg_out, parts_out):
    members, variables, _ = every.shape
    eps_fair = (1.0 - FAIRNESS) / members
    coef_pair = (1.0 - eps_fair) / (members * (members - 1))
    smooth = SMOOTHING * SMOOTHING
    member = lax.axis_index(MEMBER)
    f = field[...]
    weight_map = wm[...]
    d = f - target[...]
    s = d * d + smooth
    r = lax.rsqrt(s)
    spread, slope = s * r, d * r
    pair_total = jnp.full_like(f, -SMOOTHING)
    pair_slope = jnp.zeros_like(f)
    for k in range(members):
        other = jnp.where(member == k, f, every[k])
        d = f - other
        s = d * d + smooth
        r = lax.rsqrt(s)
        pair_total = pair_total + s * r
        pair_slope = pair_slope + d * r
    terms = weight_map * (spread / members - 0.5 * coef_pair * pair_total)
    loss = jnp.sum(jnp.sum(terms, axis=0, keepdims=True), axis=1, keepdims=True)
    fore_grad = (weight_map * (slope / members - coef_pair * pair_slope)).astype(BF16)
    fg_out[...] = fore_grad
    wout = dot(fore_grad, scaled[...], ((1,), (0,)))
    product = jnp.sum(wout * proj[...].astype(F32), axis=0, keepdims=True) / gain[...]
    last = variables // CHUNK
    for i in range(last):
        parts_out[i] = wout[i * CHUNK : (i + 1) * CHUNK].astype(BF16)
    channels = wout.shape[1]
    high = loss.astype(BF16).astype(F32)
    rest = variables - last * CHUNK
    parts_out[last] = jnp.concatenate(
        [
            wout[last * CHUNK :],
            product,
            jnp.broadcast_to(high, (1, channels)),
            jnp.broadcast_to(loss - high, (1, channels)),
            jnp.zeros((CHUNK - rest - 3, channels), F32),
        ],
        axis=0,
    ).astype(BF16)
    for i in range(last + 1, parts_out.shape[0]):
        parts_out[i] = jnp.zeros((CHUNK, channels), BF16)


def back_kernel(earlier, nb, ew, fore_grad, proj, scaled, gain, rscale, own_out, near_out, far_out):
    channels = scaled.shape[1]
    rim = near_out.shape[0]
    mesh_count = own_out.shape[0]
    scaled_grad = dot(fore_grad[...], proj[...], ((0,), (0,)))
    values = scaled[...].astype(F32)
    norm_grad = scaled_grad * gain[...]
    first = jnp.sum(norm_grad, axis=1, keepdims=True) / channels
    second = jnp.sum(scaled_grad * values, axis=1, keepdims=True) / channels
    mixed_grad = rscale[...] * (norm_grad - first - values * (1.0 / gain[...]) * second)
    mixed_grad = mixed_grad.astype(BF16)
    weights = ew[...]
    weights = weights / jnp.sum(weights, axis=0, keepdims=True)
    rows = nb[...]
    near_start, far_start, far_there = borrowed_rows(rim + mesh_count)

    def back(start, count, there=None):
        row = lax.broadcasted_iota(jnp.int32, (count, nb.shape[1]), 0) + start
        edges = jnp.zeros(row.shape, F32)
        for k in range(nb.shape[0]):
            edges = edges + jnp.where(row == rows[k : k + 1], weights[k : k + 1], 0.0)
        if there is not None:
            edges = jnp.where(there, edges, 0.0)
        return dot(edges.astype(BF16), mixed_grad, ((1,), (0,)))

    far_out[...] = back(far_start, rim, far_there).astype(BF16)
    near_out[...] = back(near_start, rim).astype(BF16)
    own_out[...] = back(rim, mesh_count)


def finish_latent_kernel(own, near, far, out):
    rim = near.shape[0]
    a, b = near[...].astype(F32), far[...].astype(F32)
    second = lax.axis_index("c") == 1
    out[0, :rim] = (own[:rim] + jnp.where(second, a, b)).astype(BF16)
    out[0, rim:] = (own[rim:] + jnp.where(second, b, a)).astype(BF16)


def narrowed(total, variables):
    here = lax.axis_index(MEMBER) == variables // CHUNK
    first = variables % CHUNK + 1
    loss = total[first : first + 1] + total[first + 1 : first + 2]
    high = loss.astype(BF16).astype(F32)
    row = lax.broadcasted_iota(jnp.int32, total.shape, 0)
    split = jnp.where(row == first, high, jnp.where(row == first + 1, loss - high, total))
    return jnp.where(here, split, total).astype(BF16)


def fold_kernel(variables, parts, out):
    out[...] = narrowed(jnp.sum(parts[...].astype(F32), axis=0), variables)


def quad_kernel(variables, mine, a, b, c, out):
    pair = mine[...].astype(F32) + a[...].astype(F32)
    total = narrowed(pair + (b[...].astype(F32) + c[...].astype(F32)), variables)
    for i in range(out.shape[0]):
        out[i] = total


def spread_kernel(variables, parts, earlier, out):
    total = narrowed(jnp.sum(parts[...].astype(F32), axis=0), variables)
    for i in range(out.shape[0]):
        out[i] = total


def finish_weights_kernel(count, parts, earlier, wout_out, gain_out, loss_out):
    variables = wout_out.shape[0]
    last = variables // CHUNK
    for i in range(last):
        wout_out[i * CHUNK : (i + 1) * CHUNK] = parts[i].astype(F32)
    chunk = parts[last].astype(F32)
    rest = variables - last * CHUNK
    wout_out[last * CHUNK :] = chunk[:rest]
    gain_out[...] = chunk[rest : rest + 1]
    loss = chunk[rest + 1 : rest + 2, :1] + chunk[rest + 2 : rest + 3, :1]
    loss_out[...] = loss * (1.0 / count)


def per_device(
    latent,
    grid_latent_skip,
    initial_member_state,
    target,
    neighbours,
    edge_weight,
    area_weight,
    variable_weight,
    output_projection,
    layer_norm_gain,
):
    latent, skip, state = latent[0], grid_latent_skip[0], initial_member_state[0]
    mesh_count, channels = latent.shape
    points = skip.shape[0]
    rim = mesh_count // 2
    extent = mesh_count + 2 * rim
    variables = output_projection.shape[0]
    members = lax.axis_size(MEMBER)
    slabs = lax.axis_size(GRID)
    gain = layer_norm_gain[None]
    swap = [(0, 1), (1, 0)]
    links = [((i + 1) % slabs, (i + 2) % slabs) for i in range(0, slabs, 2)]
    links = links + [(j, i) for i, j in links]

    (far_send,) = call(
        cut_kernel, [((rim, channels), BF16)], "h", [pltpu.SemaphoreType.DMA]
    )(latent)
    far = lax.ppermute(far_send, GRID, links)
    near_send, edges, part, weight_map, state = call(
        prepare_kernel,
        [
            ((rim, channels), BF16),
            ((points, 4 * rim), BF16),
            ((points, channels), F32),
            ((variables, points), F32),
            ((variables, points), F32),
        ],
        "hhhhhhha",
        [
            pltpu.VMEM(neighbours.shape, jnp.int32),
            pltpu.VMEM(edge_weight.shape, F32),
            pltpu.VMEM((1, variables), F32),
            pltpu.VMEM((1, points), F32),
            pltpu.VMEM((mesh_count, channels), BF16),
            pltpu.VMEM((points, channels), BF16),
            pltpu.VMEM((variables, 1, points), F32),
            pltpu.SemaphoreType.DMA((8,)),
        ],
        flops=6 * points * mesh_count * channels,
        moved=8_000_000,
    )(
        neighbours, edge_weight, variable_weight[None], area_weight[None], latent, skip,
        state.reshape(variables, 1, points), far_send,
    )
    near = lax.ppermute(near_send, "c", swap)
    field, scaled, rscale = call(
        forward_kernel,
        [
            ((variables, points), F32),
            ((points, channels), BF16),
            ((points, 1), F32),
        ],
        flops=2 * points * channels * (2 * rim + variables),
        moved=5_000_000,
    )(part, edges, near, far, gain, output_projection, state)
    sent = jnp.broadcast_to(field.astype(jnp.float16)[None], (members, variables, points))
    every = lax.all_to_all(sent, MEMBER, 0, 0, tiled=True).astype(F32)
    fore_grad, parts = call(
        loss_kernel,
        [((variables, points), BF16), ((members, CHUNK, channels), BF16)],
        flops=4 * points * channels * variables,
        moved=4_000_000,
    )(every, field, target, weight_map, output_projection, scaled, gain)

    parts = lax.all_to_all(parts, MEMBER, 0, 0, tiled=True)
    (mine,) = call(functools.partial(fold_kernel, variables), [((CHUNK, channels), BF16)])(parts)
    met = lax.ppermute(mine, "c", swap)
    across = lax.ppermute(mine, "xh", swap)
    oblique = lax.ppermute(mine, NEAR, [(i, 3 - i) for i in range(4)])
    depth = lax.axis_size("z")
    (parts,) = call(
        functools.partial(quad_kernel, variables), [((depth, CHUNK, channels), BF16)]
    )(mine, met, across, oblique)
    own, near_grad, far_grad = call(
        back_kernel,
        [((mesh_count, channels), F32), ((rim, channels), BF16), ((rim, channels), BF16)],
        flops=2 * points * channels * (extent + variables),
        moved=6_000_000,
        spaces="a",
    )(oblique, neighbours, edge_weight, fore_grad, output_projection, scaled, gain, rscale)
    far_grad = lax.ppermute(far_grad, GRID, links)
    near_grad = lax.ppermute(near_grad, "c", swap)
    (latent_grad,) = call(finish_latent_kernel, [((1, mesh_count, channels), BF16)])(
        own, near_grad, far_grad
    )
    parts = lax.all_to_all(parts, "z", 0, 0, tiled=True)
    (parts,) = call(
        functools.partial(spread_kernel, variables), [((members, CHUNK, channels), BF16)], "va"
    )(parts, own)
    parts = lax.all_to_all(parts, MEMBER, 0, 0, tiled=True)
    wout, gain_grad, crps = call(
        functools.partial(finish_weights_kernel, points * slabs * variables),
        [((variables, channels), F32), ((1, channels), F32), ((1, 1), F32)],
        "vh",
    )(parts, latent_grad)
    return (crps[0, 0], latent_grad, wout, gain_grad[0])


def solution(mesh):
    fine = Mesh(mesh.devices.reshape(2, 4, 2, 8, 2), ("xl", "y", "xh", "z", "c"))
    placed = (
        P(MEMBER, GRID, None),
        P(MEMBER, GRID, None),
        P(MEMBER, None, GRID),
        P(None, GRID),
        P(None, GRID),
        P(None, GRID),
        P(GRID),
        P(),
        P(),
        P(),
    )
    return jax.shard_map(
        per_device,
        mesh=fine,
        in_specs=placed,
        out_specs=(P(), P(MEMBER, GRID, None), P(), P()),
        check_vma=False,
    )
```

```python
import functools

import jax
import jax.numpy as jnp
from jax import lax
from jax.experimental import pallas as pl
from jax.experimental.pallas import tpu as pltpu
from jax.sharding import Mesh
from jax.sharding import PartitionSpec as P

SMOOTHING = 0.25
FAIRNESS = 0.95
NORM_EPS = 1e-05
MEMBER = ("xl", "y")
GRID = ("xh", "z", "c")
PLANE = ("xl", "y", "xh")
CHUNK = 8
BLOCK = 128
BF16 = jnp.bfloat16
F32 = jnp.float32
VMEM_LIMIT = 24 * 1024 * 1024


def dot(a, b, dims):
    return lax.dot_general(a, b, (dims, ((), ())), preferred_element_type=F32)


def call(kernel, outs, spaces="", scratch=(), flops=0, moved=0):
    places = {"s": pltpu.SMEM, "h": pltpu.HBM, "a": pl.ANY, "v": pltpu.VMEM}

    def run(*operands):
        letters = spaces.ljust(len(operands), "v")
        operands = [
            pltpu.with_memory_space_constraint(x, pltpu.HBM) if c == "h" else x
            for x, c in zip(operands, letters)
        ]
        return pl.pallas_call(
            kernel,
            out_shape=[jax.ShapeDtypeStruct(s, d) for s, d in outs],
            in_specs=[pl.BlockSpec(memory_space=places[c]) for c in letters],
            out_specs=[pl.BlockSpec(memory_space=pltpu.VMEM) for _ in outs],
            scratch_shapes=list(scratch),
            compiler_params=pltpu.CompilerParams(vmem_limit_bytes=VMEM_LIMIT),
            cost_estimate=pl.CostEstimate(flops=flops, bytes_accessed=moved, transcendentals=0),
        )(*operands)

    return run


def cut_kernel(latent, out, sem):
    rim = out.shape[0]
    start = pl.multiple_of(lax.axis_index("c") * rim, rim)
    copy = pltpu.make_async_copy(latent.at[pl.ds(start, rim)], out, sem)
    copy.start()
    copy.wait()


def borrowed_rows(distance):
    core, slab = lax.axis_index("c"), lax.axis_index(GRID)
    inner = jnp.logical_and(slab > 0, slab < lax.axis_size(GRID) - 1)
    return (1 - core) * distance, core * distance, inner


def prepare_kernel(
    nb_in, ew_in, vw_in, area_in, latent_in, skip_in, state_in, earlier,
    near_out, edges_out, part_out, wm_out, state_out,
    nb, ew, vw, area, latent, skip, state, sems,
):
    pairs = (
        (nb_in, nb), (ew_in, ew), (vw_in, vw), (area_in, area),
        (latent_in, latent), (skip_in, skip), (state_in, state),
    )
    copies = [pltpu.make_async_copy(a, b, sems.at[i]) for i, (a, b) in enumerate(pairs)]
    rim = near_out.shape[0]
    near_rows = pl.ds(pl.multiple_of((1 - lax.axis_index("c")) * rim, rim), rim)
    copies.append(pltpu.make_async_copy(latent_in.at[near_rows], near_out, sems.at[len(pairs)]))
    for copy in copies:
        copy.start()
    for copy in copies[:4]:
        copy.wait()
    slots, points = nb.shape
    mesh_count = latent.shape[0]
    near_start, far_start, far_there = borrowed_rows(rim + mesh_count)
    weights = ew[...]
    weights = weights / jnp.sum(weights, axis=0, keepdims=True)
    rows = nb[...]
    both = jnp.concatenate(
        [rows.astype(F32), weights, jnp.zeros((8 - 2 * slots, points), F32)], axis=0
    )
    columns = jnp.transpose(both)
    ids = columns.astype(jnp.int32)

    def edges(start, count):
        lane = lax.broadcasted_iota(jnp.int32, (points, count), 1) + start
        total = jnp.zeros((points, count), F32)
        for k in range(slots):
            total = total + jnp.where(
                lane == ids[:, k : k + 1], columns[:, slots + k : slots + k + 1], 0.0
            )
        return total

    def parts(value):
        high = value.astype(BF16)
        return high, (value - high.astype(F32)).astype(BF16)

    near_high, near_low = parts(edges(near_start, rim))
    own_high, own_low = parts(edges(rim, mesh_count))
    far_high, far_low = parts(jnp.where(far_there, edges(far_start, rim), 0.0))
    for i, value in enumerate((near_high, near_low, far_high, far_low)):
        edges_out[:, i * rim : (i + 1) * rim] = value
    copies[4].wait()
    own = latent[...]
    mix = dot(
        jnp.concatenate([own_high, own_low], axis=1), jnp.concatenate([own, own], axis=0), ((1,), (0,))
    )
    copies[5].wait()
    part_out[...] = skip[...].astype(F32) + mix
    variables = vw.shape[1]
    diagonal = lax.broadcasted_iota(jnp.int32, (variables, variables), 0) == (
        lax.broadcasted_iota(jnp.int32, (variables, variables), 1)
    )
    vw_column = jnp.sum(jnp.where(diagonal, vw[...], 0.0), axis=1, keepdims=True)
    wm_out[...] = vw_column * area[...]
    copies[6].wait()
    state_out[...] = state[:, 0, :]
    copies[7].wait()


def near_kernel(part, edges, near, out):
    close = near[...]
    twice = jnp.concatenate([close, close], axis=0)
    out[...] = part[...] + dot(edges[:, : twice.shape[0]], twice, ((1,), (0,)))


def forward_kernel(part, edges, far, gain, proj, state, f_out, sc_out, rs_out):
    distant = far[...]
    twice = jnp.concatenate([distant, distant], axis=0)
    for r in range(0, part.shape[0], BLOCK):
        at = slice(r, r + BLOCK)
        mixed = part[at] + dot(edges[at, twice.shape[0] :], twice, ((1,), (0,)))
        centred = mixed - jnp.mean(mixed, axis=1, keepdims=True)
        rscale = lax.rsqrt(jnp.mean(centred * centred, axis=1, keepdims=True) + NORM_EPS)
        sc_out[at] = (centred * rscale * gain[...]).astype(BF16)
        rs_out[at] = rscale
    f_out[...] = state[...] + dot(proj[...], sc_out[...], ((1,), (1,)))


def loss_kernel(every, field, target, wm, proj, scaled, gain, fg_out, parts_out):
    members, variables, _ = every.shape
    eps_fair = (1.0 - FAIRNESS) / members
    coef_pair = (1.0 - eps_fair) / (members * (members - 1))
    smooth = SMOOTHING * SMOOTHING
    member = lax.axis_index(MEMBER)
    f = field[...]
    weight_map = wm[...]
    d = f - target[...]
    s = d * d + smooth
    r = lax.rsqrt(s)
    spread, slope = s * r, d * r
    pair_total = jnp.full_like(f, -SMOOTHING)
    pair_slope = jnp.zeros_like(f)
    for k in range(members):
        other = jnp.where(member == k, f, every[k])
        d = f - other
        s = d * d + smooth
        r = lax.rsqrt(s)
        pair_total = pair_total + s * r
        pair_slope = pair_slope + d * r
    terms = weight_map * (spread / members - 0.5 * coef_pair * pair_total)
    loss = jnp.sum(jnp.sum(terms, axis=0, keepdims=True), axis=1, keepdims=True)
    fore_grad = (weight_map * (slope / members - coef_pair * pair_slope)).astype(BF16)
    fg_out[...] = fore_grad
    wout = dot(fore_grad, scaled[...], ((1,), (0,)))
    product = jnp.sum(wout * proj[...].astype(F32), axis=0, keepdims=True) / gain[...]
    last = variables // CHUNK
    for i in range(last):
        parts_out[i] = wout[i * CHUNK : (i + 1) * CHUNK].astype(BF16)
    channels = wout.shape[1]
    high = loss.astype(BF16).astype(F32)
    rest = variables - last * CHUNK
    parts_out[last] = jnp.concatenate(
        [
            wout[last * CHUNK :],
            product,
            jnp.broadcast_to(high, (1, channels)),
            jnp.broadcast_to(loss - high, (1, channels)),
            jnp.zeros((CHUNK - rest - 3, channels), F32),
        ],
        axis=0,
    ).astype(BF16)
    for i in range(last + 1, parts_out.shape[0]):
        parts_out[i] = jnp.zeros((CHUNK, channels), BF16)


def back_kernel(earlier, nb, ew, fore_grad, proj, scaled, gain, rscale, own_out, near_out, far_out):
    channels = scaled.shape[1]
    rim = near_out.shape[0]
    mesh_count = own_out.shape[0]
    scaled_grad = dot(fore_grad[...], proj[...], ((0,), (0,)))
    values = scaled[...].astype(F32)
    norm_grad = scaled_grad * gain[...]
    first = jnp.sum(norm_grad, axis=1, keepdims=True) / channels
    second = jnp.sum(scaled_grad * values, axis=1, keepdims=True) / channels
    mixed_grad = rscale[...] * (norm_grad - first - values * (1.0 / gain[...]) * second)
    mixed_grad = mixed_grad.astype(BF16)
    weights = ew[...]
    weights = weights / jnp.sum(weights, axis=0, keepdims=True)
    rows = nb[...]
    near_start, far_start, far_there = borrowed_rows(rim + mesh_count)

    def back(start, count, there=None):
        row = lax.broadcasted_iota(jnp.int32, (count, nb.shape[1]), 0) + start
        edges = jnp.zeros(row.shape, F32)
        for k in range(nb.shape[0]):
            edges = edges + jnp.where(row == rows[k : k + 1], weights[k : k + 1], 0.0)
        if there is not None:
            edges = jnp.where(there, edges, 0.0)
        return dot(edges.astype(BF16), mixed_grad, ((1,), (0,)))

    far_out[...] = back(far_start, rim, far_there).astype(BF16)
    near_out[...] = back(near_start, rim).astype(BF16)
    own_out[...] = back(rim, mesh_count)


def finish_latent_kernel(own, near, far, out):
    rim = near.shape[0]
    a, b = near[...].astype(F32), far[...].astype(F32)
    second = lax.axis_index("c") == 1
    out[0, :rim] = (own[:rim] + jnp.where(second, a, b)).astype(BF16)
    out[0, rim:] = (own[rim:] + jnp.where(second, b, a)).astype(BF16)


def narrowed(total, variables):
    here = lax.axis_index(PLANE) == variables // CHUNK
    first = variables % CHUNK + 1
    loss = total[first : first + 1] + total[first + 1 : first + 2]
    high = loss.astype(BF16).astype(F32)
    row = lax.broadcasted_iota(jnp.int32, total.shape, 0)
    split = jnp.where(row == first, high, jnp.where(row == first + 1, loss - high, total))
    return jnp.where(here, split, total).astype(BF16)


def fold_kernel(parts, out):
    out[...] = jnp.sum(parts[...].astype(F32), axis=0)


def pair_kernel(variables, mine, met, out):
    total = narrowed(mine[...] + met[...], variables)
    for i in range(out.shape[0]):
        out[i] = total


def spread_kernel(variables, parts, earlier, out):
    total = narrowed(jnp.sum(parts[...].astype(F32), axis=0), variables)
    for i in range(out.shape[0]):
        out[i] = total


def finish_weights_kernel(count, parts, earlier, wout_out, gain_out, loss_out):
    variables = wout_out.shape[0]
    last = variables // CHUNK
    for i in range(last):
        wout_out[i * CHUNK : (i + 1) * CHUNK] = parts[i].astype(F32)
    chunk = parts[last].astype(F32)
    rest = variables - last * CHUNK
    wout_out[last * CHUNK :] = chunk[:rest]
    gain_out[...] = chunk[rest : rest + 1]
    loss = chunk[rest + 1 : rest + 2, :1] + chunk[rest + 2 : rest + 3, :1]
    loss_out[...] = loss * (1.0 / count)


def per_device(
    latent,
    grid_latent_skip,
    initial_member_state,
    target,
    neighbours,
    edge_weight,
    area_weight,
    variable_weight,
    output_projection,
    layer_norm_gain,
):
    latent, skip, state = latent[0], grid_latent_skip[0], initial_member_state[0]
    mesh_count, channels = latent.shape
    points = skip.shape[0]
    rim = mesh_count // 2
    extent = mesh_count + 2 * rim
    variables = output_projection.shape[0]
    members = lax.axis_size(MEMBER)
    slabs = lax.axis_size(GRID)
    plane = lax.axis_size(PLANE)
    gain = layer_norm_gain[None]
    swap = [(0, 1), (1, 0)]
    links = [((i + 1) % slabs, (i + 2) % slabs) for i in range(0, slabs, 2)]
    links = links + [(j, i) for i, j in links]

    (far_send,) = call(
        cut_kernel, [((rim, channels), BF16)], "h", [pltpu.SemaphoreType.DMA]
    )(latent)
    far = lax.ppermute(far_send, GRID, links)
    near_send, edges, part, weight_map, state = call(
        prepare_kernel,
        [
            ((rim, channels), BF16),
            ((points, 4 * rim), BF16),
            ((points, channels), F32),
            ((variables, points), F32),
            ((variables, points), F32),
        ],
        "hhhhhhha",
        [
            pltpu.VMEM(neighbours.shape, jnp.int32),
            pltpu.VMEM(edge_weight.shape, F32),
            pltpu.VMEM((1, variables), F32),
            pltpu.VMEM((1, points), F32),
            pltpu.VMEM((mesh_count, channels), BF16),
            pltpu.VMEM((points, channels), BF16),
            pltpu.VMEM((variables, 1, points), F32),
            pltpu.SemaphoreType.DMA((8,)),
        ],
        flops=6 * points * mesh_count * channels,
        moved=8_000_000,
    )(
        neighbours, edge_weight, variable_weight[None], area_weight[None], latent, skip,
        state.reshape(variables, 1, points), far_send,
    )
    near = lax.ppermute(near_send, "c", swap)
    (part,) = call(
        near_kernel,
        [((points, channels), F32)],
        flops=4 * points * channels * rim,
        moved=5_000_000,
    )(part, edges, near)
    field, scaled, rscale = call(
        forward_kernel,
        [
            ((variables, points), F32),
            ((points, channels), BF16),
            ((points, 1), F32),
        ],
        flops=2 * points * channels * (2 * rim + variables),
        moved=5_000_000,
    )(part, edges, far, gain, output_projection, state)
    sent = jnp.broadcast_to(field.astype(jnp.float16)[None], (members, variables, points))
    every = lax.all_to_all(sent, MEMBER, 0, 0, tiled=True).astype(F32)
    fore_grad, parts = call(
        loss_kernel,
        [((variables, points), BF16), ((plane, CHUNK, channels), BF16)],
        flops=4 * points * channels * variables,
        moved=4_000_000,
    )(every, field, target, weight_map, output_projection, scaled, gain)

    parts = lax.all_to_all(parts, PLANE, 0, 0, tiled=True)
    (mine,) = call(fold_kernel, [((CHUNK, channels), F32)])(parts)
    met = lax.ppermute(mine, "c", swap)
    depth = lax.axis_size("z")
    (parts,) = call(
        functools.partial(pair_kernel, variables), [((depth, CHUNK, channels), BF16)]
    )(mine, met)
    own, near_grad, far_grad = call(
        back_kernel,
        [((mesh_count, channels), F32), ((rim, channels), BF16), ((rim, channels), BF16)],
        flops=2 * points * channels * (extent + variables),
        moved=6_000_000,
        spaces="a",
    )(met, neighbours, edge_weight, fore_grad, output_projection, scaled, gain, rscale)
    far_grad = lax.ppermute(far_grad, GRID, links)
    near_grad = lax.ppermute(near_grad, "c", swap)
    (latent_grad,) = call(finish_latent_kernel, [((1, mesh_count, channels), BF16)])(
        own, near_grad, far_grad
    )
    parts = lax.all_to_all(parts, "z", 0, 0, tiled=True)
    (parts,) = call(
        functools.partial(spread_kernel, variables), [((plane, CHUNK, channels), BF16)], "va"
    )(parts, own)
    parts = lax.all_to_all(parts, PLANE, 0, 0, tiled=True)
    wout, gain_grad, crps = call(
        functools.partial(finish_weights_kernel, points * slabs * variables),
        [((variables, channels), F32), ((1, channels), F32), ((1, 1), F32)],
        "vh",
    )(parts, latent_grad)
    return (crps[0, 0], latent_grad, wout, gain_grad[0])


def solution(mesh):
    fine = Mesh(mesh.devices.reshape(2, 4, 2, 8, 2), ("xl", "y", "xh", "z", "c"))
    placed = (
        P(MEMBER, GRID, None),
        P(MEMBER, GRID, None),
        P(MEMBER, None, GRID),
        P(None, GRID),
        P(None, GRID),
        P(None, GRID),
        P(GRID),
        P(),
        P(),
        P(),
    )
    return jax.shard_map(
        per_device,
        mesh=fine,
        in_specs=placed,
        out_specs=(P(), P(MEMBER, GRID, None), P(), P()),
        check_vma=False,
    )
```

```python
import functools

import jax
import jax.numpy as jnp
from jax import lax
from jax.experimental import pallas as pl
from jax.experimental.pallas import tpu as pltpu
from jax.sharding import Mesh
from jax.sharding import PartitionSpec as P

SMOOTHING = 0.25
FAIRNESS = 0.95
NORM_EPS = 1e-05
MEMBER = ("xl", "y")
GRID = ("xh", "z", "c")
PLANE = ("xl", "y", "xh")
CHUNK = 8
BLOCK = 128
BF16 = jnp.bfloat16
F32 = jnp.float32
VMEM_LIMIT = 24 * 1024 * 1024


def dot(a, b, dims):
    return lax.dot_general(a, b, (dims, ((), ())), preferred_element_type=F32)


def call(kernel, outs, spaces="", scratch=(), flops=0, moved=0):
    places = {"s": pltpu.SMEM, "h": pltpu.HBM, "a": pl.ANY, "v": pltpu.VMEM}

    def run(*operands):
        letters = spaces.ljust(len(operands), "v")
        operands = [
            pltpu.with_memory_space_constraint(x, pltpu.HBM) if c == "h" else x
            for x, c in zip(operands, letters)
        ]
        return pl.pallas_call(
            kernel,
            out_shape=[jax.ShapeDtypeStruct(s, d) for s, d in outs],
            in_specs=[pl.BlockSpec(memory_space=places[c]) for c in letters],
            out_specs=[pl.BlockSpec(memory_space=pltpu.VMEM) for _ in outs],
            scratch_shapes=list(scratch),
            compiler_params=pltpu.CompilerParams(vmem_limit_bytes=VMEM_LIMIT),
            cost_estimate=pl.CostEstimate(flops=flops, bytes_accessed=moved, transcendentals=0),
        )(*operands)

    return run


def cut_kernel(latent, first_out, second_out, sems):
    rim = first_out.shape[0]
    core = lax.axis_index("c")
    start = pl.multiple_of((1 - core) * rim, rim)
    other = pl.multiple_of(core * rim, rim)
    one = pltpu.make_async_copy(latent.at[pl.ds(start, rim)], first_out, sems.at[0])
    two = pltpu.make_async_copy(latent.at[pl.ds(other, rim)], second_out, sems.at[1])
    one.start()
    two.start()
    one.wait()
    two.wait()


def borrowed_rows(distance):
    core, slab = lax.axis_index("c"), lax.axis_index(GRID)
    inner = jnp.logical_and(slab > 0, slab < lax.axis_size(GRID) - 1)
    return (1 - core) * distance, core * distance, inner


def prepare_kernel(
    nb_in, ew_in, vw_in, area_in, latent_in, skip_in, state_in, near,
    far_out, part_out, wm_out, state_out,
    nb, ew, vw, area, latent, skip, state, sems,
):
    pairs = (
        (nb_in, nb), (ew_in, ew), (vw_in, vw), (area_in, area),
        (latent_in, latent), (skip_in, skip), (state_in, state),
    )
    copies = [pltpu.make_async_copy(a, b, sems.at[i]) for i, (a, b) in enumerate(pairs)]
    for copy in copies:
        copy.start()
    for copy in copies[:4]:
        copy.wait()
    slots, points = nb.shape
    mesh_count = latent.shape[0]
    rim = mesh_count // 2
    near_start, far_start, far_there = borrowed_rows(rim + mesh_count)
    weights = ew[...]
    weights = weights / jnp.sum(weights, axis=0, keepdims=True)
    rows = nb[...]
    both = jnp.concatenate(
        [rows.astype(F32), weights, jnp.zeros((8 - 2 * slots, points), F32)], axis=0
    )
    columns = jnp.transpose(both)
    ids = columns.astype(jnp.int32)

    def edges(start, count):
        lane = lax.broadcasted_iota(jnp.int32, (points, count), 1) + start
        total = jnp.zeros((points, count), F32)
        for k in range(slots):
            total = total + jnp.where(
                lane == ids[:, k : k + 1], columns[:, slots + k : slots + k + 1], 0.0
            )
        return total

    def parts(value):
        high = value.astype(BF16)
        return high, (value - high.astype(F32)).astype(BF16)

    near_high, near_low = parts(edges(near_start, rim))
    own_high, own_low = parts(edges(rim, mesh_count))
    far_high, far_low = parts(jnp.where(far_there, edges(far_start, rim), 0.0))
    far_out[:, :rim] = far_high
    far_out[:, rim:] = far_low
    copies[4].wait()
    borrowed, own = near[...], latent[...]
    mix = dot(
        jnp.concatenate([near_high, near_low, own_high, own_low], axis=1),
        jnp.concatenate([borrowed, borrowed, own, own], axis=0),
        ((1,), (0,)),
    )
    copies[5].wait()
    part_out[...] = skip[...].astype(F32) + mix
    variables = vw.shape[1]
    diagonal = lax.broadcasted_iota(jnp.int32, (variables, variables), 0) == (
        lax.broadcasted_iota(jnp.int32, (variables, variables), 1)
    )
    vw_column = jnp.sum(jnp.where(diagonal, vw[...], 0.0), axis=1, keepdims=True)
    wm_out[...] = vw_column * area[...]
    copies[6].wait()
    state_out[...] = state[:, 0, :]


def forward_kernel(part, edges, far, gain, proj, state, f_out, sc_out, rs_out):
    distant = far[...]
    twice = jnp.concatenate([distant, distant], axis=0)
    for r in range(0, part.shape[0], BLOCK):
        at = slice(r, r + BLOCK)
        mixed = part[at] + dot(edges[at], twice, ((1,), (0,)))
        centred = mixed - jnp.mean(mixed, axis=1, keepdims=True)
        rscale = lax.rsqrt(jnp.mean(centred * centred, axis=1, keepdims=True) + NORM_EPS)
        sc_out[at] = (centred * rscale * gain[...]).astype(BF16)
        rs_out[at] = rscale
    f_out[...] = state[...] + dot(proj[...], sc_out[...], ((1,), (1,)))


def loss_kernel(every, field, target, wm, proj, scaled, gain, fg_out, parts_out):
    members, variables, _ = every.shape
    eps_fair = (1.0 - FAIRNESS) / members
    coef_pair = (1.0 - eps_fair) / (members * (members - 1))
    smooth = SMOOTHING * SMOOTHING
    member = lax.axis_index(MEMBER)
    f = field[...]
    weight_map = wm[...]
    d = f - target[...]
    s = d * d + smooth
    r = lax.rsqrt(s)
    spread, slope = s * r, d * r
    pair_total = jnp.full_like(f, -SMOOTHING)
    pair_slope = jnp.zeros_like(f)
    for k in range(members):
        other = jnp.where(member == k, f, every[k])
        d = f - other
        s = d * d + smooth
        r = lax.rsqrt(s)
        pair_total = pair_total + s * r
        pair_slope = pair_slope + d * r
    terms = weight_map * (spread / members - 0.5 * coef_pair * pair_total)
    loss = jnp.sum(jnp.sum(terms, axis=0, keepdims=True), axis=1, keepdims=True)
    fore_grad = (weight_map * (slope / members - coef_pair * pair_slope)).astype(BF16)
    fg_out[...] = fore_grad
    wout = dot(fore_grad, scaled[...], ((1,), (0,)))
    product = jnp.sum(wout * proj[...].astype(F32), axis=0, keepdims=True) / gain[...]
    last = variables // CHUNK
    for i in range(last):
        parts_out[i] = wout[i * CHUNK : (i + 1) * CHUNK].astype(BF16)
    channels = wout.shape[1]
    high = loss.astype(BF16).astype(F32)
    rest = variables - last * CHUNK
    parts_out[last] = jnp.concatenate(
        [
            wout[last * CHUNK :],
            product,
            jnp.broadcast_to(high, (1, channels)),
            jnp.broadcast_to(loss - high, (1, channels)),
            jnp.zeros((CHUNK - rest - 3, channels), F32),
        ],
        axis=0,
    ).astype(BF16)
    for i in range(last + 1, parts_out.shape[0]):
        parts_out[i] = jnp.zeros((CHUNK, channels), BF16)


def back_kernel(earlier, nb, ew, fore_grad, proj, scaled, gain, rscale, own_out, near_out, far_out):
    channels = scaled.shape[1]
    rim = near_out.shape[0]
    mesh_count = own_out.shape[0]
    scaled_grad = dot(fore_grad[...], proj[...], ((0,), (0,)))
    values = scaled[...].astype(F32)
    norm_grad = scaled_grad * gain[...]
    first = jnp.sum(norm_grad, axis=1, keepdims=True) / channels
    second = jnp.sum(scaled_grad * values, axis=1, keepdims=True) / channels
    mixed_grad = rscale[...] * (norm_grad - first - values * (1.0 / gain[...]) * second)
    mixed_grad = mixed_grad.astype(BF16)
    weights = ew[...]
    weights = weights / jnp.sum(weights, axis=0, keepdims=True)
    rows = nb[...]
    near_start, far_start, far_there = borrowed_rows(rim + mesh_count)

    def back(start, count, there=None):
        row = lax.broadcasted_iota(jnp.int32, (count, nb.shape[1]), 0) + start
        edges = jnp.zeros(row.shape, F32)
        for k in range(nb.shape[0]):
            edges = edges + jnp.where(row == rows[k : k + 1], weights[k : k + 1], 0.0)
        if there is not None:
            edges = jnp.where(there, edges, 0.0)
        return dot(edges.astype(BF16), mixed_grad, ((1,), (0,)))

    far_out[...] = back(far_start, rim, far_there).astype(BF16)
    near_out[...] = back(near_start, rim).astype(BF16)
    own_out[...] = back(rim, mesh_count)


def finish_latent_kernel(own, near, far, out):
    rim = near.shape[0]
    a, b = near[...].astype(F32), far[...].astype(F32)
    second = lax.axis_index("c") == 1
    out[0, :rim] = (own[:rim] + jnp.where(second, a, b)).astype(BF16)
    out[0, rim:] = (own[rim:] + jnp.where(second, b, a)).astype(BF16)


def narrowed(total, variables):
    here = lax.axis_index(PLANE) == variables // CHUNK
    first = variables % CHUNK + 1
    loss = total[first : first + 1] + total[first + 1 : first + 2]
    high = loss.astype(BF16).astype(F32)
    row = lax.broadcasted_iota(jnp.int32, total.shape, 0)
    split = jnp.where(row == first, high, jnp.where(row == first + 1, loss - high, total))
    return jnp.where(here, split, total).astype(BF16)


def fold_kernel(parts, out):
    out[...] = jnp.sum(parts[...].astype(F32), axis=0)


def pair_kernel(variables, mine, met, out):
    total = narrowed(mine[...] + met[...], variables)
    for i in range(out.shape[0]):
        out[i] = total


def spread_kernel(variables, parts, earlier, out):
    total = narrowed(jnp.sum(parts[...].astype(F32), axis=0), variables)
    for i in range(out.shape[0]):
        out[i] = total


def finish_weights_kernel(count, parts, earlier, wout_out, gain_out, loss_out):
    variables = wout_out.shape[0]
    last = variables // CHUNK
    for i in range(last):
        wout_out[i * CHUNK : (i + 1) * CHUNK] = parts[i].astype(F32)
    chunk = parts[last].astype(F32)
    rest = variables - last * CHUNK
    wout_out[last * CHUNK :] = chunk[:rest]
    gain_out[...] = chunk[rest : rest + 1]
    loss = chunk[rest + 1 : rest + 2, :1] + chunk[rest + 2 : rest + 3, :1]
    loss_out[...] = loss * (1.0 / count)


def per_device(
    latent,
    grid_latent_skip,
    initial_member_state,
    target,
    neighbours,
    edge_weight,
    area_weight,
    variable_weight,
    output_projection,
    layer_norm_gain,
):
    latent, skip, state = latent[0], grid_latent_skip[0], initial_member_state[0]
    mesh_count, channels = latent.shape
    points = skip.shape[0]
    rim = mesh_count // 2
    extent = mesh_count + 2 * rim
    variables = output_projection.shape[0]
    members = lax.axis_size(MEMBER)
    slabs = lax.axis_size(GRID)
    plane = lax.axis_size(PLANE)
    gain = layer_norm_gain[None]
    swap = [(0, 1), (1, 0)]
    links = [((i + 1) % slabs, (i + 2) % slabs) for i in range(0, slabs, 2)]
    links = links + [(j, i) for i, j in links]

    near_send, far_send = call(
        cut_kernel,
        [((rim, channels), BF16), ((rim, channels), BF16)],
        "h",
        [pltpu.SemaphoreType.DMA((2,))],
    )(latent)
    far = lax.ppermute(far_send, GRID, links)
    near = lax.ppermute(near_send, "c", swap)
    edges, part, weight_map, state = call(
        prepare_kernel,
        [
            ((points, 2 * rim), BF16),
            ((points, channels), F32),
            ((variables, points), F32),
            ((variables, points), F32),
        ],
        "hhhhhhhv",
        [
            pltpu.VMEM(neighbours.shape, jnp.int32),
            pltpu.VMEM(edge_weight.shape, F32),
            pltpu.VMEM((1, variables), F32),
            pltpu.VMEM((1, points), F32),
            pltpu.VMEM((mesh_count, channels), BF16),
            pltpu.VMEM((points, channels), BF16),
            pltpu.VMEM((variables, 1, points), F32),
            pltpu.SemaphoreType.DMA((7,)),
        ],
        flops=6 * points * mesh_count * channels,
        moved=8_000_000,
    )(
        neighbours, edge_weight, variable_weight[None], area_weight[None], latent, skip,
        state.reshape(variables, 1, points), near,
    )
    field, scaled, rscale = call(
        forward_kernel,
        [
            ((variables, points), F32),
            ((points, channels), BF16),
            ((points, 1), F32),
        ],
        flops=2 * points * channels * (2 * rim + variables),
        moved=5_000_000,
    )(part, edges, far, gain, output_projection, state)
    sent = jnp.broadcast_to(field.astype(jnp.float16)[None], (members, variables, points))
    every = lax.all_to_all(sent, MEMBER, 0, 0, tiled=True).astype(F32)
    fore_grad, parts = call(
        loss_kernel,
        [((variables, points), BF16), ((plane, CHUNK, channels), BF16)],
        flops=4 * points * channels * variables,
        moved=4_000_000,
    )(every, field, target, weight_map, output_projection, scaled, gain)

    parts = lax.all_to_all(parts, PLANE, 0, 0, tiled=True)
    (mine,) = call(fold_kernel, [((CHUNK, channels), F32)])(parts)
    met = lax.ppermute(mine, "c", swap)
    depth = lax.axis_size("z")
    (parts,) = call(
        functools.partial(pair_kernel, variables), [((depth, CHUNK, channels), BF16)]
    )(mine, met)
    own, near_grad, far_grad = call(
        back_kernel,
        [((mesh_count, channels), F32), ((rim, channels), BF16), ((rim, channels), BF16)],
        flops=2 * points * channels * (extent + variables),
        moved=6_000_000,
        spaces="a",
    )(met, neighbours, edge_weight, fore_grad, output_projection, scaled, gain, rscale)
    far_grad = lax.ppermute(far_grad, GRID, links)
    near_grad = lax.ppermute(near_grad, "c", swap)
    (latent_grad,) = call(finish_latent_kernel, [((1, mesh_count, channels), BF16)])(
        own, near_grad, far_grad
    )
    parts = lax.all_to_all(parts, "z", 0, 0, tiled=True)
    (parts,) = call(
        functools.partial(spread_kernel, variables), [((plane, CHUNK, channels), BF16)], "va"
    )(parts, own)
    parts = lax.all_to_all(parts, PLANE, 0, 0, tiled=True)
    wout, gain_grad, crps = call(
        functools.partial(finish_weights_kernel, points * slabs * variables),
        [((variables, channels), F32), ((1, channels), F32), ((1, 1), F32)],
        "vh",
    )(parts, latent_grad)
    return (crps[0, 0], latent_grad, wout, gain_grad[0])


def solution(mesh):
    fine = Mesh(mesh.devices.reshape(2, 4, 2, 8, 2), ("xl", "y", "xh", "z", "c"))
    placed = (
        P(MEMBER, GRID, None),
        P(MEMBER, GRID, None),
        P(MEMBER, None, GRID),
        P(None, GRID),
        P(None, GRID),
        P(None, GRID),
        P(GRID),
        P(),
        P(),
        P(),
    )
    return jax.shard_map(
        per_device,
        mesh=fine,
        in_specs=placed,
        out_specs=(P(), P(MEMBER, GRID, None), P(), P()),
        check_vma=False,
    )
```

```python
import functools

import jax
import jax.numpy as jnp
from jax import lax
from jax.experimental import pallas as pl
from jax.experimental.pallas import tpu as pltpu
from jax.sharding import Mesh
from jax.sharding import PartitionSpec as P

SMOOTHING = 0.25
FAIRNESS = 0.95
NORM_EPS = 1e-05
MEMBER = ("xl", "y")
GRID = ("xh", "z", "c")
PLANE = ("xl", "y", "xh")
CHUNK = 8
BLOCK = 128
BF16 = jnp.bfloat16
F32 = jnp.float32
VMEM_LIMIT = 24 * 1024 * 1024


def dot(a, b, dims):
    return lax.dot_general(a, b, (dims, ((), ())), preferred_element_type=F32)


def call(kernel, outs, spaces="", scratch=(), flops=0, moved=0):
    places = {"s": pltpu.SMEM, "h": pltpu.HBM, "a": pl.ANY, "v": pltpu.VMEM}

    def run(*operands):
        letters = spaces.ljust(len(operands), "v")
        operands = [
            pltpu.with_memory_space_constraint(x, pltpu.HBM) if c == "h" else x
            for x, c in zip(operands, letters)
        ]
        return pl.pallas_call(
            kernel,
            out_shape=[jax.ShapeDtypeStruct(s, d) for s, d in outs],
            in_specs=[pl.BlockSpec(memory_space=places[c]) for c in letters],
            out_specs=[pl.BlockSpec(memory_space=pltpu.VMEM) for _ in outs],
            scratch_shapes=list(scratch),
            compiler_params=pltpu.CompilerParams(vmem_limit_bytes=VMEM_LIMIT),
            cost_estimate=pl.CostEstimate(flops=flops, bytes_accessed=moved, transcendentals=0),
        )(*operands)

    return run


def cut_kernel(latent, out, sem):
    rim = out.shape[0]
    start = pl.multiple_of(lax.axis_index("c") * rim, rim)
    copy = pltpu.make_async_copy(latent.at[pl.ds(start, rim)], out, sem)
    copy.start()
    copy.wait()


def borrowed_rows(distance):
    core, slab = lax.axis_index("c"), lax.axis_index(GRID)
    inner = jnp.logical_and(slab > 0, slab < lax.axis_size(GRID) - 1)
    return (1 - core) * distance, core * distance, inner


def prepare_kernel(
    nb_in, ew_in, vw_in, area_in, latent_in, skip_in, state_in, earlier,
    near_out, edges_out, part_out, wm_out, state_out,
    nb, ew, vw, area, latent, skip, state, sems,
):
    pairs = (
        (nb_in, nb), (ew_in, ew), (vw_in, vw), (area_in, area),
        (latent_in, latent), (skip_in, skip), (state_in, state),
    )
    copies = [pltpu.make_async_copy(a, b, sems.at[i]) for i, (a, b) in enumerate(pairs)]
    rim = near_out.shape[0]
    near_rows = pl.ds(pl.multiple_of((1 - lax.axis_index("c")) * rim, rim), rim)
    copies.append(pltpu.make_async_copy(latent_in.at[near_rows], near_out, sems.at[len(pairs)]))
    for copy in copies:
        copy.start()
    for copy in copies[:4]:
        copy.wait()
    slots, points = nb.shape
    mesh_count = latent.shape[0]
    near_start, far_start, far_there = borrowed_rows(rim + mesh_count)
    weights = ew[...]
    weights = weights / jnp.sum(weights, axis=0, keepdims=True)
    rows = nb[...]
    both = jnp.concatenate(
        [rows.astype(F32), weights, jnp.zeros((8 - 2 * slots, points), F32)], axis=0
    )
    columns = jnp.transpose(both)
    ids = columns.astype(jnp.int32)

    def edges(start, count):
        lane = lax.broadcasted_iota(jnp.int32, (points, count), 1) + start
        total = jnp.zeros((points, count), F32)
        for k in range(slots):
            total = total + jnp.where(
                lane == ids[:, k : k + 1], columns[:, slots + k : slots + k + 1], 0.0
            )
        return total

    def parts(value):
        high = value.astype(BF16)
        return high, (value - high.astype(F32)).astype(BF16)

    near_high, near_low = parts(edges(near_start, rim))
    own_high, own_low = parts(edges(rim, mesh_count))
    far_high, far_low = parts(jnp.where(far_there, edges(far_start, rim), 0.0))
    for i, value in enumerate((near_high, near_low, far_high, far_low)):
        edges_out[:, i * rim : (i + 1) * rim] = value
    copies[4].wait()
    own = latent[...]
    mix = dot(
        jnp.concatenate([own_high, own_low], axis=1), jnp.concatenate([own, own], axis=0), ((1,), (0,))
    )
    copies[5].wait()
    part_out[...] = skip[...].astype(F32) + mix
    variables = vw.shape[1]
    diagonal = lax.broadcasted_iota(jnp.int32, (variables, variables), 0) == (
        lax.broadcasted_iota(jnp.int32, (variables, variables), 1)
    )
    vw_column = jnp.sum(jnp.where(diagonal, vw[...], 0.0), axis=1, keepdims=True)
    wm_out[...] = vw_column * area[...]
    copies[6].wait()
    state_out[...] = state[:, 0, :]
    copies[7].wait()


def forward_kernel(part, edges, near, far, gain, proj, state, f_out, sc_out, rs_out):
    close, distant = near[...], far[...]
    twice = jnp.concatenate([close, close, distant, distant], axis=0)
    for r in range(0, part.shape[0], BLOCK):
        at = slice(r, r + BLOCK)
        mixed = part[at] + dot(edges[at], twice, ((1,), (0,)))
        centred = mixed - jnp.mean(mixed, axis=1, keepdims=True)
        rscale = lax.rsqrt(jnp.mean(centred * centred, axis=1, keepdims=True) + NORM_EPS)
        sc_out[at] = (centred * rscale * gain[...]).astype(BF16)
        rs_out[at] = rscale
    f_out[...] = state[...] + dot(proj[...], sc_out[...], ((1,), (1,)))


def loss_kernel(every, field, target, wm, proj, scaled, gain, fg_out, parts_out):
    members, variables, _ = every.shape
    eps_fair = (1.0 - FAIRNESS) / members
    coef_pair = (1.0 - eps_fair) / (members * (members - 1))
    smooth = SMOOTHING * SMOOTHING
    member = lax.axis_index(MEMBER)
    f = field[...]
    weight_map = wm[...]
    d = f - target[...]
    s = d * d + smooth
    r = lax.rsqrt(s)
    spread, slope = s * r, d * r
    pair_total = jnp.full_like(f, -SMOOTHING)
    pair_slope = jnp.zeros_like(f)
    for k in range(members):
        other = jnp.where(member == k, f, every[k])
        d = f - other
        s = d * d + smooth
        r = lax.rsqrt(s)
        pair_total = pair_total + s * r
        pair_slope = pair_slope + d * r
    terms = weight_map * (spread / members - 0.5 * coef_pair * pair_total)
    loss = jnp.sum(jnp.sum(terms, axis=0, keepdims=True), axis=1, keepdims=True)
    fore_grad = (weight_map * (slope / members - coef_pair * pair_slope)).astype(BF16)
    fg_out[...] = fore_grad
    wout = dot(fore_grad, scaled[...], ((1,), (0,)))
    product = jnp.sum(wout * proj[...].astype(F32), axis=0, keepdims=True) / gain[...]
    last = variables // CHUNK
    for i in range(last):
        parts_out[i] = wout[i * CHUNK : (i + 1) * CHUNK].astype(BF16)
    channels = wout.shape[1]
    high = loss.astype(BF16).astype(F32)
    rest = variables - last * CHUNK
    parts_out[last] = jnp.concatenate(
        [
            wout[last * CHUNK :],
            product,
            jnp.broadcast_to(high, (1, channels)),
            jnp.broadcast_to(loss - high, (1, channels)),
            jnp.zeros((CHUNK - rest - 3, channels), F32),
        ],
        axis=0,
    ).astype(BF16)
    for i in range(last + 1, parts_out.shape[0]):
        parts_out[i] = jnp.zeros((CHUNK, channels), BF16)


def back_kernel(earlier, nb, ew, fore_grad, proj, scaled, gain, rscale, own_out, near_out, far_out):
    channels = scaled.shape[1]
    rim = near_out.shape[0]
    mesh_count = own_out.shape[0]
    scaled_grad = dot(fore_grad[...], proj[...], ((0,), (0,)))
    values = scaled[...].astype(F32)
    norm_grad = scaled_grad * gain[...]
    first = jnp.sum(norm_grad, axis=1, keepdims=True) / channels
    second = jnp.sum(scaled_grad * values, axis=1, keepdims=True) / channels
    mixed_grad = rscale[...] * (norm_grad - first - values * (1.0 / gain[...]) * second)
    mixed_grad = mixed_grad.astype(BF16)
    weights = ew[...]
    weights = weights / jnp.sum(weights, axis=0, keepdims=True)
    rows = nb[...]
    near_start, far_start, far_there = borrowed_rows(rim + mesh_count)

    def back(start, count, there=None):
        row = lax.broadcasted_iota(jnp.int32, (count, nb.shape[1]), 0) + start
        edges = jnp.zeros(row.shape, F32)
        for k in range(nb.shape[0]):
            edges = edges + jnp.where(row == rows[k : k + 1], weights[k : k + 1], 0.0)
        if there is not None:
            edges = jnp.where(there, edges, 0.0)
        return dot(edges.astype(BF16), mixed_grad, ((1,), (0,)))

    far_out[...] = back(far_start, rim, far_there).astype(BF16)
    near_out[...] = back(near_start, rim).astype(BF16)
    own_out[...] = back(rim, mesh_count)


def finish_latent_kernel(own, near, far, out):
    rim = near.shape[0]
    a, b = near[...].astype(F32), far[...].astype(F32)
    second = lax.axis_index("c") == 1
    out[0, :rim] = (own[:rim] + jnp.where(second, a, b)).astype(BF16)
    out[0, rim:] = (own[rim:] + jnp.where(second, b, a)).astype(BF16)


def narrowed(total, variables):
    here = lax.axis_index(PLANE) == variables // CHUNK
    first = variables % CHUNK + 1
    loss = total[first : first + 1] + total[first + 1 : first + 2]
    high = loss.astype(BF16).astype(F32)
    row = lax.broadcasted_iota(jnp.int32, total.shape, 0)
    split = jnp.where(row == first, high, jnp.where(row == first + 1, loss - high, total))
    return jnp.where(here, split, total).astype(BF16)


def fold_kernel(parts, out):
    out[...] = jnp.sum(parts[...].astype(F32), axis=0)


def pair_kernel(variables, mine, met, out):
    total = narrowed(mine[...] + met[...], variables)
    for i in range(out.shape[0]):
        out[i] = total


def spread_kernel(variables, parts, earlier, out):
    total = narrowed(jnp.sum(parts[...].astype(F32), axis=0), variables)
    for i in range(out.shape[0]):
        out[i] = total


def finish_weights_kernel(count, parts, earlier, wout_out, gain_out, loss_out):
    variables = wout_out.shape[0]
    last = variables // CHUNK
    for i in range(last):
        wout_out[i * CHUNK : (i + 1) * CHUNK] = parts[i].astype(F32)
    chunk = parts[last].astype(F32)
    rest = variables - last * CHUNK
    wout_out[last * CHUNK :] = chunk[:rest]
    gain_out[...] = chunk[rest : rest + 1]
    loss = chunk[rest + 1 : rest + 2, :1] + chunk[rest + 2 : rest + 3, :1]
    loss_out[...] = loss * (1.0 / count)


def per_device(
    latent,
    grid_latent_skip,
    initial_member_state,
    target,
    neighbours,
    edge_weight,
    area_weight,
    variable_weight,
    output_projection,
    layer_norm_gain,
):
    latent, skip, state = latent[0], grid_latent_skip[0], initial_member_state[0]
    mesh_count, channels = latent.shape
    points = skip.shape[0]
    rim = mesh_count // 2
    extent = mesh_count + 2 * rim
    variables = output_projection.shape[0]
    members = lax.axis_size(MEMBER)
    slabs = lax.axis_size(GRID)
    plane = lax.axis_size(PLANE)
    gain = layer_norm_gain[None]
    swap = [(0, 1), (1, 0)]
    links = [(i, i + 1) for i in range(1, slabs - 1, 2)]
    links = links + [(j, i) for i, j in links] + [(0, 0), (slabs - 1, slabs - 1)]

    (far_send,) = call(
        cut_kernel, [((rim, channels), BF16)], "h", [pltpu.SemaphoreType.DMA]
    )(latent)
    far = lax.ppermute(far_send, GRID, links)
    near_send, edges, part, weight_map, state = call(
        prepare_kernel,
        [
            ((rim, channels), BF16),
            ((points, 4 * rim), BF16),
            ((points, channels), F32),
            ((variables, points), F32),
            ((variables, points), F32),
        ],
        "hhhhhhha",
        [
            pltpu.VMEM(neighbours.shape, jnp.int32),
            pltpu.VMEM(edge_weight.shape, F32),
            pltpu.VMEM((1, variables), F32),
            pltpu.VMEM((1, points), F32),
            pltpu.VMEM((mesh_count, channels), BF16),
            pltpu.VMEM((points, channels), BF16),
            pltpu.VMEM((variables, 1, points), F32),
            pltpu.SemaphoreType.DMA((8,)),
        ],
        flops=6 * points * mesh_count * channels,
        moved=8_000_000,
    )(
        neighbours, edge_weight, variable_weight[None], area_weight[None], latent, skip,
        state.reshape(variables, 1, points), far_send,
    )
    near = lax.ppermute(near_send, "c", swap)
    field, scaled, rscale = call(
        forward_kernel,
        [
            ((variables, points), F32),
            ((points, channels), BF16),
            ((points, 1), F32),
        ],
        flops=2 * points * channels * (2 * rim + variables),
        moved=5_000_000,
    )(part, edges, near, far, gain, output_projection, state)
    sent = jnp.broadcast_to(field.astype(jnp.float16)[None], (members, variables, points))
    every = lax.all_to_all(sent, MEMBER, 0, 0, tiled=True).astype(F32)
    fore_grad, parts = call(
        loss_kernel,
        [((variables, points), BF16), ((plane, CHUNK, channels), BF16)],
        flops=4 * points * channels * variables,
        moved=4_000_000,
    )(every, field, target, weight_map, output_projection, scaled, gain)

    parts = lax.all_to_all(parts, PLANE, 0, 0, tiled=True)
    (mine,) = call(fold_kernel, [((CHUNK, channels), F32)])(parts)
    met = lax.ppermute(mine, "c", swap)
    depth = lax.axis_size("z")
    (parts,) = call(
        functools.partial(pair_kernel, variables), [((depth, CHUNK, channels), BF16)]
    )(mine, met)
    own, near_grad, far_grad = call(
        back_kernel,
        [((mesh_count, channels), F32), ((rim, channels), BF16), ((rim, channels), BF16)],
        flops=2 * points * channels * (extent + variables),
        moved=6_000_000,
        spaces="a",
    )(met, neighbours, edge_weight, fore_grad, output_projection, scaled, gain, rscale)
    far_grad = lax.ppermute(far_grad, GRID, links)
    near_grad = lax.ppermute(near_grad, "c", swap)
    (latent_grad,) = call(finish_latent_kernel, [((1, mesh_count, channels), BF16)])(
        own, near_grad, far_grad
    )
    parts = lax.all_to_all(parts, "z", 0, 0, tiled=True)
    (parts,) = call(
        functools.partial(spread_kernel, variables), [((plane, CHUNK, channels), BF16)], "va"
    )(parts, own)
    parts = lax.all_to_all(parts, PLANE, 0, 0, tiled=True)
    wout, gain_grad, crps = call(
        functools.partial(finish_weights_kernel, points * slabs * variables),
        [((variables, channels), F32), ((1, channels), F32), ((1, 1), F32)],
        "vh",
    )(parts, latent_grad)
    return (crps[0, 0], latent_grad, wout, gain_grad[0])


def solution(mesh):
    fine = Mesh(mesh.devices.reshape(2, 4, 2, 8, 2), ("xl", "y", "xh", "z", "c"))
    placed = (
        P(MEMBER, GRID, None),
        P(MEMBER, GRID, None),
        P(MEMBER, None, GRID),
        P(None, GRID),
        P(None, GRID),
        P(None, GRID),
        P(GRID),
        P(),
        P(),
        P(),
    )
    return jax.shard_map(
        per_device,
        mesh=fine,
        in_specs=placed,
        out_specs=(P(), P(MEMBER, GRID, None), P(), P()),
        check_vma=False,
    )
```

```python
import functools

import jax
import jax.numpy as jnp
from jax import lax
from jax.experimental import pallas as pl
from jax.experimental.pallas import tpu as pltpu
from jax.sharding import Mesh
from jax.sharding import PartitionSpec as P

SMOOTHING = 0.25
FAIRNESS = 0.95
NORM_EPS = 1e-05
MEMBER = ("xl", "y")
GRID = ("xh", "z", "c")
PLANE = ("xl", "y", "xh")
CHUNK = 8
BLOCK = 128
BF16 = jnp.bfloat16
F32 = jnp.float32
VMEM_LIMIT = 24 * 1024 * 1024


def dot(a, b, dims):
    return lax.dot_general(a, b, (dims, ((), ())), preferred_element_type=F32)


def call(kernel, outs, spaces="", scratch=(), flops=0, moved=0):
    places = {"s": pltpu.SMEM, "h": pltpu.HBM, "a": pl.ANY, "v": pltpu.VMEM}

    def run(*operands):
        letters = spaces.ljust(len(operands), "v")
        operands = [
            pltpu.with_memory_space_constraint(x, pltpu.HBM) if c == "h" else x
            for x, c in zip(operands, letters)
        ]
        return pl.pallas_call(
            kernel,
            out_shape=[jax.ShapeDtypeStruct(s, d) for s, d in outs],
            in_specs=[pl.BlockSpec(memory_space=places[c]) for c in letters],
            out_specs=[pl.BlockSpec(memory_space=pltpu.VMEM) for _ in outs],
            scratch_shapes=list(scratch),
            compiler_params=pltpu.CompilerParams(vmem_limit_bytes=VMEM_LIMIT),
            cost_estimate=pl.CostEstimate(flops=flops, bytes_accessed=moved, transcendentals=0),
        )(*operands)

    return run


def cut_kernel(latent, out, sem):
    rim = out.shape[0]
    start = pl.multiple_of(lax.axis_index("c") * rim, rim)
    copy = pltpu.make_async_copy(latent.at[pl.ds(start, rim)], out, sem)
    copy.start()
    copy.wait()


def borrowed_rows(distance):
    core, slab = lax.axis_index("c"), lax.axis_index(GRID)
    inner = jnp.logical_and(slab > 0, slab < lax.axis_size(GRID) - 1)
    return (1 - core) * distance, core * distance, inner


def prepare_kernel(
    nb_in, ew_in, vw_in, area_in, latent_in, skip_in, state_in, earlier,
    near_out, edges_out, part_out, wm_out, state_out,
    nb, ew, vw, area, latent, skip, state, sems,
):
    pairs = (
        (nb_in, nb), (ew_in, ew), (vw_in, vw), (area_in, area),
        (latent_in, latent), (skip_in, skip), (state_in, state),
    )
    copies = [pltpu.make_async_copy(a, b, sems.at[i]) for i, (a, b) in enumerate(pairs)]
    rim = near_out.shape[0]
    near_rows = pl.ds(pl.multiple_of((1 - lax.axis_index("c")) * rim, rim), rim)
    copies.append(pltpu.make_async_copy(latent_in.at[near_rows], near_out, sems.at[len(pairs)]))
    for copy in copies:
        copy.start()
    for copy in copies[:4]:
        copy.wait()
    slots, points = nb.shape
    mesh_count = latent.shape[0]
    near_start, far_start, far_there = borrowed_rows(rim + mesh_count)
    weights = ew[...]
    weights = weights / jnp.sum(weights, axis=0, keepdims=True)
    rows = nb[...]
    both = jnp.concatenate(
        [rows.astype(F32), weights, jnp.zeros((8 - 2 * slots, points), F32)], axis=0
    )
    columns = jnp.transpose(both)
    ids = columns.astype(jnp.int32)

    def edges(start, count):
        lane = lax.broadcasted_iota(jnp.int32, (points, count), 1) + start
        total = jnp.zeros((points, count), F32)
        for k in range(slots):
            total = total + jnp.where(
                lane == ids[:, k : k + 1], columns[:, slots + k : slots + k + 1], 0.0
            )
        return total

    def parts(value):
        high = value.astype(BF16)
        return high, (value - high.astype(F32)).astype(BF16)

    near_high, near_low = parts(edges(near_start, rim))
    own_high, own_low = parts(edges(rim, mesh_count))
    far_high, far_low = parts(jnp.where(far_there, edges(far_start, rim), 0.0))
    for i, value in enumerate((near_high, near_low, far_high, far_low)):
        edges_out[:, i * rim : (i + 1) * rim] = value
    copies[4].wait()
    own = latent[...]
    mix = dot(
        jnp.concatenate([own_high, own_low], axis=1), jnp.concatenate([own, own], axis=0), ((1,), (0,))
    )
    copies[5].wait()
    part_out[...] = skip[...].astype(F32) + mix
    variables = vw.shape[1]
    diagonal = lax.broadcasted_iota(jnp.int32, (variables, variables), 0) == (
        lax.broadcasted_iota(jnp.int32, (variables, variables), 1)
    )
    vw_column = jnp.sum(jnp.where(diagonal, vw[...], 0.0), axis=1, keepdims=True)
    wm_out[...] = vw_column * area[...]
    copies[6].wait()
    state_out[...] = state[:, 0, :]
    copies[7].wait()


def forward_kernel(part, edges, near, far, gain, proj, state, f_out, sc_out, rs_out):
    close, distant = near[...], far[...]
    twice = jnp.concatenate([close, close, distant, distant], axis=0)
    for r in range(0, part.shape[0], BLOCK):
        at = slice(r, r + BLOCK)
        mixed = part[at] + dot(edges[at], twice, ((1,), (0,)))
        centred = mixed - jnp.mean(mixed, axis=1, keepdims=True)
        rscale = lax.rsqrt(jnp.mean(centred * centred, axis=1, keepdims=True) + NORM_EPS)
        sc_out[at] = (centred * rscale * gain[...]).astype(BF16)
        rs_out[at] = rscale
    f_out[...] = state[...] + dot(proj[...], sc_out[...], ((1,), (1,)))


def loss_kernel(every, field, target, wm, proj, scaled, gain, fg_out, parts_out):
    members, variables, _ = every.shape
    eps_fair = (1.0 - FAIRNESS) / members
    coef_pair = (1.0 - eps_fair) / (members * (members - 1))
    smooth = SMOOTHING * SMOOTHING
    member = lax.axis_index(MEMBER)
    f = field[...]
    weight_map = wm[...]
    d = f - target[...]
    s = d * d + smooth
    r = lax.rsqrt(s)
    spread, slope = s * r, d * r
    pair_total = jnp.full_like(f, -SMOOTHING)
    pair_slope = jnp.zeros_like(f)
    for k in range(members):
        other = jnp.where(member == k, f, every[k])
        d = f - other
        s = d * d + smooth
        r = lax.rsqrt(s)
        pair_total = pair_total + s * r
        pair_slope = pair_slope + d * r
    terms = weight_map * (spread / members - 0.5 * coef_pair * pair_total)
    loss = jnp.sum(jnp.sum(terms, axis=0, keepdims=True), axis=1, keepdims=True)
    fore_grad = (weight_map * (slope / members - coef_pair * pair_slope)).astype(BF16)
    fg_out[...] = fore_grad
    wout = dot(fore_grad, scaled[...], ((1,), (0,)))
    product = jnp.sum(wout * proj[...].astype(F32), axis=0, keepdims=True) / gain[...]
    last = variables // CHUNK
    for i in range(last):
        parts_out[i] = wout[i * CHUNK : (i + 1) * CHUNK].astype(BF16)
    channels = wout.shape[1]
    high = loss.astype(BF16).astype(F32)
    rest = variables - last * CHUNK
    parts_out[last] = jnp.concatenate(
        [
            wout[last * CHUNK :],
            product,
            jnp.broadcast_to(high, (1, channels)),
            jnp.broadcast_to(loss - high, (1, channels)),
            jnp.zeros((CHUNK - rest - 3, channels), F32),
        ],
        axis=0,
    ).astype(BF16)
    for i in range(last + 1, parts_out.shape[0]):
        parts_out[i] = jnp.zeros((CHUNK, channels), BF16)


def back_kernel(earlier, nb, ew, fore_grad, proj, scaled, gain, rscale, own_out, near_out, far_out):
    channels = scaled.shape[1]
    rim = near_out.shape[0]
    mesh_count = own_out.shape[0]
    scaled_grad = dot(fore_grad[...], proj[...], ((0,), (0,)))
    values = scaled[...].astype(F32)
    norm_grad = scaled_grad * gain[...]
    first = jnp.sum(norm_grad, axis=1, keepdims=True) / channels
    second = jnp.sum(scaled_grad * values, axis=1, keepdims=True) / channels
    mixed_grad = rscale[...] * (norm_grad - first - values * (1.0 / gain[...]) * second)
    mixed_grad = mixed_grad.astype(BF16)
    weights = ew[...]
    weights = weights / jnp.sum(weights, axis=0, keepdims=True)
    rows = nb[...]
    near_start, far_start, far_there = borrowed_rows(rim + mesh_count)

    def back(start, count, there=None):
        row = lax.broadcasted_iota(jnp.int32, (count, nb.shape[1]), 0) + start
        edges = jnp.zeros(row.shape, F32)
        for k in range(nb.shape[0]):
            edges = edges + jnp.where(row == rows[k : k + 1], weights[k : k + 1], 0.0)
        if there is not None:
            edges = jnp.where(there, edges, 0.0)
        return dot(edges.astype(BF16), mixed_grad, ((1,), (0,)))

    far_out[...] = back(far_start, rim, far_there).astype(BF16)
    near_out[...] = back(near_start, rim).astype(BF16)
    own_out[...] = back(rim, mesh_count)


def finish_latent_kernel(own, near, far, out):
    rim = near.shape[0]
    a, b = near[...].astype(F32), far[...].astype(F32)
    second = lax.axis_index("c") == 1
    out[0, :rim] = (own[:rim] + jnp.where(second, a, b)).astype(BF16)
    out[0, rim:] = (own[rim:] + jnp.where(second, b, a)).astype(BF16)


def narrowed(total, variables):
    here = lax.axis_index(PLANE) == variables // CHUNK
    first = variables % CHUNK + 1
    loss = total[first : first + 1] + total[first + 1 : first + 2]
    high = loss.astype(BF16).astype(F32)
    row = lax.broadcasted_iota(jnp.int32, total.shape, 0)
    split = jnp.where(row == first, high, jnp.where(row == first + 1, loss - high, total))
    return jnp.where(here, split, total).astype(BF16)


def fold_kernel(parts, out):
    out[...] = jnp.sum(parts[...].astype(F32), axis=0)


def pair_kernel(variables, mine, met, out):
    total = narrowed(mine[...] + met[...], variables)
    for i in range(out.shape[0]):
        out[i] = total


def spread_kernel(variables, parts, earlier, out):
    total = narrowed(jnp.sum(parts[...].astype(F32), axis=0), variables)
    for i in range(out.shape[0]):
        out[i] = total


def finish_weights_kernel(count, parts, earlier, wout_out, gain_out, loss_out):
    variables = wout_out.shape[0]
    last = variables // CHUNK
    for i in range(last):
        wout_out[i * CHUNK : (i + 1) * CHUNK] = parts[i].astype(F32)
    chunk = parts[last].astype(F32)
    rest = variables - last * CHUNK
    wout_out[last * CHUNK :] = chunk[:rest]
    gain_out[...] = chunk[rest : rest + 1]
    loss = chunk[rest + 1 : rest + 2, :1] + chunk[rest + 2 : rest + 3, :1]
    loss_out[...] = loss * (1.0 / count)


def per_device(
    latent,
    grid_latent_skip,
    initial_member_state,
    target,
    neighbours,
    edge_weight,
    area_weight,
    variable_weight,
    output_projection,
    layer_norm_gain,
):
    latent, skip, state = latent[0], grid_latent_skip[0], initial_member_state[0]
    mesh_count, channels = latent.shape
    points = skip.shape[0]
    rim = mesh_count // 2
    extent = mesh_count + 2 * rim
    variables = output_projection.shape[0]
    members = lax.axis_size(MEMBER)
    slabs = lax.axis_size(GRID)
    plane = lax.axis_size(PLANE)
    gain = layer_norm_gain[None]
    swap = [(0, 1), (1, 0)]
    links = [
        (m * slabs + i, (m * slabs + i + 1) if i < slabs - 1 and i > 0 else ((m ^ 1) * slabs + i))
        for m in range(members)
        for i in range(slabs)
        if i % 2 == 1 or i == 0
    ]
    links = [p for p in links if p[0] < p[1]]
    links = links + [(j, i) for i, j in links]

    (far_send,) = call(
        cut_kernel, [((rim, channels), BF16)], "h", [pltpu.SemaphoreType.DMA]
    )(latent)
    far = lax.ppermute(far_send, MEMBER + GRID, links)
    near_send, edges, part, weight_map, state = call(
        prepare_kernel,
        [
            ((rim, channels), BF16),
            ((points, 4 * rim), BF16),
            ((points, channels), F32),
            ((variables, points), F32),
            ((variables, points), F32),
        ],
        "hhhhhhha",
        [
            pltpu.VMEM(neighbours.shape, jnp.int32),
            pltpu.VMEM(edge_weight.shape, F32),
            pltpu.VMEM((1, variables), F32),
            pltpu.VMEM((1, points), F32),
            pltpu.VMEM((mesh_count, channels), BF16),
            pltpu.VMEM((points, channels), BF16),
            pltpu.VMEM((variables, 1, points), F32),
            pltpu.SemaphoreType.DMA((8,)),
        ],
        flops=6 * points * mesh_count * channels,
        moved=8_000_000,
    )(
        neighbours, edge_weight, variable_weight[None], area_weight[None], latent, skip,
        state.reshape(variables, 1, points), far_send,
    )
    near = lax.ppermute(near_send, "c", swap)
    field, scaled, rscale = call(
        forward_kernel,
        [
            ((variables, points), F32),
            ((points, channels), BF16),
            ((points, 1), F32),
        ],
        flops=2 * points * channels * (2 * rim + variables),
        moved=5_000_000,
    )(part, edges, near, far, gain, output_projection, state)
    sent = jnp.broadcast_to(field.astype(jnp.float16)[None], (members, variables, points))
    every = lax.all_to_all(sent, MEMBER, 0, 0, tiled=True).astype(F32)
    fore_grad, parts = call(
        loss_kernel,
        [((variables, points), BF16), ((plane, CHUNK, channels), BF16)],
        flops=4 * points * channels * variables,
        moved=4_000_000,
    )(every, field, target, weight_map, output_projection, scaled, gain)

    parts = lax.all_to_all(parts, PLANE, 0, 0, tiled=True)
    (mine,) = call(fold_kernel, [((CHUNK, channels), F32)])(parts)
    met = lax.ppermute(mine, "c", swap)
    depth = lax.axis_size("z")
    (parts,) = call(
        functools.partial(pair_kernel, variables), [((depth, CHUNK, channels), BF16)]
    )(mine, met)
    own, near_grad, far_grad = call(
        back_kernel,
        [((mesh_count, channels), F32), ((rim, channels), BF16), ((rim, channels), BF16)],
        flops=2 * points * channels * (extent + variables),
        moved=6_000_000,
        spaces="a",
    )(met, neighbours, edge_weight, fore_grad, output_projection, scaled, gain, rscale)
    far_grad = lax.ppermute(far_grad, MEMBER + GRID, links)
    near_grad = lax.ppermute(near_grad, "c", swap)
    (latent_grad,) = call(finish_latent_kernel, [((1, mesh_count, channels), BF16)])(
        own, near_grad, far_grad
    )
    parts = lax.all_to_all(parts, "z", 0, 0, tiled=True)
    (parts,) = call(
        functools.partial(spread_kernel, variables), [((plane, CHUNK, channels), BF16)], "va"
    )(parts, own)
    parts = lax.all_to_all(parts, PLANE, 0, 0, tiled=True)
    wout, gain_grad, crps = call(
        functools.partial(finish_weights_kernel, points * slabs * variables),
        [((variables, channels), F32), ((1, channels), F32), ((1, 1), F32)],
        "vh",
    )(parts, latent_grad)
    return (crps[0, 0], latent_grad, wout, gain_grad[0])


def solution(mesh):
    fine = Mesh(mesh.devices.reshape(2, 4, 2, 8, 2), ("xl", "y", "xh", "z", "c"))
    placed = (
        P(MEMBER, GRID, None),
        P(MEMBER, GRID, None),
        P(MEMBER, None, GRID),
        P(None, GRID),
        P(None, GRID),
        P(None, GRID),
        P(GRID),
        P(),
        P(),
        P(),
    )
    return jax.shard_map(
        per_device,
        mesh=fine,
        in_specs=placed,
        out_specs=(P(), P(MEMBER, GRID, None), P(), P()),
        check_vma=False,
    )
```

```python
import functools

import jax
import jax.numpy as jnp
from jax import lax
from jax.experimental import pallas as pl
from jax.experimental.pallas import tpu as pltpu
from jax.sharding import Mesh
from jax.sharding import PartitionSpec as P

SMOOTHING = 0.25
FAIRNESS = 0.95
NORM_EPS = 1e-05
MEMBER = ("xl", "y")
GRID = ("xh", "z", "c")
PLANE = ("xl", "y", "xh")
CHUNK = 8
BLOCK = 128
BF16 = jnp.bfloat16
F32 = jnp.float32
VMEM_LIMIT = 24 * 1024 * 1024


def dot(a, b, dims):
    return lax.dot_general(a, b, (dims, ((), ())), preferred_element_type=F32)


def call(kernel, outs, spaces="", scratch=(), flops=0, moved=0):
    places = {"s": pltpu.SMEM, "h": pltpu.HBM, "a": pl.ANY, "v": pltpu.VMEM}

    def run(*operands):
        letters = spaces.ljust(len(operands), "v")
        operands = [
            pltpu.with_memory_space_constraint(x, pltpu.HBM) if c == "h" else x
            for x, c in zip(operands, letters)
        ]
        return pl.pallas_call(
            kernel,
            out_shape=[jax.ShapeDtypeStruct(s, d) for s, d in outs],
            in_specs=[pl.BlockSpec(memory_space=places[c]) for c in letters],
            out_specs=[pl.BlockSpec(memory_space=pltpu.VMEM) for _ in outs],
            scratch_shapes=list(scratch),
            compiler_params=pltpu.CompilerParams(vmem_limit_bytes=VMEM_LIMIT),
            cost_estimate=pl.CostEstimate(flops=flops, bytes_accessed=moved, transcendentals=0),
        )(*operands)

    return run


def cut_kernel(latent, out, sem):
    rim = out.shape[0]
    start = pl.multiple_of(lax.axis_index("c") * rim, rim)
    copy = pltpu.make_async_copy(latent.at[pl.ds(start, rim)], out, sem)
    copy.start()
    copy.wait()


def borrowed_rows(distance):
    core, slab = lax.axis_index("c"), lax.axis_index(GRID)
    inner = jnp.logical_and(slab > 0, slab < lax.axis_size(GRID) - 1)
    return (1 - core) * distance, core * distance, inner


def prepare_kernel(
    nb_in, ew_in, vw_in, area_in, latent_in, skip_in, state_in, earlier,
    near_out, edges_out, part_out, wm_out, state_out,
    nb, ew, vw, area, latent, skip, state, sems,
):
    pairs = (
        (nb_in, nb), (ew_in, ew), (vw_in, vw), (area_in, area),
        (latent_in, latent), (skip_in, skip), (state_in, state),
    )
    copies = [pltpu.make_async_copy(a, b, sems.at[i]) for i, (a, b) in enumerate(pairs)]
    rim = near_out.shape[0]
    near_rows = pl.ds(pl.multiple_of((1 - lax.axis_index("c")) * rim, rim), rim)
    copies.append(pltpu.make_async_copy(latent_in.at[near_rows], near_out, sems.at[len(pairs)]))
    for copy in copies:
        copy.start()
    for copy in copies[:4]:
        copy.wait()
    slots, points = nb.shape
    mesh_count = latent.shape[0]
    near_start, far_start, far_there = borrowed_rows(rim + mesh_count)
    weights = ew[...]
    weights = weights / jnp.sum(weights, axis=0, keepdims=True)
    rows = nb[...]
    both = jnp.concatenate(
        [rows.astype(F32), weights, jnp.zeros((8 - 2 * slots, points), F32)], axis=0
    )
    columns = jnp.transpose(both)
    ids = columns.astype(jnp.int32)

    def edges(start, count):
        lane = lax.broadcasted_iota(jnp.int32, (points, count), 1) + start
        total = jnp.zeros((points, count), F32)
        for k in range(slots):
            total = total + jnp.where(
                lane == ids[:, k : k + 1], columns[:, slots + k : slots + k + 1], 0.0
            )
        return total

    def parts(value):
        high = value.astype(BF16)
        return high, (value - high.astype(F32)).astype(BF16)

    near_high, near_low = parts(edges(near_start, rim))
    own_high, own_low = parts(edges(rim, mesh_count))
    far_high, far_low = parts(jnp.where(far_there, edges(far_start, rim), 0.0))
    for i, value in enumerate((near_high, near_low, far_high, far_low)):
        edges_out[:, i * rim : (i + 1) * rim] = value
    copies[4].wait()
    own = latent[...]
    mix = dot(
        jnp.concatenate([own_high, own_low], axis=1), jnp.concatenate([own, own], axis=0), ((1,), (0,))
    )
    copies[5].wait()
    part_out[...] = skip[...].astype(F32) + mix
    variables = vw.shape[1]
    diagonal = lax.broadcasted_iota(jnp.int32, (variables, variables), 0) == (
        lax.broadcasted_iota(jnp.int32, (variables, variables), 1)
    )
    vw_column = jnp.sum(jnp.where(diagonal, vw[...], 0.0), axis=1, keepdims=True)
    wm_out[...] = vw_column * area[...]
    copies[6].wait()
    state_out[...] = state[:, 0, :]
    copies[7].wait()


def forward_kernel(part, edges, near, far, gain, proj, state, f_out, sc_out, rs_out):
    close, distant = near[...], far[...]
    twice = jnp.concatenate([close, close, distant, distant], axis=0)
    for r in range(0, part.shape[0], BLOCK):
        at = slice(r, r + BLOCK)
        mixed = part[at] + dot(edges[at], twice, ((1,), (0,)))
        centred = mixed - jnp.mean(mixed, axis=1, keepdims=True)
        rscale = lax.rsqrt(jnp.mean(centred * centred, axis=1, keepdims=True) + NORM_EPS)
        sc_out[at] = (centred * rscale * gain[...]).astype(BF16)
        rs_out[at] = rscale
    f_out[...] = state[...] + dot(proj[...], sc_out[...], ((1,), (1,)))


def loss_kernel(every, field, target, wm, proj, scaled, gain, fg_out, parts_out):
    members, variables, _ = every.shape
    eps_fair = (1.0 - FAIRNESS) / members
    coef_pair = (1.0 - eps_fair) / (members * (members - 1))
    smooth = SMOOTHING * SMOOTHING
    member = lax.axis_index(MEMBER)
    f = field[...]
    weight_map = wm[...]
    d = f - target[...]
    s = d * d + smooth
    r = lax.rsqrt(s)
    spread, slope = s * r, d * r
    pair_total = jnp.full_like(f, -SMOOTHING)
    pair_slope = jnp.zeros_like(f)
    for k in range(members):
        other = jnp.where(member == k, f, every[k])
        d = f - other
        s = d * d + smooth
        r = lax.rsqrt(s)
        pair_total = pair_total + s * r
        pair_slope = pair_slope + d * r
    terms = weight_map * (spread / members - 0.5 * coef_pair * pair_total)
    loss = jnp.sum(jnp.sum(terms, axis=0, keepdims=True), axis=1, keepdims=True)
    fore_grad = (weight_map * (slope / members - coef_pair * pair_slope)).astype(BF16)
    fg_out[...] = fore_grad
    wout = dot(fore_grad, scaled[...], ((1,), (0,)))
    product = jnp.sum(wout * proj[...].astype(F32), axis=0, keepdims=True) / gain[...]
    last = variables // CHUNK
    for i in range(last):
        parts_out[i] = wout[i * CHUNK : (i + 1) * CHUNK].astype(BF16)
    channels = wout.shape[1]
    high = loss.astype(BF16).astype(F32)
    rest = variables - last * CHUNK
    parts_out[last] = jnp.concatenate(
        [
            wout[last * CHUNK :],
            product,
            jnp.broadcast_to(high, (1, channels)),
            jnp.broadcast_to(loss - high, (1, channels)),
            jnp.zeros((CHUNK - rest - 3, channels), F32),
        ],
        axis=0,
    ).astype(BF16)
    for i in range(last + 1, parts_out.shape[0]):
        parts_out[i] = jnp.zeros((CHUNK, channels), BF16)


def turned_edges(nb, ew, start, count):
    weights = ew[...]
    weights = weights / jnp.sum(weights, axis=0, keepdims=True)
    rows = nb[...]
    row = lax.broadcasted_iota(jnp.int32, (count, nb.shape[1]), 0) + start
    edges = jnp.zeros(row.shape, F32)
    for k in range(nb.shape[0]):
        edges = edges + jnp.where(row == rows[k : k + 1], weights[k : k + 1], 0.0)
    return edges


def back_kernel(earlier, nb, ew, fore_grad, proj, scaled, gain, rscale, mg_out, near_out, far_out):
    channels = scaled.shape[1]
    rim = near_out.shape[0]
    scaled_grad = dot(fore_grad[...], proj[...], ((0,), (0,)))
    values = scaled[...].astype(F32)
    norm_grad = scaled_grad * gain[...]
    first = jnp.sum(norm_grad, axis=1, keepdims=True) / channels
    second = jnp.sum(scaled_grad * values, axis=1, keepdims=True) / channels
    mixed_grad = rscale[...] * (norm_grad - first - values * (1.0 / gain[...]) * second)
    mixed_grad = mixed_grad.astype(BF16)
    mg_out[...] = mixed_grad
    near_start, far_start, far_there = borrowed_rows(3 * rim)
    far = jnp.where(far_there, turned_edges(nb, ew, far_start, rim), 0.0).astype(BF16)
    far_out[...] = dot(far, mixed_grad, ((1,), (0,))).astype(BF16)
    near = turned_edges(nb, ew, near_start, rim).astype(BF16)
    near_out[...] = dot(near, mixed_grad, ((1,), (0,))).astype(BF16)


def finish_latent_kernel(nb, ew, mixed_grad, near, far, out):
    rim = near.shape[0]
    edges = turned_edges(nb, ew, rim, 2 * rim).astype(BF16)
    own = dot(edges, mixed_grad[...], ((1,), (0,)))
    a, b = near[...].astype(F32), far[...].astype(F32)
    second = lax.axis_index("c") == 1
    out[0, :rim] = (own[:rim] + jnp.where(second, a, b)).astype(BF16)
    out[0, rim:] = (own[rim:] + jnp.where(second, b, a)).astype(BF16)


def narrowed(total, variables):
    here = lax.axis_index(PLANE) == variables // CHUNK
    first = variables % CHUNK + 1
    loss = total[first : first + 1] + total[first + 1 : first + 2]
    high = loss.astype(BF16).astype(F32)
    row = lax.broadcasted_iota(jnp.int32, total.shape, 0)
    split = jnp.where(row == first, high, jnp.where(row == first + 1, loss - high, total))
    return jnp.where(here, split, total).astype(BF16)


def fold_kernel(parts, out):
    out[...] = jnp.sum(parts[...].astype(F32), axis=0)


def pair_kernel(variables, mine, met, out):
    total = narrowed(mine[...] + met[...], variables)
    for i in range(out.shape[0]):
        out[i] = total


def spread_kernel(variables, parts, earlier, out):
    total = narrowed(jnp.sum(parts[...].astype(F32), axis=0), variables)
    for i in range(out.shape[0]):
        out[i] = total


def finish_weights_kernel(count, parts, earlier, wout_out, gain_out, loss_out):
    variables = wout_out.shape[0]
    last = variables // CHUNK
    for i in range(last):
        wout_out[i * CHUNK : (i + 1) * CHUNK] = parts[i].astype(F32)
    chunk = parts[last].astype(F32)
    rest = variables - last * CHUNK
    wout_out[last * CHUNK :] = chunk[:rest]
    gain_out[...] = chunk[rest : rest + 1]
    loss = chunk[rest + 1 : rest + 2, :1] + chunk[rest + 2 : rest + 3, :1]
    loss_out[...] = loss * (1.0 / count)


def per_device(
    latent,
    grid_latent_skip,
    initial_member_state,
    target,
    neighbours,
    edge_weight,
    area_weight,
    variable_weight,
    output_projection,
    layer_norm_gain,
):
    latent, skip, state = latent[0], grid_latent_skip[0], initial_member_state[0]
    mesh_count, channels = latent.shape
    points = skip.shape[0]
    rim = mesh_count // 2
    extent = mesh_count + 2 * rim
    variables = output_projection.shape[0]
    members = lax.axis_size(MEMBER)
    slabs = lax.axis_size(GRID)
    plane = lax.axis_size(PLANE)
    gain = layer_norm_gain[None]
    swap = [(0, 1), (1, 0)]
    links = [
        (m * slabs + i, (m * slabs + i + 1) if i < slabs - 1 and i > 0 else ((m ^ 1) * slabs + i))
        for m in range(members)
        for i in range(slabs)
        if i % 2 == 1 or i == 0
    ]
    links = [p for p in links if p[0] < p[1]]
    links = links + [(j, i) for i, j in links]

    (far_send,) = call(
        cut_kernel, [((rim, channels), BF16)], "h", [pltpu.SemaphoreType.DMA]
    )(latent)
    far = lax.ppermute(far_send, MEMBER + GRID, links)
    near_send, edges, part, weight_map, state = call(
        prepare_kernel,
        [
            ((rim, channels), BF16),
            ((points, 4 * rim), BF16),
            ((points, channels), F32),
            ((variables, points), F32),
            ((variables, points), F32),
        ],
        "hhhhhhha",
        [
            pltpu.VMEM(neighbours.shape, jnp.int32),
            pltpu.VMEM(edge_weight.shape, F32),
            pltpu.VMEM((1, variables), F32),
            pltpu.VMEM((1, points), F32),
            pltpu.VMEM((mesh_count, channels), BF16),
            pltpu.VMEM((points, channels), BF16),
            pltpu.VMEM((variables, 1, points), F32),
            pltpu.SemaphoreType.DMA((8,)),
        ],
        flops=6 * points * mesh_count * channels,
        moved=8_000_000,
    )(
        neighbours, edge_weight, variable_weight[None], area_weight[None], latent, skip,
        state.reshape(variables, 1, points), far_send,
    )
    near = lax.ppermute(near_send, "c", swap)
    field, scaled, rscale = call(
        forward_kernel,
        [
            ((variables, points), F32),
            ((points, channels), BF16),
            ((points, 1), F32),
        ],
        flops=2 * points * channels * (2 * rim + variables),
        moved=5_000_000,
    )(part, edges, near, far, gain, output_projection, state)
    sent = jnp.broadcast_to(field.astype(jnp.float16)[None], (members, variables, points))
    every = lax.all_to_all(sent, MEMBER, 0, 0, tiled=True).astype(F32)
    fore_grad, parts = call(
        loss_kernel,
        [((variables, points), BF16), ((plane, CHUNK, channels), BF16)],
        flops=4 * points * channels * variables,
        moved=4_000_000,
    )(every, field, target, weight_map, output_projection, scaled, gain)

    parts = lax.all_to_all(parts, PLANE, 0, 0, tiled=True)
    (mine,) = call(fold_kernel, [((CHUNK, channels), F32)])(parts)
    met = lax.ppermute(mine, "c", swap)
    depth = lax.axis_size("z")
    (parts,) = call(
        functools.partial(pair_kernel, variables), [((depth, CHUNK, channels), BF16)]
    )(mine, met)
    mixed_grad, near_grad, far_grad = call(
        back_kernel,
        [((points, channels), BF16), ((rim, channels), BF16), ((rim, channels), BF16)],
        flops=2 * points * channels * (extent + variables),
        moved=6_000_000,
        spaces="a",
    )(met, neighbours, edge_weight, fore_grad, output_projection, scaled, gain, rscale)
    far_grad = lax.ppermute(far_grad, MEMBER + GRID, links)
    near_grad = lax.ppermute(near_grad, "c", swap)
    (latent_grad,) = call(
        finish_latent_kernel,
        [((1, mesh_count, channels), BF16)],
        flops=2 * points * channels * mesh_count,
        moved=3_000_000,
    )(neighbours, edge_weight, mixed_grad, near_grad, far_grad)
    parts = lax.all_to_all(parts, "z", 0, 0, tiled=True)
    (parts,) = call(
        functools.partial(spread_kernel, variables), [((plane, CHUNK, channels), BF16)], "va"
    )(parts, mixed_grad)
    parts = lax.all_to_all(parts, PLANE, 0, 0, tiled=True)
    wout, gain_grad, crps = call(
        functools.partial(finish_weights_kernel, points * slabs * variables),
        [((variables, channels), F32), ((1, channels), F32), ((1, 1), F32)],
        "vh",
    )(parts, latent_grad)
    return (crps[0, 0], latent_grad, wout, gain_grad[0])


def solution(mesh):
    fine = Mesh(mesh.devices.reshape(2, 4, 2, 8, 2), ("xl", "y", "xh", "z", "c"))
    placed = (
        P(MEMBER, GRID, None),
        P(MEMBER, GRID, None),
        P(MEMBER, None, GRID),
        P(None, GRID),
        P(None, GRID),
        P(None, GRID),
        P(GRID),
        P(),
        P(),
        P(),
    )
    return jax.shard_map(
        per_device,
        mesh=fine,
        in_specs=placed,
        out_specs=(P(), P(MEMBER, GRID, None), P(), P()),
        check_vma=False,
    )
```

```python
import functools

import jax
import jax.numpy as jnp
from jax import lax
from jax.experimental import pallas as pl
from jax.experimental.pallas import tpu as pltpu
from jax.sharding import Mesh
from jax.sharding import PartitionSpec as P

SMOOTHING = 0.25
FAIRNESS = 0.95
NORM_EPS = 1e-05
MEMBER = ("xl", "y")
GRID = ("xh", "z", "c")
PLANE = ("xl", "y", "xh")
CHUNK = 8
BLOCK = 128
BF16 = jnp.bfloat16
F32 = jnp.float32
VMEM_LIMIT = 24 * 1024 * 1024


def dot(a, b, dims):
    return lax.dot_general(a, b, (dims, ((), ())), preferred_element_type=F32)


def call(kernel, outs, spaces="", scratch=(), flops=0, moved=0):
    places = {"s": pltpu.SMEM, "h": pltpu.HBM, "a": pl.ANY, "v": pltpu.VMEM}

    def run(*operands):
        letters = spaces.ljust(len(operands), "v")
        operands = [
            pltpu.with_memory_space_constraint(x, pltpu.HBM) if c == "h" else x
            for x, c in zip(operands, letters)
        ]
        return pl.pallas_call(
            kernel,
            out_shape=[jax.ShapeDtypeStruct(s, d) for s, d in outs],
            in_specs=[pl.BlockSpec(memory_space=places[c]) for c in letters],
            out_specs=[pl.BlockSpec(memory_space=pltpu.VMEM) for _ in outs],
            scratch_shapes=list(scratch),
            compiler_params=pltpu.CompilerParams(vmem_limit_bytes=VMEM_LIMIT),
            cost_estimate=pl.CostEstimate(flops=flops, bytes_accessed=moved, transcendentals=0),
        )(*operands)

    return run


def cut_kernel(latent, out, sem):
    rim = out.shape[0]
    start = pl.multiple_of(lax.axis_index("c") * rim, rim)
    copy = pltpu.make_async_copy(latent.at[pl.ds(start, rim)], out, sem)
    copy.start()
    copy.wait()


def borrowed_rows(distance):
    core, slab = lax.axis_index("c"), lax.axis_index(GRID)
    inner = jnp.logical_and(slab > 0, slab < lax.axis_size(GRID) - 1)
    return (1 - core) * distance, core * distance, inner


def prepare_kernel(
    nb_in, ew_in, vw_in, area_in, latent_in, skip_in, state_in, earlier,
    near_out, edges_out, part_out, wm_out, state_out,
    nb, ew, vw, area, latent, skip, state, sems,
):
    pairs = (
        (nb_in, nb), (ew_in, ew), (vw_in, vw), (area_in, area),
        (latent_in, latent), (skip_in, skip), (state_in, state),
    )
    copies = [pltpu.make_async_copy(a, b, sems.at[i]) for i, (a, b) in enumerate(pairs)]
    rim = near_out.shape[0]
    near_rows = pl.ds(pl.multiple_of((1 - lax.axis_index("c")) * rim, rim), rim)
    copies.append(pltpu.make_async_copy(latent_in.at[near_rows], near_out, sems.at[len(pairs)]))
    for copy in copies:
        copy.start()
    for copy in copies[:4]:
        copy.wait()
    slots, points = nb.shape
    mesh_count = latent.shape[0]
    near_start, far_start, far_there = borrowed_rows(rim + mesh_count)
    weights = ew[...]
    weights = weights / jnp.sum(weights, axis=0, keepdims=True)
    rows = nb[...]
    both = jnp.concatenate(
        [rows.astype(F32), weights, jnp.zeros((8 - 2 * slots, points), F32)], axis=0
    )
    columns = jnp.transpose(both)
    ids = columns.astype(jnp.int32)

    def edges(start, count):
        lane = lax.broadcasted_iota(jnp.int32, (points, count), 1) + start
        total = jnp.zeros((points, count), F32)
        for k in range(slots):
            total = total + jnp.where(
                lane == ids[:, k : k + 1], columns[:, slots + k : slots + k + 1], 0.0
            )
        return total

    def parts(value):
        high = value.astype(BF16)
        return high, (value - high.astype(F32)).astype(BF16)

    near_high, near_low = parts(edges(near_start, rim))
    own_high, own_low = parts(edges(rim, mesh_count))
    far_high, far_low = parts(jnp.where(far_there, edges(far_start, rim), 0.0))
    for i, value in enumerate((near_high, near_low, far_high, far_low)):
        edges_out[:, i * rim : (i + 1) * rim] = value
    copies[4].wait()
    own = latent[...]
    mix = dot(
        jnp.concatenate([own_high, own_low], axis=1), jnp.concatenate([own, own], axis=0), ((1,), (0,))
    )
    copies[5].wait()
    part_out[...] = skip[...].astype(F32) + mix
    variables = vw.shape[1]
    diagonal = lax.broadcasted_iota(jnp.int32, (variables, variables), 0) == (
        lax.broadcasted_iota(jnp.int32, (variables, variables), 1)
    )
    vw_column = jnp.sum(jnp.where(diagonal, vw[...], 0.0), axis=1, keepdims=True)
    wm_out[...] = vw_column * area[...]
    copies[6].wait()
    state_out[...] = state[:, 0, :]
    copies[7].wait()


def forward_kernel(part, edges, near, far, gain, proj, state, f_out, sc_out, rs_out):
    close, distant = near[...], far[...]
    twice = jnp.concatenate([close, close, distant, distant], axis=0)
    for r in range(0, part.shape[0], BLOCK):
        at = slice(r, r + BLOCK)
        mixed = part[at] + dot(edges[at], twice, ((1,), (0,)))
        centred = mixed - jnp.mean(mixed, axis=1, keepdims=True)
        rscale = lax.rsqrt(jnp.mean(centred * centred, axis=1, keepdims=True) + NORM_EPS)
        sc_out[at] = (centred * rscale * gain[...]).astype(BF16)
        rs_out[at] = rscale
    f_out[...] = state[...] + dot(proj[...], sc_out[...], ((1,), (1,)))


def loss_kernel(every, field, target, wm, proj, scaled, gain, fg_out, parts_out):
    members, variables, _ = every.shape
    eps_fair = (1.0 - FAIRNESS) / members
    coef_pair = (1.0 - eps_fair) / (members * (members - 1))
    smooth = SMOOTHING * SMOOTHING
    member = lax.axis_index(MEMBER)
    f = field[...]
    weight_map = wm[...]
    d = f - target[...]
    s = d * d + smooth
    r = lax.rsqrt(s)
    spread, slope = s * r, d * r
    pair_total = jnp.full_like(f, -SMOOTHING)
    pair_slope = jnp.zeros_like(f)
    for k in range(members):
        other = jnp.where(member == k, f, every[k])
        d = f - other
        s = d * d + smooth
        r = lax.rsqrt(s)
        pair_total = pair_total + s * r
        pair_slope = pair_slope + d * r
    terms = weight_map * (spread / members - 0.5 * coef_pair * pair_total)
    loss = jnp.sum(jnp.sum(terms, axis=0, keepdims=True), axis=1, keepdims=True)
    fore_grad = (weight_map * (slope / members - coef_pair * pair_slope)).astype(BF16)
    fg_out[...] = fore_grad
    wout = dot(fore_grad, scaled[...], ((1,), (0,)))
    product = jnp.sum(wout * proj[...].astype(F32), axis=0, keepdims=True) / gain[...]
    last = variables // CHUNK
    for i in range(last):
        parts_out[i] = wout[i * CHUNK : (i + 1) * CHUNK].astype(BF16)
    channels = wout.shape[1]
    high = loss.astype(BF16).astype(F32)
    rest = variables - last * CHUNK
    parts_out[last] = jnp.concatenate(
        [
            wout[last * CHUNK :],
            product,
            jnp.broadcast_to(high, (1, channels)),
            jnp.broadcast_to(loss - high, (1, channels)),
            jnp.zeros((CHUNK - rest - 3, channels), F32),
        ],
        axis=0,
    ).astype(BF16)
    for i in range(last + 1, parts_out.shape[0]):
        parts_out[i] = jnp.zeros((CHUNK, channels), BF16)


def back_kernel(nb, ew, fore_grad, proj, scaled, gain, rscale, own_out, near_out, far_out):
    channels = scaled.shape[1]
    rim = near_out.shape[0]
    mesh_count = own_out.shape[0]
    scaled_grad = dot(fore_grad[...], proj[...], ((0,), (0,)))
    values = scaled[...].astype(F32)
    norm_grad = scaled_grad * gain[...]
    first = jnp.sum(norm_grad, axis=1, keepdims=True) / channels
    second = jnp.sum(scaled_grad * values, axis=1, keepdims=True) / channels
    mixed_grad = rscale[...] * (norm_grad - first - values * (1.0 / gain[...]) * second)
    mixed_grad = mixed_grad.astype(BF16)
    weights = ew[...]
    weights = weights / jnp.sum(weights, axis=0, keepdims=True)
    rows = nb[...]
    near_start, far_start, far_there = borrowed_rows(rim + mesh_count)

    def back(start, count, there=None):
        row = lax.broadcasted_iota(jnp.int32, (count, nb.shape[1]), 0) + start
        edges = jnp.zeros(row.shape, F32)
        for k in range(nb.shape[0]):
            edges = edges + jnp.where(row == rows[k : k + 1], weights[k : k + 1], 0.0)
        if there is not None:
            edges = jnp.where(there, edges, 0.0)
        return dot(edges.astype(BF16), mixed_grad, ((1,), (0,)))

    far_out[...] = back(far_start, rim, far_there).astype(BF16)
    near_out[...] = back(near_start, rim).astype(BF16)
    own_out[...] = back(rim, mesh_count)


def finish_latent_kernel(own, near, far, out):
    rim = near.shape[0]
    a, b = near[...].astype(F32), far[...].astype(F32)
    second = lax.axis_index("c") == 1
    out[0, :rim] = (own[:rim] + jnp.where(second, a, b)).astype(BF16)
    out[0, rim:] = (own[rim:] + jnp.where(second, b, a)).astype(BF16)


def narrowed(total, variables):
    here = lax.axis_index(PLANE) == variables // CHUNK
    first = variables % CHUNK + 1
    loss = total[first : first + 1] + total[first + 1 : first + 2]
    high = loss.astype(BF16).astype(F32)
    row = lax.broadcasted_iota(jnp.int32, total.shape, 0)
    split = jnp.where(row == first, high, jnp.where(row == first + 1, loss - high, total))
    return jnp.where(here, split, total).astype(BF16)


def fold_kernel(parts, earlier, out):
    out[...] = jnp.sum(parts[...].astype(F32), axis=0)


def pair_kernel(variables, mine, met, out):
    total = narrowed(mine[...] + met[...], variables)
    for i in range(out.shape[0]):
        out[i] = total


def spread_kernel(variables, parts, earlier, out):
    total = narrowed(jnp.sum(parts[...].astype(F32), axis=0), variables)
    for i in range(out.shape[0]):
        out[i] = total


def finish_weights_kernel(count, parts, wout_out, gain_out, loss_out):
    variables = wout_out.shape[0]
    last = variables // CHUNK
    for i in range(last):
        wout_out[i * CHUNK : (i + 1) * CHUNK] = parts[i].astype(F32)
    chunk = parts[last].astype(F32)
    rest = variables - last * CHUNK
    wout_out[last * CHUNK :] = chunk[:rest]
    gain_out[...] = chunk[rest : rest + 1]
    loss = chunk[rest + 1 : rest + 2, :1] + chunk[rest + 2 : rest + 3, :1]
    loss_out[...] = loss * (1.0 / count)


def per_device(
    latent,
    grid_latent_skip,
    initial_member_state,
    target,
    neighbours,
    edge_weight,
    area_weight,
    variable_weight,
    output_projection,
    layer_norm_gain,
):
    latent, skip, state = latent[0], grid_latent_skip[0], initial_member_state[0]
    mesh_count, channels = latent.shape
    points = skip.shape[0]
    rim = mesh_count // 2
    extent = mesh_count + 2 * rim
    variables = output_projection.shape[0]
    members = lax.axis_size(MEMBER)
    slabs = lax.axis_size(GRID)
    plane = lax.axis_size(PLANE)
    gain = layer_norm_gain[None]
    swap = [(0, 1), (1, 0)]
    links = [
        (m * slabs + i, (m * slabs + i + 1) if i < slabs - 1 and i > 0 else ((m ^ 1) * slabs + i))
        for m in range(members)
        for i in range(slabs)
        if i % 2 == 1 or i == 0
    ]
    links = [p for p in links if p[0] < p[1]]
    links = links + [(j, i) for i, j in links]

    (far_send,) = call(
        cut_kernel, [((rim, channels), BF16)], "h", [pltpu.SemaphoreType.DMA]
    )(latent)
    far = lax.ppermute(far_send, MEMBER + GRID, links)
    near_send, edges, part, weight_map, state = call(
        prepare_kernel,
        [
            ((rim, channels), BF16),
            ((points, 4 * rim), BF16),
            ((points, channels), F32),
            ((variables, points), F32),
            ((variables, points), F32),
        ],
        "hhhhhhha",
        [
            pltpu.VMEM(neighbours.shape, jnp.int32),
            pltpu.VMEM(edge_weight.shape, F32),
            pltpu.VMEM((1, variables), F32),
            pltpu.VMEM((1, points), F32),
            pltpu.VMEM((mesh_count, channels), BF16),
            pltpu.VMEM((points, channels), BF16),
            pltpu.VMEM((variables, 1, points), F32),
            pltpu.SemaphoreType.DMA((8,)),
        ],
        flops=6 * points * mesh_count * channels,
        moved=8_000_000,
    )(
        neighbours, edge_weight, variable_weight[None], area_weight[None], latent, skip,
        state.reshape(variables, 1, points), far_send,
    )
    near = lax.ppermute(near_send, "c", swap)
    field, scaled, rscale = call(
        forward_kernel,
        [
            ((variables, points), F32),
            ((points, channels), BF16),
            ((points, 1), F32),
        ],
        flops=2 * points * channels * (2 * rim + variables),
        moved=5_000_000,
    )(part, edges, near, far, gain, output_projection, state)
    sent = jnp.broadcast_to(field.astype(jnp.float16)[None], (members, variables, points))
    every = lax.all_to_all(sent, MEMBER, 0, 0, tiled=True).astype(F32)
    fore_grad, parts = call(
        loss_kernel,
        [((variables, points), BF16), ((plane, CHUNK, channels), BF16)],
        flops=4 * points * channels * variables,
        moved=4_000_000,
    )(every, field, target, weight_map, output_projection, scaled, gain)

    own, near_grad, far_grad = call(
        back_kernel,
        [((mesh_count, channels), F32), ((rim, channels), BF16), ((rim, channels), BF16)],
        flops=2 * points * channels * (extent + variables),
        moved=6_000_000,
    )(neighbours, edge_weight, fore_grad, output_projection, scaled, gain, rscale)
    far_grad = lax.ppermute(far_grad, MEMBER + GRID, links)
    near_grad = lax.ppermute(near_grad, "c", swap)
    (latent_grad,) = call(finish_latent_kernel, [((1, mesh_count, channels), BF16)])(
        own, near_grad, far_grad
    )
    parts = lax.all_to_all(parts, PLANE, 0, 0, tiled=True)
    (mine,) = call(fold_kernel, [((CHUNK, channels), F32)], "va")(parts, own)
    met = lax.ppermute(mine, "c", swap)
    depth = lax.axis_size("z")
    (parts,) = call(
        functools.partial(pair_kernel, variables), [((depth, CHUNK, channels), BF16)]
    )(mine, met)
    parts = lax.all_to_all(parts, "z", 0, 0, tiled=True)
    (parts,) = call(
        functools.partial(spread_kernel, variables), [((plane, CHUNK, channels), BF16)], "vh"
    )(parts, latent_grad)
    parts = lax.all_to_all(parts, PLANE, 0, 0, tiled=True)
    wout, gain_grad, crps = call(
        functools.partial(finish_weights_kernel, points * slabs * variables),
        [((variables, channels), F32), ((1, channels), F32), ((1, 1), F32)],
    )(parts)
    return (crps[0, 0], latent_grad, wout, gain_grad[0])


def solution(mesh):
    fine = Mesh(mesh.devices.reshape(2, 4, 2, 8, 2), ("xl", "y", "xh", "z", "c"))
    placed = (
        P(MEMBER, GRID, None),
        P(MEMBER, GRID, None),
        P(MEMBER, None, GRID),
        P(None, GRID),
        P(None, GRID),
        P(None, GRID),
        P(GRID),
        P(),
        P(),
        P(),
    )
    return jax.shard_map(
        per_device,
        mesh=fine,
        in_specs=placed,
        out_specs=(P(), P(MEMBER, GRID, None), P(), P()),
        check_vma=False,
    )
```
